256 devices in a mesh: row: 64 (over y, x, z_hi, core), rep: 4 (over z_lo).
Axes of the slice: x: 4, y: 4, z: 8 (z_hi: 2, z_lo: 4; z = z_hi * 4 + z_lo), core: 2. Of those that a mesh axis runs over, the one named last changes fastest.
Arguments:
- features: bfloat16 [65536, 128], P(('row', 'rep')), may hold values from -6 to 6
- adjacency: bfloat16 [64, 4, 256, 128, 128], P('row', 'rep'), may hold values from -0.046875 to 0.046875
- block_list: int32 [64, 4, 64, 4, 3], P('row', 'rep'), may hold values from 0 to 255, as said below
- block_counts: int32 [64, 4, 64], P('row', 'rep'), may hold values from 2 to 4
- weight: bfloat16 [128, 256], replicated, may hold values from -0.5 to 0.5
- cotangent: bfloat16 [65536, 256], P(('row', 'rep')), may hold values from -6 to 6
Outputs:
- activations: bfloat16 [65536, 256], P(('row', 'rep'))
- feature_grad: bfloat16 [65536, 128], P(('row', 'rep'))
- weight_grad: float32 [128, 256], replicated
The draws below stay inside these ranges and needn't reach their ends.
Inputs may be any that keep to these rules, and one draw needn't show every extreme that they name: `block_list`: entry 0 is a block row 0 to 7, entry 1 a block 0 to 1, entry 2 a storage slot; the storage slots of one device are each named once.
All inputs are finite; a program needn't handle non-finite values.
Results may differ from the reference program's by a relative error of at most 0.02.
Values may be sent and summed in bfloat16 or wider, within the bound.
No kernel may reach another device: no remote copies, remote signals or barrier semaphores. Data moves between devices by JAX's collectives and lax.ppermute only.
A program may use at most 64 MiB of HBM per device.

```python
import jax
import jax.numpy as jnp
from jax import lax

FIN = 128
HID = 256
BLOCK_NODES = 128
DEVICE_BLOCKS = 2
SECTION_SLOTS = 4
COLUMN_SECTIONS = 64
BROWS = 8
DEVICE_SLOTS = 256
NODES = 65536
N_ROW = 64
N_REP = 4


def draw_block_list(key, part):
    key = jax.random.fold_in(key, 11)
    key_rows, key_cols, key_slots = jax.random.split(key, 3)
    array_shape = (N_ROW, N_REP, COLUMN_SECTIONS, SECTION_SLOTS)
    block_rows = jax.random.randint(key_rows, array_shape, 0, BROWS)
    block_cols = jax.random.randint(key_cols, array_shape, 0, DEVICE_BLOCKS)
    per_device_keys = jax.random.split(key_slots, N_ROW * N_REP)
    block_storage = jax.vmap(lambda single_block: jax.random.permutation(single_block, DEVICE_SLOTS))(per_device_keys)
    block_storage = block_storage.reshape(array_shape)
    return jnp.stack([block_rows, block_cols, block_storage], axis=-1).astype(jnp.int32)


def draw_block_counts(key, part):
    key = jax.random.fold_in(key, 23)
    unsorted_draw = jax.random.randint(key, (N_ROW, N_REP, COLUMN_SECTIONS), 0, 1 << 20)
    block_tally = 2 + unsorted_draw % (SECTION_SLOTS - 1)
    device_ids = jnp.arange(N_ROW)[:, None] * N_REP + jnp.arange(N_REP)[None, :]
    complete_section = device_ids % COLUMN_SECTIONS
    low_section = (device_ids + 1) % COLUMN_SECTIONS
    section_index = jnp.arange(COLUMN_SECTIONS)[None, None, :]
    block_tally = jnp.where(section_index == complete_section[..., None], SECTION_SLOTS, block_tally)
    block_tally = jnp.where(section_index == low_section[..., None], 2, block_tally)
    return block_tally.astype(jnp.int32)


def level_of(key, dims, pieces, low, largest):
    def one(axis_at, shards_of):
        draws = jax.random.uniform(jax.random.fold_in(jax.random.fold_in(key, 6), axis_at), (shards_of,), jnp.float32, low / len(pieces), largest / len(pieces))
        return jnp.repeat(jnp.exp(draws), dims[axis_at] // shards_of).reshape((-1,) + (1,) * (len(dims) - axis_at - 1))

    level = one(*pieces[0])
    for cut in pieces[1:]:
        level = level * one(*cut)
    return level


def scatter_about(key, extent, width, reach, cuts=(), held_as=jnp.bfloat16):
    drawn = width * jax.random.normal(key, extent, jnp.float32)
    if cuts:
        drawn = drawn * level_of(key, extent, cuts, -0.22, 0.18)
    return jnp.clip(drawn, -reach, reach).astype(held_as)


def setup_inputs(seed: int = 0) -> dict:
    key_of = jax.random.split(jax.random.key(seed), 7)
    features = scatter_about(key_of[0], (NODES, FIN), 1.0, 6.0, ((0, 256),))
    adjacency = scatter_about(key_of[1], (N_ROW, N_REP, DEVICE_SLOTS, BLOCK_NODES, BLOCK_NODES), (N_ROW * SECTION_SLOTS * BLOCK_NODES // DEVICE_BLOCKS) ** -0.5, 0.046875, ((0, 64), (1, 4)))
    block_list = draw_block_list(jax.random.fold_in(key_of[6], 71), 0)
    block_counts = draw_block_counts(jax.random.fold_in(key_of[6], 71), 0)
    weight = scatter_about(key_of[4], (FIN, HID), FIN ** -0.5, 0.5)
    cotangent = scatter_about(key_of[5], (NODES, HID), 1.0, 6.0, ((0, 256),))
    return {"features": features, "adjacency": adjacency, "block_list": block_list, "block_counts": block_counts, "weight": weight, "cotangent": cotangent}


def reference(features, adjacency, block_list, block_counts, weight, cotangent):
    rows_n = adjacency.shape[0]
    reps_n = adjacency.shape[1]
    sections = block_list.shape[2]
    slot_count = block_list.shape[3]
    block_size = adjacency.shape[3]
    in_width = features.shape[1]
    own_blocks = features.shape[0] // (rows_n * reps_n * block_size)
    brows_n = reps_n * own_blocks
    source = features.reshape(rows_n, reps_n, own_blocks, block_size, in_width)
    alive_all = (jnp.arange(slot_count)[None, None, None, :] < block_counts[..., None]).astype(jnp.float32)
    section_index = jnp.arange(sections)[:, None]

    def forward_step(running, device):
        row_index = device // reps_n
        rep_index = device % reps_n
        slot_list = block_list[row_index, rep_index]
        alive = alive_all[row_index, rep_index]
        stored = adjacency[row_index, rep_index]
        picked = source[:, rep_index][section_index, slot_list[..., 1]].astype(jnp.float32)
        blocks = stored[slot_list[..., 2]].astype(jnp.float32)
        products = jnp.einsum('skab,skbc->skac', blocks, picked)
        placing = (slot_list[..., 0][..., None] == jnp.arange(brows_n)[None, None, :]).astype(jnp.float32) * alive[..., None]
        contrib = jnp.einsum('skr,skac->rac', placing, products)
        return running.at[row_index].add(contrib), None

    start_fwd = jnp.zeros((rows_n, brows_n, block_size, in_width), jnp.float32)
    aggregated, _ = lax.scan(forward_step, start_fwd, jnp.arange(rows_n * reps_n))
    pooled = aggregated.reshape(NODES, in_width).astype(jnp.bfloat16)
    hidden = jnp.dot(pooled, weight, preferred_element_type=jnp.float32)
    squash = jax.nn.sigmoid(hidden)
    activations = (hidden * squash).astype(jnp.bfloat16)
    slope = (cotangent.astype(jnp.float32) * squash * (1.0 + hidden * (1.0 - squash))).astype(jnp.bfloat16)
    weight_grad = jnp.einsum('na,nh->ah', pooled.astype(jnp.float32), slope.astype(jnp.float32)) * (float(NODES) ** -0.5)
    values = jnp.dot(slope, weight.T, preferred_element_type=jnp.float32).astype(jnp.bfloat16)
    value_groups = values.reshape(rows_n, brows_n, block_size, in_width)

    def backward_step(running, device):
        row_index = device // reps_n
        rep_index = device % reps_n
        slot_list = block_list[row_index, rep_index]
        alive = alive_all[row_index, rep_index]
        stored = adjacency[row_index, rep_index]
        picked = value_groups[row_index][slot_list[..., 0]].astype(jnp.float32)
        blocks = stored[slot_list[..., 2]].astype(jnp.float32)
        products = jnp.einsum('skba,skbc->skac', blocks, picked)
        placing = (slot_list[..., 1][..., None] == jnp.arange(own_blocks)[None, None, :]).astype(jnp.float32) * alive[..., None]
        contrib = jnp.einsum('skx,skac->sxac', placing, products)
        return running.at[:, rep_index].add(contrib), None

    start_bwd = jnp.zeros((rows_n, reps_n, own_blocks, block_size, in_width), jnp.float32)
    gradient, _ = lax.scan(backward_step, start_bwd, jnp.arange(rows_n * reps_n))
    feature_grad = gradient.reshape(NODES, in_width).astype(jnp.bfloat16)
    return activations, feature_grad, weight_grad
```

```python
import functools

import jax
import jax.numpy as jnp
import numpy as np
from jax import lax
from jax.experimental import pallas as pl
from jax.experimental.pallas import tpu as pltpu
from jax.sharding import PartitionSpec as P

B = 128
SLOTS = 4
BROWS = 8
SECTIONS = 64
ROWS = 2 * B
PIECE = 64
SPLIT = 3 * PIECE
COST = B * B * 8
F32 = jnp.float32
BF16 = jnp.bfloat16
VMEM = pl.BlockSpec(memory_space=pltpu.VMEM)
SMEM = pl.BlockSpec(memory_space=pltpu.SMEM)

COUNTS = SECTIONS * SLOTS * 3
FORWARD_ORDER = COUNTS + SECTIONS
BACKWARD_ORDER = FORWARD_ORDER + SECTIONS
PLACE = BACKWARD_ORDER + SECTIONS


def group(flip, e, ds=(0, 1, 2, 3)):
    return [(flip, e, d, u) for d in ds for u in range(2)]


FORWARD_GROUPS = [
    [group(0, 0)],
    [group(0, 1), group(0, 3)],
    [group(1, 0), group(1, 1), group(1, 3)],
    [group(0, 2), group(1, 2)],
]
BACKWARD_GROUPS = [group(1, 2), group(1, 1) + group(1, 3), group(0, 2), group(1, 0), group(0, 1) + group(0, 3), group(0, 0)]


def section_order(r, entries, sign):
    flip, e, d, u = (np.array(column, np.int32) for column in zip(*entries))
    y, x, z, core = r // 16, (r // 4) % 4, (r // 2) % 2, r % 2
    role = core ^ flip
    dy, dx = jnp.where(role == 0, e, d), jnp.where(role == 0, d, e)
    return ((y + sign * dy) & 3) * 16 + ((x + sign * dx) & 3) * 4 + (z ^ role) * 2 + u


def at(y, x, z, core):
    return (y % 4) * 16 + (x % 4) * 4 + z * 2 + core


def row_permute(array, target):
    pairs = []
    for r in range(64):
        to = target(r // 16, (r // 4) % 4, (r // 2) % 2, r % 2)
        if to is not None:
            pairs.append((r, to))
    return lax.ppermute(array, "row", pairs)


def small_axis(array, d):
    return row_permute(array, lambda y, x, z, c: at(y + d * c, x + d * (1 - c), z, c))


def large_axis(array, e):
    return row_permute(array, lambda y, x, z, c: at(y + e * (1 - c), x + e * c, z, c))


def sibling(array):
    return row_permute(array, lambda y, x, z, c: at(y, x, z, 1 - c))


def cross(array, forwards):
    if forwards:
        return row_permute(array, lambda y, x, z, c: at(y, x, z, 0) if c else at(y, x, 1 - z, 1))
    return row_permute(array, lambda y, x, z, c: at(y, x, 1 - z, 0) if c else at(y, x, z, 1))


def other_z(array):
    return row_permute(array, lambda y, x, z, c: at(y, x, 1 - z, 1) if c else None)


def turn(array, d):
    return lax.ppermute(array, "rep", [(q, (q + d) % 4) for q in range(4)])


def params():
    return pltpu.CompilerParams(vmem_limit_bytes=20 * 1024 * 1024)


def cost(slots):
    return pl.CostEstimate(flops=slots * COST, bytes_accessed=slots * COST, transcendentals=0)


def small_cost(size):
    return pl.CostEstimate(flops=size // 64, bytes_accessed=size // 64, transcendentals=0)


def touch_kernel(meta, stored, out):
    out[...] = stored[0, 0:16, :].astype(F32)


def touch(meta, stored):
    return pl.pallas_call(
        touch_kernel,
        out_shape=jax.ShapeDtypeStruct((16, B), F32),
        in_specs=[SMEM, VMEM],
        out_specs=VMEM,
        compiler_params=params(),
        cost_estimate=small_cost(1 << 10),
        name="touch_blocks",
    )(meta, stored)


def pair_up_kernel(core, own, near, far, out):
    first = core[0] == 0
    out[0:ROWS] = jnp.where(first, own[...], near[...])
    out[ROWS : 2 * ROWS] = jnp.where(first, near[...], far[...])


def pair_up(core, own, near, far):
    return pl.pallas_call(
        pair_up_kernel,
        out_shape=jax.ShapeDtypeStruct((2 * ROWS, B), BF16),
        in_specs=[SMEM] + [VMEM] * 3,
        out_specs=VMEM,
        compiler_params=params(),
        cost_estimate=small_cost(1 << 16),
        name="pair_up",
    )(core, own, near, far)


def place_kernel(counts, parts, *refs):
    sources, outs = refs[: len(counts)], refs[-len(parts) :]
    for out, pieces in zip(outs, parts):
        row = 0
        for source, start, size in pieces:
            out[row : row + size * ROWS] = sources[source][start * ROWS : (start + size) * ROWS]
            row += size * ROWS


def place(name, parts, sources, after=()):
    shapes = [jax.ShapeDtypeStruct((sum(p[2] for p in pieces) * ROWS, B), BF16) for pieces in parts]
    args = [*sources, *after]
    return pl.pallas_call(
        functools.partial(place_kernel, tuple(range(len(sources))), parts),
        out_shape=shapes,
        in_specs=[VMEM] * len(args),
        out_specs=[VMEM] * len(shapes),
        compiler_params=params(),
        cost_estimate=small_cost(1 << 18),
        name=name,
    )(*args)


STEP = 4


def forward_kernel(first_section, sizes, first, last, after, *refs):
    meta, stored = refs[:2]
    chunk_refs = refs[2 : 2 + len(sizes)]
    refs = refs[2 + len(sizes) + after :]
    if first:
        out_refs, acc = refs[:-1], refs[-1]
        acc[...] = jnp.zeros_like(acc)
    else:
        out_refs, acc = refs[1:-1], refs[-1]
        acc[0:BROWS] = refs[0][...]
    begin = first_section
    for size, chunk_ref in zip(sizes, chunk_refs):

        def step(g, carry, begin=begin, chunk_ref=chunk_ref):
            products, places = [], []
            for n in range(STEP):
                sid = meta[FORWARD_ORDER + begin + g * STEP + n]
                count = meta[COUNTS + sid]
                for k in range(SLOTS):
                    base = sid * (SLOTS * 3) + 3 * k
                    start = pl.multiple_of((g * STEP + n) * ROWS + meta[base + 1] * B, B)
                    source = chunk_ref[pl.ds(start, B)]
                    products.append(jnp.dot(stored[meta[base + 2]], source, preferred_element_type=F32))
                    places.append(jnp.where(k < count, meta[base], BROWS))
            for product, place in zip(products, places):
                acc[place] += product
            return carry

        lax.fori_loop(0, size // STEP, step, 0)
        begin += size
    if not last:
        out_refs[0][...] = acc[0:BROWS]
        return
    rep = meta[PLACE]
    for d in range(4):
        for b in range(2):
            piece = acc[lax.rem(rep + d, 4) * 2 + b]
            out_refs[d][b * B : (b + 1) * B] = piece.astype(out_refs[d].dtype)


def forward(meta, stored, first_section, chunk_list, start, last, after=()):
    sizes = tuple(chunk.shape[0] // ROWS for chunk in chunk_list)
    first = start is None
    if last:
        out_shape = [jax.ShapeDtypeStruct((2 * B, B), F32)] + [jax.ShapeDtypeStruct((2 * B, B), BF16)] * 3
    else:
        out_shape = [jax.ShapeDtypeStruct((BROWS, B, B), F32)]
    args = [meta, stored, *chunk_list, *after] + ([] if first else [start])
    return pl.pallas_call(
        functools.partial(forward_kernel, first_section, sizes, first, last, len(after)),
        out_shape=out_shape,
        in_specs=[SMEM] + [VMEM] * (len(args) - 1),
        out_specs=[VMEM] * len(out_shape),
        scratch_shapes=[pltpu.VMEM((BROWS + 1, B, B), F32)],
        compiler_params=params(),
        cost_estimate=cost(sum(sizes) * SLOTS),
        name="forward_slots",
    )(*args)


def middle_kernel(meta, own, p1, p2, p3, weight, cot, act, values, m1, m2, m3, w0):
    pooled = (own[...] + p1[...].astype(F32) + p2[...].astype(F32) + p3[...].astype(F32)).astype(BF16)
    hidden = jnp.dot(pooled, weight[...], preferred_element_type=F32)
    squash = jax.nn.sigmoid(hidden)
    act[...] = (hidden * squash).astype(BF16)
    slope = (cot[...].astype(F32) * squash * (1.0 + hidden * (1.0 - squash))).astype(BF16)
    values_t = lax.dot_general(weight[...], slope, (((1,), (1,)), ((), ())), preferred_element_type=F32)
    values_t = values_t.astype(BF16)
    for out in (values, m1, m2, m3):
        out[0:B] = values_t[:, :B]
        out[B:ROWS] = values_t[:, B:]
    term = lax.dot_general(pooled, slope, (((0,), (0,)), ((), ())), preferred_element_type=F32)
    rep = meta[PLACE]
    for q in range(4):
        piece = jnp.concatenate([term[q * 32 : (q + 1) * 32, :B], term[q * 32 : (q + 1) * 32, B:]], axis=0)

        @pl.when(rep == q)
        def _(piece=piece):
            w0[...] = piece

        for d, out in enumerate((m1, m2, m3)):

            @pl.when(lax.rem(rep + d + 1, 4) == q)
            def _(out=out, piece=piece):
                out[ROWS : ROWS + PIECE] = piece.astype(BF16)


def middle(meta, own, pieces, weight, cot):
    return pl.pallas_call(
        middle_kernel,
        out_shape=[jax.ShapeDtypeStruct((2 * B, 2 * B), BF16), jax.ShapeDtypeStruct((ROWS, B), BF16)]
        + [jax.ShapeDtypeStruct((ROWS + PIECE, B), BF16)] * 3
        + [jax.ShapeDtypeStruct((PIECE, B), F32)],
        in_specs=[SMEM] + [VMEM] * 6,
        out_specs=[VMEM] * 6,
        compiler_params=params(),
        cost_estimate=small_cost(1 << 16),
        name="middle_rows",
    )(meta, own, *pieces, weight, cot)


def split(total, out_ref, row):
    rest = total
    for n in range(3):
        part = rest.astype(BF16)
        out_ref[row + n * PIECE : row + (n + 1) * PIECE] = part
        rest = rest - part.astype(F32)


def joined(ref, row):
    parts = [ref[row + n * PIECE : row + (n + 1) * PIECE].astype(F32) for n in range(3)]
    return (parts[2] + parts[1]) + parts[0]


def gather_terms(extra, outs, extra_outs):
    total = extra[0][...]
    for ref in extra[1:]:
        total = total + ref[ROWS : ROWS + PIECE].astype(F32)
    split(total, outs[0], 8 * ROWS)
    extra_outs[0][...] = total


def sibling_terms(extra, outs, extra_outs):
    total = extra[0][...] + joined(extra[1], 8 * ROWS)
    split(total, outs[0], 4 * ROWS)
    extra_outs[0][...] = total
    extra_outs[1][...] = extra[2][...]


def spread_terms(extra, outs, extra_outs):
    half_1, half_3, own, passed = extra
    extra_outs[0][...] = passed[...]
    first, second = slice(0, 4 * ROWS), slice(4 * ROWS, 8 * ROWS)
    outs[0][first] = (outs[0][first].astype(F32) + half_1[first].astype(F32)).astype(BF16)
    outs[1][second] = (outs[1][second].astype(F32) + half_3[...].astype(F32)).astype(BF16)
    for out in outs:
        split(own[...], out, 8 * ROWS)
    outs[0][8 * ROWS + SPLIT :] = half_1[4 * ROWS :]


def backward_kernel(first_section, sizes, added, extras, finish, *refs):
    meta, stored = refs[:2]
    value_refs, refs = refs[2:6], refs[6:]
    if added:
        add_ref, refs = refs[0], refs[1:]
    extra, refs = refs[:extras], refs[extras:]
    out_refs, extra_outs, values = refs[: len(sizes)], refs[len(sizes) : -1], refs[-1]
    rep = meta[PLACE]
    for d in range(4):
        for b in range(2):
            values[lax.rem(rep + 4 - d, 4) * 2 + b] = value_refs[d][b * B : (b + 1) * B]
    values[BROWS] = jnp.zeros((B, B), BF16)

    begin = 0
    for size, out_ref in zip(sizes, out_refs):

        def step(g, carry, begin=begin, out_ref=out_ref):
            for m in range(STEP):
                n = g * STEP + m
                sid = meta[BACKWARD_ORDER + first_section + begin + n]
                count = meta[COUNTS + sid]
                base = sid * (SLOTS * 3)
                rows = []
                for j in range(2):
                    columns = []
                    for k in range(SLOTS):
                        live = (k < count) & (meta[base + 3 * k + 1] == j)
                        columns.append(values[jnp.where(live, meta[base + 3 * k], BROWS)])
                    rows.append(jnp.concatenate(columns, axis=1))
                left = jnp.concatenate(rows, axis=0)
                right = jnp.concatenate([stored[meta[base + 3 * k + 2]] for k in range(SLOTS)], axis=0)
                result = jnp.dot(left, right, preferred_element_type=F32)
                if added:
                    result = result + add_ref[pl.ds(pl.multiple_of((begin + n) * ROWS, ROWS), ROWS)].astype(F32)
                out_ref[pl.ds(pl.multiple_of(n * ROWS, ROWS), ROWS)] = result.astype(BF16)
            return carry

        lax.fori_loop(0, size // STEP, step, 0)
        begin += size
    if finish is not None:
        finish(extra, out_refs, extra_outs)


def backward(meta, stored, values, first_section, sizes, add=None, extra=(), finish=None, tails=None, extra_out=()):
    added = add is not None
    args = [meta, stored, *values] + ([add] if added else []) + list(extra)
    tails = tails or (0,) * len(sizes)
    shapes = [jax.ShapeDtypeStruct((size * ROWS + tail, B), BF16) for size, tail in zip(sizes, tails)]
    shapes += [jax.ShapeDtypeStruct(a.shape, a.dtype) for a in extra_out]
    return pl.pallas_call(
        functools.partial(backward_kernel, first_section, sizes, added, len(extra), finish),
        out_shape=shapes,
        in_specs=[SMEM] + [VMEM] * (len(args) - 1),
        out_specs=[VMEM] * len(shapes),
        scratch_shapes=[pltpu.VMEM((BROWS + 1, B, B), BF16)],
        compiler_params=params(),
        cost_estimate=cost(sum(sizes) * SLOTS),
        name="backward_slots",
    )(*args)


def sum_kernel(a, b, c, own, t0, t1, t2, t3, w):
    row = 8 * ROWS
    total = (own[...] + joined(b, row + SPLIT)) + (joined(b, row) + joined(c, row))
    w[...] = total
    for d, out in enumerate((t0, t1, t2, t3)):
        part = slice(2 * ROWS * d, 2 * ROWS * (d + 1))
        group_sum = a[part].astype(F32) + b[part].astype(F32) + c[part].astype(F32)
        out[0 : 2 * ROWS] = group_sum.astype(BF16)
        if d:
            split(total, out, 2 * ROWS)


def sum_groups(*arrays):
    return pl.pallas_call(
        sum_kernel,
        out_shape=[jax.ShapeDtypeStruct((2 * ROWS, B), BF16)]
        + [jax.ShapeDtypeStruct((2 * ROWS + SPLIT, B), BF16)] * 3
        + [jax.ShapeDtypeStruct((PIECE, B), F32)],
        in_specs=[VMEM] * 4,
        out_specs=[VMEM] * 5,
        compiler_params=params(),
        cost_estimate=small_cost(1 << 18),
        name="sum_groups",
    )(*arrays)


def unit_sum(meta, refs, out, flip):
    core = meta[PLACE + 1]
    unit = 1 - core if flip else core
    part = pl.ds(pl.multiple_of(unit * ROWS, ROWS), ROWS)
    total = refs[0][part].astype(F32)
    for ref in refs[1:]:
        total = total + ref[part].astype(F32)
    out[...] = total.astype(BF16)


def mine_kernel(meta, a, b, c, d, own, mine, w):
    unit_sum(meta, (a, b, c, d), mine, False)
    w[...] = (own[...] + joined(c, 2 * ROWS)) + (joined(b, 2 * ROWS) + joined(d, 2 * ROWS))


def sum_mine(meta, *arrays):
    return pl.pallas_call(
        mine_kernel,
        out_shape=[jax.ShapeDtypeStruct((ROWS, B), BF16), jax.ShapeDtypeStruct((PIECE, B), F32)],
        in_specs=[SMEM] + [VMEM] * 5,
        out_specs=[VMEM] * 2,
        compiler_params=params(),
        cost_estimate=small_cost(1 << 17),
        name="sum_mine",
    )(meta, *arrays)


def other_kernel(meta, mine, a, b, c, d, other):
    unit_sum(meta, (a, b, c, d), other, True)


def sum_other(meta, *arrays):
    return pl.pallas_call(
        other_kernel,
        out_shape=jax.ShapeDtypeStruct((ROWS, B), BF16),
        in_specs=[SMEM] + [VMEM] * 5,
        out_specs=VMEM,
        compiler_params=params(),
        cost_estimate=small_cost(1 << 17),
        name="sum_other",
    )(meta, *arrays)


def meet_kernel(meta, mine, far, w, w_z, own, total):
    first = meta[PLACE + 1] == 0
    own[...] = jnp.where(first, mine[...], far[...])
    total[...] = w[...] + w_z[...]


def meet(meta, *arrays):
    return pl.pallas_call(
        meet_kernel,
        out_shape=[jax.ShapeDtypeStruct((ROWS, B), BF16), jax.ShapeDtypeStruct((PIECE, B), F32)],
        in_specs=[SMEM] + [VMEM] * 4,
        out_specs=[VMEM] * 2,
        compiler_params=params(),
        cost_estimate=small_cost(1 << 15),
        name="meet_other_z",
    )(meta, *arrays)


def last_kernel(scaling, meta, own, crossed, w0, w1, w2, w3, out, weight_grad):
    for s in range(2):
        part = slice(s * B, (s + 1) * B)
        out[part] = (own[part].astype(F32) + crossed[part].astype(F32)).T.astype(BF16)
    rep = meta[PLACE]
    for back, piece in enumerate((w0, w1, w2, w3)):
        rows = pl.ds(pl.multiple_of(lax.rem(rep + 4 - back, 4) * 32, 32), 32)
        weight_grad[rows, 0:B] = piece[0:32] * scaling
        weight_grad[rows, B : 2 * B] = piece[32:64] * scaling


def last_sum(meta, scaling, *arrays):
    return pl.pallas_call(
        functools.partial(last_kernel, scaling),
        out_shape=[jax.ShapeDtypeStruct((ROWS, B), BF16), jax.ShapeDtypeStruct((B, 2 * B), F32)],
        in_specs=[SMEM] + [VMEM] * 6,
        out_specs=[VMEM] * 2,
        compiler_params=params(),
        cost_estimate=small_cost(1 << 16),
        name="last_sum",
    )(meta, *arrays)


def per_device(features, adjacency, block_list, block_counts, weight, cotangent):
    stored = adjacency[0, 0]
    r = lax.axis_index("row").astype(jnp.int32)
    rep = lax.axis_index("rep").astype(jnp.int32)
    core = r % 2
    nodes = float(features.shape[0] * 256)

    order = [entry for call in FORWARD_GROUPS for part in call for entry in part]
    back_order = [entry for part in BACKWARD_GROUPS for entry in part]
    meta = jnp.concatenate(
        [
            block_list.reshape(-1),
            block_counts.reshape(-1),
            section_order(r, order, -1),
            section_order(r, back_order, 1),
            jnp.stack([rep, core]),
        ]
    )

    near_unit, far_unit = cross(features, True), other_z(features)
    pair = pair_up(core.reshape(1), features, near_unit, far_unit)
    pairs = [pair] + [small_axis(pair, d) for d in (1, 2, 3)]
    touched = touch(meta, stored)
    (quad,) = place("place_quad", [[(n, 0, 2) for n in range(4)]], pairs, [touched])
    n1, n3 = large_axis(quad, 1), large_axis(quad, 3)
    (acc,) = forward(meta, stored, 0, [quad], None, False)
    parts = [[(0, 0, 8), (1, 0, 8), (2, 0, 8)], [(1, 0, 4)], [(2, 4, 4)]]
    near, h1, h3 = place("place_near", parts, [quad, n1, n3], [acc])
    f1, f3 = large_axis(h1, 1), large_axis(h3, 3)
    near_s = sibling(near)
    (acc,) = forward(meta, stored, 8, [n1, n3], acc, False, after=[h1])
    (far,) = place("place_far", [[(0, 0, 4), (1, 0, 4)]], [f1, f3], [acc])
    far_s = sibling(far)
    (acc,) = forward(meta, stored, 24, [near_s], acc, False)
    own_part, *pieces = forward(meta, stored, 48, [far, far_s], acc, True)

    pieces = [turn(piece, d + 1) for d, piece in enumerate(pieces)]
    activations, values, m1, m2, m3, w = middle(meta, own_part, pieces, weight, cotangent)
    messages = [turn(m1, 1), turn(m2, 2), turn(m3, 3)]

    bwd = functools.partial(backward, meta, stored, [values] + messages)
    far_b, w4 = bwd(0, (8,), extra=[w] + messages, finish=gather_terms, tails=(SPLIT,), extra_out=[w])
    far_s = sibling(far_b)
    (near_b,) = bwd(8, (16,), extra=[far_b])
    h1, h3, w8, near_b = bwd(
        24, (4, 4), far_s, extra=[w4, far_s, near_b], finish=sibling_terms, tails=(SPLIT, 0), extra_out=[w, near_b]
    )
    f1, f3, near_s = large_axis(h1, 1), large_axis(h3, 3), sibling(near_b)
    (own_b,) = bwd(32, (8,), extra=[h1])
    g1, g3, own_b = bwd(
        40,
        (8, 8),
        near_s,
        extra=[f1, f3, w8, own_b],
        finish=spread_terms,
        tails=(2 * SPLIT, SPLIT),
        extra_out=[own_b],
    )
    r1, r3, own_s = large_axis(g1, 1), large_axis(g3, 3), sibling(own_b)
    (g0,) = bwd(56, (8,), own_s, extra=[g1])
    t0, t1, t2, t3, w32 = sum_groups(g0, r1, r3, w8)
    sums = [t0, small_axis(t1, 1), small_axis(t2, 2), small_axis(t3, 3)]
    mine, w = sum_mine(meta, *sums, w32)
    far = other_z(mine)
    w_z = row_permute(w, lambda y, x, z, c: at(y, x, 1 - z, c))
    crossed = cross(sum_other(meta, mine, *sums), False)
    own, w = meet(meta, mine, far, w, w_z)
    feature_grad, weight_grad = last_sum(
        meta, nodes ** (-0.5), own, crossed, w, *[turn(w, d) for d in (1, 2, 3)]
    )
    return activations, feature_grad, weight_grad


def solution(mesh):
    in_specs = (
        P(("row", "rep"), None),
        P("row", "rep", None, None, None),
        P("row", "rep", None, None, None),
        P("row", "rep", None),
        P(),
        P(("row", "rep"), None),
    )
    out_specs = (P(("row", "rep"), None), P(("row", "rep"), None), P())
    return jax.shard_map(
        per_device, mesh=mesh, in_specs=in_specs, out_specs=out_specs, check_vma=False
    )
```

```python
import functools

import jax
import jax.numpy as jnp
import numpy as np
from jax import lax
from jax.experimental import pallas as pl
from jax.experimental.pallas import tpu as pltpu
from jax.sharding import PartitionSpec as P

B = 128
SLOTS = 4
BROWS = 8
SECTIONS = 64
ROWS = 2 * B
PIECE = 64
SPLIT = 3 * PIECE
COST = B * B * 8
LONG = 1 << 40
F32 = jnp.float32
BF16 = jnp.bfloat16
VMEM = pl.BlockSpec(memory_space=pltpu.VMEM)
SMEM = pl.BlockSpec(memory_space=pltpu.SMEM)

COUNTS = SECTIONS * SLOTS * 3
FORWARD_ORDER = COUNTS + SECTIONS
BACKWARD_ORDER = FORWARD_ORDER + SECTIONS
PLACE = BACKWARD_ORDER + SECTIONS


def group(flip, e, ds=(0, 1, 2, 3)):
    return [(flip, e, d, u) for d in ds for u in range(2)]


FORWARD_GROUPS = [
    [group(0, 0)],
    [group(0, 1), group(0, 3)],
    [group(1, 0), group(1, 1), group(1, 3)],
    [group(0, 2), group(1, 2)],
]
LOW, HIGH = (0, 1), (2, 3)
BACKWARD_GROUPS = [
    group(1, 2),
    group(1, 1, HIGH) + group(1, 3, LOW) + group(1, 1, LOW) + group(1, 3, HIGH),
    group(0, 2),
    group(1, 0),
    group(0, 1, HIGH) + group(0, 3, LOW),
    group(0, 1, LOW) + group(0, 3, HIGH),
    group(0, 0),
]


def section_order(r, entries, sign):
    flip, e, d, u = (np.array(column, np.int32) for column in zip(*entries))
    y, x, z, core = r // 16, (r // 4) % 4, (r // 2) % 2, r % 2
    role = core ^ flip
    dy, dx = jnp.where(role == 0, e, d), jnp.where(role == 0, d, e)
    return ((y + sign * dy) & 3) * 16 + ((x + sign * dx) & 3) * 4 + (z ^ role) * 2 + u


def at(y, x, z, core):
    return (y % 4) * 16 + (x % 4) * 4 + z * 2 + core


def row_permute(array, target):
    pairs = []
    for r in range(64):
        to = target(r // 16, (r // 4) % 4, (r // 2) % 2, r % 2)
        if to is not None:
            pairs.append((r, to))
    return lax.ppermute(array, "row", pairs)


def small_axis(array, d):
    return row_permute(array, lambda y, x, z, c: at(y + d * c, x + d * (1 - c), z, c))


def large_axis(array, e):
    return row_permute(array, lambda y, x, z, c: at(y + e * (1 - c), x + e * c, z, c))


def sibling(array):
    return row_permute(array, lambda y, x, z, c: at(y, x, z, 1 - c))


def cross(array, forwards):
    if forwards:
        return row_permute(array, lambda y, x, z, c: at(y, x, z, 0) if c else at(y, x, 1 - z, 1))
    return row_permute(array, lambda y, x, z, c: at(y, x, 1 - z, 0) if c else at(y, x, z, 1))


def other_z(array):
    return row_permute(array, lambda y, x, z, c: at(y, x, 1 - z, 1) if c else None)


def turn(array, d):
    return lax.ppermute(array, "rep", [(q, (q + d) % 4) for q in range(4)])


def params():
    return pltpu.CompilerParams(vmem_limit_bytes=20 * 1024 * 1024)


def cost(slots):
    return pl.CostEstimate(flops=slots * COST, bytes_accessed=slots * COST, transcendentals=0)


def small_cost(size):
    return pl.CostEstimate(flops=size // 64, bytes_accessed=size // 64, transcendentals=0)


def touch_kernel(meta, stored, out):
    out[...] = stored[0, 0:16, :].astype(F32)


def touch(meta, stored):
    return pl.pallas_call(
        touch_kernel,
        out_shape=jax.ShapeDtypeStruct((16, B), F32),
        in_specs=[SMEM, VMEM],
        out_specs=VMEM,
        compiler_params=params(),
        cost_estimate=small_cost(1 << 10),
        name="touch_blocks",
    )(meta, stored)


def pair_up_kernel(core, own, near, far, out):
    first = core[0] == 0
    out[0:ROWS] = jnp.where(first, own[...], near[...])
    out[ROWS : 2 * ROWS] = jnp.where(first, near[...], far[...])


def pair_up(core, own, near, far):
    return pl.pallas_call(
        pair_up_kernel,
        out_shape=jax.ShapeDtypeStruct((2 * ROWS, B), BF16),
        in_specs=[SMEM] + [VMEM] * 3,
        out_specs=VMEM,
        compiler_params=params(),
        cost_estimate=small_cost(1 << 16),
        name="pair_up",
    )(core, own, near, far)


def place_kernel(counts, parts, *refs):
    sources, outs = refs[: len(counts)], refs[-len(parts) :]
    for out, pieces in zip(outs, parts):
        row = 0
        for source, start, size in pieces:
            out[row : row + size * ROWS] = sources[source][start * ROWS : (start + size) * ROWS]
            row += size * ROWS


def place(name, parts, sources, after=(), size=1 << 18):
    shapes = [jax.ShapeDtypeStruct((sum(p[2] for p in pieces) * ROWS, B), BF16) for pieces in parts]
    args = [*sources, *after]
    return pl.pallas_call(
        functools.partial(place_kernel, tuple(range(len(sources))), parts),
        out_shape=shapes,
        in_specs=[VMEM] * len(args),
        out_specs=[VMEM] * len(shapes),
        compiler_params=params(),
        cost_estimate=small_cost(size),
        name=name,
    )(*args)


STEP = 4


def forward_kernel(first_section, sizes, first, last, after, *refs):
    meta, stored = refs[:2]
    chunk_refs = refs[2 : 2 + len(sizes)]
    refs = refs[2 + len(sizes) + after :]
    if first:
        out_refs, acc = refs[:-1], refs[-1]
        acc[...] = jnp.zeros_like(acc)
    else:
        out_refs, acc = refs[1:-1], refs[-1]
        acc[0:BROWS] = refs[0][...]
    begin = first_section
    for size, chunk_ref in zip(sizes, chunk_refs):

        def step(g, carry, begin=begin, chunk_ref=chunk_ref):
            products, places = [], []
            for n in range(STEP):
                sid = meta[FORWARD_ORDER + begin + g * STEP + n]
                count = meta[COUNTS + sid]
                for k in range(SLOTS):
                    base = sid * (SLOTS * 3) + 3 * k
                    start = pl.multiple_of((g * STEP + n) * ROWS + meta[base + 1] * B, B)
                    source = chunk_ref[pl.ds(start, B)]
                    products.append(jnp.dot(stored[meta[base + 2]], source, preferred_element_type=F32))
                    places.append(jnp.where(k < count, meta[base], BROWS))
            for product, place in zip(products, places):
                acc[place] += product
            return carry

        lax.fori_loop(0, size // STEP, step, 0)
        begin += size
    if not last:
        out_refs[0][...] = acc[0:BROWS]
        return
    rep = meta[PLACE]
    for d in range(4):
        for b in range(2):
            piece = acc[lax.rem(rep + d, 4) * 2 + b]
            out_refs[d][b * B : (b + 1) * B] = piece.astype(out_refs[d].dtype)


def forward(meta, stored, first_section, chunk_list, start, last, after=()):
    sizes = tuple(chunk.shape[0] // ROWS for chunk in chunk_list)
    first = start is None
    if last:
        out_shape = [jax.ShapeDtypeStruct((2 * B, B), F32)] + [jax.ShapeDtypeStruct((2 * B, B), BF16)] * 3
    else:
        out_shape = [jax.ShapeDtypeStruct((BROWS, B, B), F32)]
    args = [meta, stored, *chunk_list, *after] + ([] if first else [start])
    return pl.pallas_call(
        functools.partial(forward_kernel, first_section, sizes, first, last, len(after)),
        out_shape=out_shape,
        in_specs=[SMEM] + [VMEM] * (len(args) - 1),
        out_specs=[VMEM] * len(out_shape),
        scratch_shapes=[pltpu.VMEM((BROWS + 1, B, B), F32)],
        compiler_params=params(),
        cost_estimate=cost(sum(sizes) * SLOTS),
        name="forward_slots",
    )(*args)


def middle_kernel(meta, own, p1, p2, p3, weight, cot, act, values, m1, m2, m3, w0):
    pooled = (own[...] + p1[...].astype(F32) + p2[...].astype(F32) + p3[...].astype(F32)).astype(BF16)
    hidden = jnp.dot(pooled, weight[...], preferred_element_type=F32)
    squash = jax.nn.sigmoid(hidden)
    act[...] = (hidden * squash).astype(BF16)
    slope = (cot[...].astype(F32) * squash * (1.0 + hidden * (1.0 - squash))).astype(BF16)
    values_t = lax.dot_general(weight[...], slope, (((1,), (1,)), ((), ())), preferred_element_type=F32)
    values_t = values_t.astype(BF16)
    for out in (values, m1, m2, m3):
        out[0:B] = values_t[:, :B]
        out[B:ROWS] = values_t[:, B:]
    term = lax.dot_general(pooled, slope, (((0,), (0,)), ((), ())), preferred_element_type=F32)
    rep = meta[PLACE]
    for q in range(4):
        piece = jnp.concatenate([term[q * 32 : (q + 1) * 32, :B], term[q * 32 : (q + 1) * 32, B:]], axis=0)

        @pl.when(rep == q)
        def _(piece=piece):
            w0[...] = piece

        for d, out in enumerate((m1, m2, m3)):

            @pl.when(lax.rem(rep + d + 1, 4) == q)
            def _(out=out, piece=piece):
                out[ROWS : ROWS + PIECE] = piece.astype(BF16)


def middle(meta, own, pieces, weight, cot):
    return pl.pallas_call(
        middle_kernel,
        out_shape=[jax.ShapeDtypeStruct((2 * B, 2 * B), BF16), jax.ShapeDtypeStruct((ROWS, B), BF16)]
        + [jax.ShapeDtypeStruct((ROWS + PIECE, B), BF16)] * 3
        + [jax.ShapeDtypeStruct((PIECE, B), F32)],
        in_specs=[SMEM] + [VMEM] * 6,
        out_specs=[VMEM] * 6,
        compiler_params=params(),
        cost_estimate=small_cost(1 << 16),
        name="middle_rows",
    )(meta, own, *pieces, weight, cot)


def split(total, out_ref, row):
    rest = total
    for n in range(3):
        part = rest.astype(BF16)
        out_ref[row + n * PIECE : row + (n + 1) * PIECE] = part
        rest = rest - part.astype(F32)


def joined(ref, row):
    parts = [ref[row + n * PIECE : row + (n + 1) * PIECE].astype(F32) for n in range(3)]
    return (parts[2] + parts[1]) + parts[0]


def gather_terms(extra, outs, extra_outs):
    total = extra[0][...]
    for ref in extra[1:]:
        total = total + ref[ROWS : ROWS + PIECE].astype(F32)
    split(total, outs[0], 8 * ROWS)
    extra_outs[0][...] = total


def sibling_terms(extra, outs, extra_outs):
    total = extra[0][...] + joined(extra[1], 8 * ROWS)
    split(total, outs[0], 4 * ROWS)
    extra_outs[0][...] = total
    extra_outs[1][...] = extra[2][...]


def spread_terms(extra, outs, extra_outs):
    half_1, half_3, own = extra[:3]
    part = slice(0, 4 * ROWS)
    for out, half in zip(outs, (half_1, half_3)):
        out[part] = (out[part].astype(F32) + half[part].astype(F32)).astype(BF16)
        split(own[...], out, 4 * ROWS)
    outs[0][4 * ROWS + SPLIT :] = half_1[4 * ROWS :]


def pass_on(extra, outs, extra_outs):
    extra_outs[0][...] = extra[0][...]


def add_halves(extra, outs, extra_outs):
    for half, start in zip(extra[:2], (4 * ROWS, 0)):
        part = slice(start, start + 4 * ROWS)
        outs[0][part] = (outs[0][part].astype(F32) + half[...].astype(F32)).astype(BF16)


def backward_kernel(first_section, sizes, added, add_from, extras, finish, *refs):
    meta, stored = refs[:2]
    value_refs, refs = refs[2:6], refs[6:]
    if added:
        add_ref, refs = refs[0], refs[1:]
    extra, refs = refs[:extras], refs[extras:]
    out_refs, extra_outs, values = refs[: len(sizes)], refs[len(sizes) : -1], refs[-1]
    rep = meta[PLACE]
    for d in range(4):
        for b in range(2):
            values[lax.rem(rep + 4 - d, 4) * 2 + b] = value_refs[d][b * B : (b + 1) * B]
    values[BROWS] = jnp.zeros((B, B), BF16)

    begin = 0
    for size, out_ref in zip(sizes, out_refs):

        def step(g, carry, begin=begin, out_ref=out_ref):
            for m in range(STEP):
                n = g * STEP + m
                sid = meta[BACKWARD_ORDER + first_section + begin + n]
                count = meta[COUNTS + sid]
                base = sid * (SLOTS * 3)
                rows = []
                for j in range(2):
                    columns = []
                    for k in range(SLOTS):
                        live = (k < count) & (meta[base + 3 * k + 1] == j)
                        columns.append(values[jnp.where(live, meta[base + 3 * k], BROWS)])
                    rows.append(jnp.concatenate(columns, axis=1))
                left = jnp.concatenate(rows, axis=0)
                right = jnp.concatenate([stored[meta[base + 3 * k + 2]] for k in range(SLOTS)], axis=0)
                result = jnp.dot(left, right, preferred_element_type=F32)
                if added:
                    result = result + add_ref[pl.ds(pl.multiple_of((add_from + begin + n) * ROWS, ROWS), ROWS)].astype(F32)
                out_ref[pl.ds(pl.multiple_of(n * ROWS, ROWS), ROWS)] = result.astype(BF16)
            return carry

        lax.fori_loop(0, size // STEP, step, 0)
        begin += size
    if finish is not None:
        finish(extra, out_refs, extra_outs)


def backward(meta, stored, values, first_section, sizes, add=None, add_from=0, extra=(), finish=None, tails=None, extra_out=(), size=0):
    added = add is not None
    args = [meta, stored, *values] + ([add] if added else []) + list(extra)
    tails = tails or (0,) * len(sizes)
    shapes = [jax.ShapeDtypeStruct((size * ROWS + tail, B), BF16) for size, tail in zip(sizes, tails)]
    shapes += [jax.ShapeDtypeStruct(a.shape, a.dtype) for a in extra_out]
    return pl.pallas_call(
        functools.partial(backward_kernel, first_section, sizes, added, add_from, len(extra), finish),
        out_shape=shapes,
        in_specs=[SMEM] + [VMEM] * (len(args) - 1),
        out_specs=[VMEM] * len(shapes),
        scratch_shapes=[pltpu.VMEM((BROWS + 1, B, B), BF16)],
        compiler_params=params(),
        cost_estimate=small_cost(size) if size else cost(sum(sizes) * SLOTS),
        name="backward_slots",
    )(*args)


def sum_kernel(a, low, high, own, t0, t1, t2, t3, w):
    row = 4 * ROWS
    total = (own[...] + joined(low, row + SPLIT)) + (joined(low, row) + joined(high, row))
    w[...] = total
    for d, out in enumerate((t0, t1, t2, t3)):
        half_ref = high if d >= 2 else low
        part, half = (slice(2 * ROWS * n, 2 * ROWS * (n + 1)) for n in (d, d % 2))
        out[0 : 2 * ROWS] = (a[part].astype(F32) + half_ref[half].astype(F32)).astype(BF16)
        if d:
            split(total, out, 2 * ROWS)


def sum_groups(*arrays):
    return pl.pallas_call(
        sum_kernel,
        out_shape=[jax.ShapeDtypeStruct((2 * ROWS, B), BF16)]
        + [jax.ShapeDtypeStruct((2 * ROWS + SPLIT, B), BF16)] * 3
        + [jax.ShapeDtypeStruct((PIECE, B), F32)],
        in_specs=[VMEM] * 4,
        out_specs=[VMEM] * 5,
        compiler_params=params(),
        cost_estimate=small_cost(1 << 18),
        name="sum_groups",
    )(*arrays)


def unit_sum(meta, refs, out, flip):
    core = meta[PLACE + 1]
    unit = 1 - core if flip else core
    part = pl.ds(pl.multiple_of(unit * ROWS, ROWS), ROWS)
    total = refs[0][part].astype(F32)
    for ref in refs[1:]:
        total = total + ref[part].astype(F32)
    out[...] = total.astype(BF16)


def mine_kernel(meta, a, b, c, d, own, mine, w):
    unit_sum(meta, (a, b, c, d), mine, False)
    w[...] = (own[...] + joined(c, 2 * ROWS)) + (joined(b, 2 * ROWS) + joined(d, 2 * ROWS))


def sum_mine(meta, *arrays):
    return pl.pallas_call(
        mine_kernel,
        out_shape=[jax.ShapeDtypeStruct((ROWS, B), BF16), jax.ShapeDtypeStruct((PIECE, B), F32)],
        in_specs=[SMEM] + [VMEM] * 5,
        out_specs=[VMEM] * 2,
        compiler_params=params(),
        cost_estimate=small_cost(1 << 17),
        name="sum_mine",
    )(meta, *arrays)


def other_kernel(meta, mine, a, b, c, d, other):
    unit_sum(meta, (a, b, c, d), other, True)


def sum_other(meta, *arrays):
    return pl.pallas_call(
        other_kernel,
        out_shape=jax.ShapeDtypeStruct((ROWS, B), BF16),
        in_specs=[SMEM] + [VMEM] * 5,
        out_specs=VMEM,
        compiler_params=params(),
        cost_estimate=small_cost(1 << 17),
        name="sum_other",
    )(meta, *arrays)


def meet_kernel(meta, mine, far, w, w_z, own, total):
    first = meta[PLACE + 1] == 0
    own[...] = jnp.where(first, mine[...], far[...])
    total[...] = w[...] + w_z[...]


def meet(meta, *arrays):
    return pl.pallas_call(
        meet_kernel,
        out_shape=[jax.ShapeDtypeStruct((ROWS, B), BF16), jax.ShapeDtypeStruct((PIECE, B), F32)],
        in_specs=[SMEM] + [VMEM] * 4,
        out_specs=[VMEM] * 2,
        compiler_params=params(),
        cost_estimate=small_cost(1 << 15),
        name="meet_other_z",
    )(meta, *arrays)


def last_kernel(scaling, meta, own, crossed, w0, w1, w2, w3, out, weight_grad):
    for s in range(2):
        part = slice(s * B, (s + 1) * B)
        out[part] = (own[part].astype(F32) + crossed[part].astype(F32)).T.astype(BF16)
    rep = meta[PLACE]
    for back, piece in enumerate((w0, w1, w2, w3)):
        rows = pl.ds(pl.multiple_of(lax.rem(rep + 4 - back, 4) * 32, 32), 32)
        weight_grad[rows, 0:B] = piece[0:32] * scaling
        weight_grad[rows, B : 2 * B] = piece[32:64] * scaling


def last_sum(meta, scaling, *arrays):
    return pl.pallas_call(
        functools.partial(last_kernel, scaling),
        out_shape=[jax.ShapeDtypeStruct((ROWS, B), BF16), jax.ShapeDtypeStruct((B, 2 * B), F32)],
        in_specs=[SMEM] + [VMEM] * 6,
        out_specs=[VMEM] * 2,
        compiler_params=params(),
        cost_estimate=small_cost(1 << 16),
        name="last_sum",
    )(meta, *arrays)


def per_device(features, adjacency, block_list, block_counts, weight, cotangent):
    stored = adjacency[0, 0]
    r = lax.axis_index("row").astype(jnp.int32)
    rep = lax.axis_index("rep").astype(jnp.int32)
    core = r % 2
    nodes = float(features.shape[0] * 256)

    order = [entry for call in FORWARD_GROUPS for part in call for entry in part]
    back_order = [entry for part in BACKWARD_GROUPS for entry in part]
    meta = jnp.concatenate(
        [
            block_list.reshape(-1),
            block_counts.reshape(-1),
            section_order(r, order, -1),
            section_order(r, back_order, 1),
            jnp.stack([rep, core]),
        ]
    )

    near_unit, far_unit = cross(features, True), other_z(features)
    pair = pair_up(core.reshape(1), features, near_unit, far_unit)
    x1, x2, x3 = small_axis(pair, 1), small_axis(pair, 2), small_axis(pair, 3)
    touched = touch(meta, stored)
    (low,) = place("place_low", [[(0, 0, 2), (1, 0, 2)]], [pair, x1])
    n1_low, n3_low = large_axis(low, 1), large_axis(low, 3)
    (high,) = place("place_high", [[(0, 0, 2), (1, 0, 2)]], [x2, x3], [touched, low])
    n1_high, n3_high = large_axis(high, 1), large_axis(high, 3)
    (acc,) = forward(meta, stored, 0, [low, high], None, False)
    f1, f3 = large_axis(n1_low, 1), large_axis(n3_high, 3)
    halves = [low, high, n1_low, n1_high, n3_low, n3_high]
    (near,) = place("place_near", [[(n, 0, 4) for n in range(6)]], halves, [acc])
    near_s = sibling(near)
    (acc,) = forward(meta, stored, 8, halves[2:], acc, False)
    (far,) = place("place_far", [[(0, 0, 4), (1, 0, 4)]], [f1, f3], [acc], size=LONG)
    far_s = sibling(far)
    (acc,) = forward(meta, stored, 24, [near_s], acc, False)
    own_part, *pieces = forward(meta, stored, 48, [far, far_s], acc, True)

    pieces = [turn(piece, d + 1) for d, piece in enumerate(pieces)]
    activations, values, m1, m2, m3, w = middle(meta, own_part, pieces, weight, cotangent)
    messages = [turn(m1, 1), turn(m2, 2), turn(m3, 3)]

    bwd = functools.partial(backward, meta, stored, [values] + messages)
    far_b, w4 = bwd(0, (8,), extra=[w] + messages, finish=gather_terms, tails=(SPLIT,), extra_out=[w])
    far_s = sibling(far_b)
    (near_b,) = bwd(8, (16,), extra=[far_b])
    h1, h3, w8, near_b = bwd(
        24, (4, 4), far_s, extra=[w4, far_s, near_b], finish=sibling_terms, tails=(SPLIT, 0), extra_out=[w, near_b]
    )
    f1, f3, near_s = large_axis(h1, 1), large_axis(h3, 3), sibling(near_b)
    (own_b,) = bwd(32, (8,), extra=[h1])
    g1_high, g3_low, own_b = bwd(40, (4, 4), near_s, extra=[own_b], finish=pass_on, extra_out=[own_b])
    r1_high, r3_low = large_axis(g1_high, 1), large_axis(g3_low, 3)
    own_s = sibling(own_b)
    g1_low, g3_high = bwd(
        48,
        (4, 4),
        near_s,
        add_from=8,
        extra=[f1, f3, w8, g1_high],
        finish=spread_terms,
        tails=(2 * SPLIT, SPLIT),
        size=LONG,
    )
    r1_low, r3_high = large_axis(g1_low, 1), large_axis(g3_high, 3)
    (g0,) = bwd(56, (8,), own_s, extra=[r1_high, r3_low, g1_low], finish=add_halves, size=LONG)
    t0, t1, t2, t3, w32 = sum_groups(g0, r1_low, r3_high, w8)
    sums = [t0, small_axis(t1, 1), small_axis(t2, 2), small_axis(t3, 3)]
    mine, w = sum_mine(meta, *sums, w32)
    far = other_z(mine)
    w_z = row_permute(w, lambda y, x, z, c: at(y, x, 1 - z, c))
    crossed = cross(sum_other(meta, mine, *sums), False)
    own, w = meet(meta, mine, far, w, w_z)
    feature_grad, weight_grad = last_sum(
        meta, nodes ** (-0.5), own, crossed, w, *[turn(w, d) for d in (1, 2, 3)]
    )
    return activations, feature_grad, weight_grad


def solution(mesh):
    in_specs = (
        P(("row", "rep"), None),
        P("row", "rep", None, None, None),
        P("row", "rep", None, None, None),
        P("row", "rep", None),
        P(),
        P(("row", "rep"), None),
    )
    out_specs = (P(("row", "rep"), None), P(("row", "rep"), None), P())
    return jax.shard_map(
        per_device, mesh=mesh, in_specs=in_specs, out_specs=out_specs, check_vma=False
    )
```

```python
import functools

import jax
import jax.numpy as jnp
import numpy as np
from jax import lax
from jax.experimental import pallas as pl
from jax.experimental.pallas import tpu as pltpu
from jax.sharding import PartitionSpec as P

B = 128
SLOTS = 4
BROWS = 8
SECTIONS = 64
ROWS = 2 * B
PIECE = 64
SPLIT = 3 * PIECE
COST = B * B * 8
LONG = 1 << 40
F32 = jnp.float32
BF16 = jnp.bfloat16
VMEM = pl.BlockSpec(memory_space=pltpu.VMEM)
SMEM = pl.BlockSpec(memory_space=pltpu.SMEM)

COUNTS = SECTIONS * SLOTS * 3
FORWARD_ORDER = COUNTS + SECTIONS
BACKWARD_ORDER = FORWARD_ORDER + SECTIONS
PLACE = BACKWARD_ORDER + SECTIONS


def group(flip, e, ds=(0, 1, 2, 3)):
    return [(flip, e, d, u) for d in ds for u in range(2)]


FORWARD_GROUPS = [
    [group(0, 0)],
    [group(0, 1), group(0, 3)],
    [group(1, 0), group(1, 1), group(1, 3)],
    [group(0, 2), group(1, 2)],
]
LOW, HIGH = (0, 1), (2, 3)
BACKWARD_GROUPS = [
    group(1, 2),
    group(1, 1, HIGH) + group(1, 3, LOW) + group(1, 1, LOW) + group(1, 3, HIGH),
    group(0, 2),
    group(1, 0),
    group(0, 1, HIGH) + group(0, 3, LOW),
    group(0, 1, LOW) + group(0, 3, HIGH),
    group(0, 0),
]


def section_order(r, entries, sign):
    flip, e, d, u = (np.array(column, np.int32) for column in zip(*entries))
    y, x, z, core = r // 16, (r // 4) % 4, (r // 2) % 2, r % 2
    role = core ^ flip
    dy, dx = jnp.where(role == 0, e, d), jnp.where(role == 0, d, e)
    return ((y + sign * dy) & 3) * 16 + ((x + sign * dx) & 3) * 4 + (z ^ role) * 2 + u


def at(y, x, z, core):
    return (y % 4) * 16 + (x % 4) * 4 + z * 2 + core


def row_permute(array, target):
    pairs = []
    for r in range(64):
        to = target(r // 16, (r // 4) % 4, (r // 2) % 2, r % 2)
        if to is not None:
            pairs.append((r, to))
    return lax.ppermute(array, "row", pairs)


def small_axis(array, d):
    return row_permute(array, lambda y, x, z, c: at(y + d * c, x + d * (1 - c), z, c))


def large_axis(array, e):
    return row_permute(array, lambda y, x, z, c: at(y + e * (1 - c), x + e * c, z, c))


def sibling(array):
    return row_permute(array, lambda y, x, z, c: at(y, x, z, 1 - c))


def cross(array, forwards):
    if forwards:
        return row_permute(array, lambda y, x, z, c: at(y, x, z, 0) if c else at(y, x, 1 - z, 1))
    return row_permute(array, lambda y, x, z, c: at(y, x, 1 - z, 0) if c else at(y, x, z, 1))


def other_z(array):
    return row_permute(array, lambda y, x, z, c: at(y, x, 1 - z, 1) if c else None)


def turn(array, d):
    return lax.ppermute(array, "rep", [(q, (q + d) % 4) for q in range(4)])


def params():
    return pltpu.CompilerParams(vmem_limit_bytes=20 * 1024 * 1024)


def cost(slots):
    return pl.CostEstimate(flops=slots * COST, bytes_accessed=slots * COST, transcendentals=0)


def small_cost(size):
    return pl.CostEstimate(flops=size // 64, bytes_accessed=size // 64, transcendentals=0)


def pair_up_kernel(core, own, near, far, out):
    first = core[0] == 0
    out[0:ROWS] = jnp.where(first, own[...], near[...])
    out[ROWS : 2 * ROWS] = jnp.where(first, near[...], far[...])


def pair_up(core, own, near, far):
    return pl.pallas_call(
        pair_up_kernel,
        out_shape=jax.ShapeDtypeStruct((2 * ROWS, B), BF16),
        in_specs=[SMEM] + [VMEM] * 3,
        out_specs=VMEM,
        compiler_params=params(),
        cost_estimate=small_cost(LONG),
        name="pair_up",
    )(core, own, near, far)


def place_kernel(counts, parts, *refs):
    sources, outs = refs[: len(counts)], refs[-len(parts) :]
    for out, pieces in zip(outs, parts):
        row = 0
        for source, start, size in pieces:
            out[row : row + size * ROWS] = sources[source][start * ROWS : (start + size) * ROWS]
            row += size * ROWS


def place(name, parts, sources, after=(), size=1 << 18):
    shapes = [jax.ShapeDtypeStruct((sum(p[2] for p in pieces) * ROWS, B), BF16) for pieces in parts]
    args = [*sources, *after]
    return pl.pallas_call(
        functools.partial(place_kernel, tuple(range(len(sources))), parts),
        out_shape=shapes,
        in_specs=[VMEM] * len(args),
        out_specs=[VMEM] * len(shapes),
        compiler_params=params(),
        cost_estimate=small_cost(size),
        name=name,
    )(*args)


STEP = 4


def forward_kernel(first_section, sizes, first, last, after, *refs):
    meta, stored = refs[:2]
    chunk_refs = refs[2 : 2 + len(sizes)]
    refs = refs[2 + len(sizes) + after :]
    if first:
        out_refs, acc = refs[:-1], refs[-1]
        acc[...] = jnp.zeros_like(acc)
    else:
        out_refs, acc = refs[1:-1], refs[-1]
        acc[0:BROWS] = refs[0][...]
    begin = first_section
    for size, chunk_ref in zip(sizes, chunk_refs):

        def step(g, carry, begin=begin, chunk_ref=chunk_ref):
            products, places = [], []
            for n in range(STEP):
                sid = meta[FORWARD_ORDER + begin + g * STEP + n]
                count = meta[COUNTS + sid]
                for k in range(SLOTS):
                    base = sid * (SLOTS * 3) + 3 * k
                    start = pl.multiple_of((g * STEP + n) * ROWS + meta[base + 1] * B, B)
                    source = chunk_ref[pl.ds(start, B)]
                    products.append(jnp.dot(stored[meta[base + 2]], source, preferred_element_type=F32))
                    places.append(jnp.where(k < count, meta[base], BROWS))
            for product, place in zip(products, places):
                acc[place] += product
            return carry

        lax.fori_loop(0, size // STEP, step, 0)
        begin += size
    if not last:
        out_refs[0][...] = acc[0:BROWS]
        return
    rep = meta[PLACE]
    for d in range(4):
        for b in range(2):
            piece = acc[lax.rem(rep + d, 4) * 2 + b]
            out_refs[d][b * B : (b + 1) * B] = piece.astype(out_refs[d].dtype)


def forward(meta, stored, first_section, chunk_list, start, last, after=()):
    sizes = tuple(chunk.shape[0] // ROWS for chunk in chunk_list)
    first = start is None
    if last:
        out_shape = [jax.ShapeDtypeStruct((2 * B, B), F32)] + [jax.ShapeDtypeStruct((2 * B, B), BF16)] * 3
    else:
        out_shape = [jax.ShapeDtypeStruct((BROWS, B, B), F32)]
    args = [meta, stored, *chunk_list, *after] + ([] if first else [start])
    return pl.pallas_call(
        functools.partial(forward_kernel, first_section, sizes, first, last, len(after)),
        out_shape=out_shape,
        in_specs=[SMEM] + [VMEM] * (len(args) - 1),
        out_specs=[VMEM] * len(out_shape),
        scratch_shapes=[pltpu.VMEM((BROWS + 1, B, B), F32)],
        compiler_params=params(),
        cost_estimate=cost(sum(sizes) * SLOTS),
        name="forward_slots",
    )(*args)


def middle_kernel(meta, own, p1, p2, p3, weight, cot, act, values, m1, m2, m3, w0):
    pooled = (own[...] + p1[...].astype(F32) + p2[...].astype(F32) + p3[...].astype(F32)).astype(BF16)
    hidden = jnp.dot(pooled, weight[...], preferred_element_type=F32)
    squash = jax.nn.sigmoid(hidden)
    act[...] = (hidden * squash).astype(BF16)
    slope = (cot[...].astype(F32) * squash * (1.0 + hidden * (1.0 - squash))).astype(BF16)
    values_t = lax.dot_general(weight[...], slope, (((1,), (1,)), ((), ())), preferred_element_type=F32)
    values_t = values_t.astype(BF16)
    for out in (values, m1, m2, m3):
        out[0:B] = values_t[:, :B]
        out[B:ROWS] = values_t[:, B:]
    term = lax.dot_general(pooled, slope, (((0,), (0,)), ((), ())), preferred_element_type=F32)
    rep = meta[PLACE]
    for q in range(4):
        piece = jnp.concatenate([term[q * 32 : (q + 1) * 32, :B], term[q * 32 : (q + 1) * 32, B:]], axis=0)

        @pl.when(rep == q)
        def _(piece=piece):
            w0[...] = piece

        for d, out in enumerate((m1, m2, m3)):

            @pl.when(lax.rem(rep + d + 1, 4) == q)
            def _(out=out, piece=piece):
                out[ROWS : ROWS + PIECE] = piece.astype(BF16)


def middle(meta, own, pieces, weight, cot):
    return pl.pallas_call(
        middle_kernel,
        out_shape=[jax.ShapeDtypeStruct((2 * B, 2 * B), BF16), jax.ShapeDtypeStruct((ROWS, B), BF16)]
        + [jax.ShapeDtypeStruct((ROWS + PIECE, B), BF16)] * 3
        + [jax.ShapeDtypeStruct((PIECE, B), F32)],
        in_specs=[SMEM] + [VMEM] * 6,
        out_specs=[VMEM] * 6,
        compiler_params=params(),
        cost_estimate=small_cost(1 << 16),
        name="middle_rows",
    )(meta, own, *pieces, weight, cot)


def split(total, out_ref, row):
    rest = total
    for n in range(3):
        part = rest.astype(BF16)
        out_ref[row + n * PIECE : row + (n + 1) * PIECE] = part
        rest = rest - part.astype(F32)


def joined(ref, row):
    parts = [ref[row + n * PIECE : row + (n + 1) * PIECE].astype(F32) for n in range(3)]
    return (parts[2] + parts[1]) + parts[0]


def gather_terms(extra, outs, extra_outs):
    total = extra[0][...]
    for ref in extra[1:]:
        total = total + ref[ROWS : ROWS + PIECE].astype(F32)
    split(total, outs[0], 8 * ROWS)
    extra_outs[0][...] = total


def sibling_terms(extra, outs, extra_outs):
    total = extra[0][...] + joined(extra[1], 8 * ROWS)
    extra_outs[0][...] = total
    extra_outs[1][...] = extra[2][...]


def spread_terms(extra, outs, extra_outs):
    half_1, half_3, own, other = extra[:4]
    total = own[...] + other[...]
    for out, half in zip(outs, (half_1, half_3)):
        part = slice(0, 4 * ROWS)
        out[part] = (out[part].astype(F32) + half[...].astype(F32)).astype(BF16)
        split(total, out, 4 * ROWS)
    extra_outs[0][...] = total


def pass_on(extra, outs, extra_outs):
    extra_outs[0][...] = extra[0][...]


def add_halves(extra, outs, extra_outs):
    for half, start in zip(extra[:2], (4 * ROWS, 0)):
        part = slice(start, start + 4 * ROWS)
        outs[0][part] = (outs[0][part].astype(F32) + half[...].astype(F32)).astype(BF16)


def backward_kernel(first_section, sizes, added, add_from, extras, finish, *refs):
    meta, stored = refs[:2]
    value_refs, refs = refs[2:6], refs[6:]
    if added:
        add_ref, refs = refs[0], refs[1:]
    extra, refs = refs[:extras], refs[extras:]
    out_refs, extra_outs, values = refs[: len(sizes)], refs[len(sizes) : -1], refs[-1]
    rep = meta[PLACE]
    for d in range(4):
        for b in range(2):
            values[lax.rem(rep + 4 - d, 4) * 2 + b] = value_refs[d][b * B : (b + 1) * B]
    values[BROWS] = jnp.zeros((B, B), BF16)

    begin = 0
    for size, out_ref in zip(sizes, out_refs):

        def step(g, carry, begin=begin, out_ref=out_ref):
            for m in range(STEP):
                n = g * STEP + m
                sid = meta[BACKWARD_ORDER + first_section + begin + n]
                count = meta[COUNTS + sid]
                base = sid * (SLOTS * 3)
                rows = []
                for j in range(2):
                    columns = []
                    for k in range(SLOTS):
                        live = (k < count) & (meta[base + 3 * k + 1] == j)
                        columns.append(values[jnp.where(live, meta[base + 3 * k], BROWS)])
                    rows.append(jnp.concatenate(columns, axis=1))
                left = jnp.concatenate(rows, axis=0)
                right = jnp.concatenate([stored[meta[base + 3 * k + 2]] for k in range(SLOTS)], axis=0)
                result = jnp.dot(left, right, preferred_element_type=F32)
                if added:
                    result = result + add_ref[pl.ds(pl.multiple_of((add_from + begin + n) * ROWS, ROWS), ROWS)].astype(F32)
                out_ref[pl.ds(pl.multiple_of(n * ROWS, ROWS), ROWS)] = result.astype(BF16)
            return carry

        lax.fori_loop(0, size // STEP, step, 0)
        begin += size
    if finish is not None:
        finish(extra, out_refs, extra_outs)


def backward(meta, stored, values, first_section, sizes, add=None, add_from=0, extra=(), finish=None, tails=None, extra_out=(), size=0):
    added = add is not None
    args = [meta, stored, *values] + ([add] if added else []) + list(extra)
    tails = tails or (0,) * len(sizes)
    shapes = [jax.ShapeDtypeStruct((size * ROWS + tail, B), BF16) for size, tail in zip(sizes, tails)]
    shapes += [jax.ShapeDtypeStruct(a.shape, a.dtype) for a in extra_out]
    return pl.pallas_call(
        functools.partial(backward_kernel, first_section, sizes, added, add_from, len(extra), finish),
        out_shape=shapes,
        in_specs=[SMEM] + [VMEM] * (len(args) - 1),
        out_specs=[VMEM] * len(shapes),
        scratch_shapes=[pltpu.VMEM((BROWS + 1, B, B), BF16)],
        compiler_params=params(),
        cost_estimate=small_cost(size) if size else cost(sum(sizes) * SLOTS),
        name="backward_slots",
    )(*args)


def sum_kernel(a, low, high, own, two, t0, t1, t2, t3, w):
    row = 4 * ROWS
    total = (own[...] + two[...]) + (joined(low, row) + joined(high, row))
    w[...] = total
    for d, out in enumerate((t0, t1, t2, t3)):
        half_ref = high if d >= 2 else low
        part, half = (slice(2 * ROWS * n, 2 * ROWS * (n + 1)) for n in (d, d % 2))
        out[0 : 2 * ROWS] = (a[part].astype(F32) + half_ref[half].astype(F32)).astype(BF16)
        if d:
            split(total, out, 2 * ROWS)


def sum_groups(*arrays):
    return pl.pallas_call(
        sum_kernel,
        out_shape=[jax.ShapeDtypeStruct((2 * ROWS, B), BF16)]
        + [jax.ShapeDtypeStruct((2 * ROWS + SPLIT, B), BF16)] * 3
        + [jax.ShapeDtypeStruct((PIECE, B), F32)],
        in_specs=[VMEM] * 5,
        out_specs=[VMEM] * 5,
        compiler_params=params(),
        cost_estimate=small_cost(1 << 18),
        name="sum_groups",
    )(*arrays)


def unit_sum(meta, refs, out, flip):
    core = meta[PLACE + 1]
    unit = 1 - core if flip else core
    part = pl.ds(pl.multiple_of(unit * ROWS, ROWS), ROWS)
    total = refs[0][part].astype(F32)
    for ref in refs[1:]:
        total = total + ref[part].astype(F32)
    out[...] = total.astype(BF16)


def mine_kernel(meta, a, b, c, d, own, mine, w):
    unit_sum(meta, (a, b, c, d), mine, False)
    w[...] = (own[...] + joined(c, 2 * ROWS)) + (joined(b, 2 * ROWS) + joined(d, 2 * ROWS))


def sum_mine(meta, *arrays):
    return pl.pallas_call(
        mine_kernel,
        out_shape=[jax.ShapeDtypeStruct((ROWS, B), BF16), jax.ShapeDtypeStruct((PIECE, B), F32)],
        in_specs=[SMEM] + [VMEM] * 5,
        out_specs=[VMEM] * 2,
        compiler_params=params(),
        cost_estimate=small_cost(1 << 17),
        name="sum_mine",
    )(meta, *arrays)


def other_kernel(meta, mine, a, b, c, d, other):
    unit_sum(meta, (a, b, c, d), other, True)


def sum_other(meta, *arrays):
    return pl.pallas_call(
        other_kernel,
        out_shape=jax.ShapeDtypeStruct((ROWS, B), BF16),
        in_specs=[SMEM] + [VMEM] * 5,
        out_specs=VMEM,
        compiler_params=params(),
        cost_estimate=small_cost(1 << 17),
        name="sum_other",
    )(meta, *arrays)


def meet_kernel(scaling, meta, mine, far, w0, w1, w2, w3, own, weight_grad):
    first = meta[PLACE + 1] == 0
    own[...] = jnp.where(first, mine[...], far[...])
    rep = meta[PLACE]
    for back, piece in enumerate((w0, w1, w2, w3)):
        rows = pl.ds(pl.multiple_of(lax.rem(rep + 4 - back, 4) * 32, 32), 32)
        weight_grad[rows, 0:B] = piece[0:32] * scaling
        weight_grad[rows, B : 2 * B] = piece[32:64] * scaling


def meet(meta, scaling, *arrays):
    return pl.pallas_call(
        functools.partial(meet_kernel, scaling),
        out_shape=[jax.ShapeDtypeStruct((ROWS, B), BF16), jax.ShapeDtypeStruct((B, 2 * B), F32)],
        in_specs=[SMEM] + [VMEM] * 6,
        out_specs=[VMEM] * 2,
        compiler_params=params(),
        cost_estimate=small_cost(LONG),
        name="meet_other_z",
    )(meta, *arrays)


def last_kernel(own, crossed, out):
    for s in range(2):
        part = slice(s * B, (s + 1) * B)
        out[part] = (own[part].astype(F32) + crossed[part].astype(F32)).T.astype(BF16)


def last_sum(*arrays):
    return pl.pallas_call(
        last_kernel,
        out_shape=jax.ShapeDtypeStruct((ROWS, B), BF16),
        in_specs=[VMEM] * 2,
        out_specs=VMEM,
        compiler_params=params(),
        cost_estimate=small_cost(1 << 16),
        name="last_sum",
    )(*arrays)


def per_device(features, adjacency, block_list, block_counts, weight, cotangent):
    stored = adjacency[0, 0]
    r = lax.axis_index("row").astype(jnp.int32)
    rep = lax.axis_index("rep").astype(jnp.int32)
    core = r % 2
    nodes = float(features.shape[0] * 256)

    order = [entry for call in FORWARD_GROUPS for part in call for entry in part]
    back_order = [entry for part in BACKWARD_GROUPS for entry in part]
    meta = jnp.concatenate(
        [
            block_list.reshape(-1),
            block_counts.reshape(-1),
            section_order(r, order, -1),
            section_order(r, back_order, 1),
            jnp.stack([rep, core]),
        ]
    )

    near_unit, far_unit = cross(features, True), other_z(features)
    pair = pair_up(core.reshape(1), features, near_unit, far_unit)
    x1, x2, x3 = small_axis(pair, 1), small_axis(pair, 2), small_axis(pair, 3)
    (low,) = place("place_low", [[(0, 0, 2), (1, 0, 2)]], [pair, x1], [meta])
    n1_low, n3_low = large_axis(low, 1), large_axis(low, 3)
    (high,) = place("place_high", [[(0, 0, 2), (1, 0, 2)]], [x2, x3], [low])
    n1_high, n3_high = large_axis(high, 1), large_axis(high, 3)
    (acc,) = forward(meta, stored, 0, [low, high], None, False)
    f1, f3 = large_axis(n1_low, 1), large_axis(n3_high, 3)
    halves = [low, high, n1_low, n1_high, n3_low, n3_high]
    (near,) = place("place_near", [[(n, 0, 4) for n in range(6)]], halves, [acc])
    near_s = sibling(near)
    (acc,) = forward(meta, stored, 8, halves[2:], acc, False)
    (far,) = place("place_far", [[(0, 0, 4), (1, 0, 4)]], [f1, f3], [acc], size=LONG)
    far_s = sibling(far)
    (acc,) = forward(meta, stored, 24, [near_s], acc, False)
    own_part, *pieces = forward(meta, stored, 48, [far, far_s], acc, True)

    pieces = [turn(piece, d + 1) for d, piece in enumerate(pieces)]
    activations, values, m1, m2, m3, w = middle(meta, own_part, pieces, weight, cotangent)
    messages = [turn(m1, 1), turn(m2, 2), turn(m3, 3)]

    bwd = functools.partial(backward, meta, stored, [values] + messages)
    far_b, w4 = bwd(0, (8,), extra=[w] + messages, finish=gather_terms, tails=(SPLIT,), extra_out=[w])
    far_s = sibling(far_b)
    (near_b,) = bwd(8, (16,), extra=[far_b])
    h1, h3, w8, near_b = bwd(
        24, (4, 4), far_s, extra=[w4, far_s, near_b], finish=sibling_terms, extra_out=[w, near_b]
    )
    f1, f3, near_s = large_axis(h1, 1), large_axis(h3, 3), sibling(near_b)
    w8_z = row_permute(w8, lambda y, x, z, c: at(y, x, 1 - z, c))
    (own_b,) = bwd(32, (8,), extra=[h1])
    g1_high, g3_low, own_b = bwd(40, (4, 4), near_s, extra=[own_b], finish=pass_on, extra_out=[own_b])
    r1_high, r3_low = large_axis(g1_high, 1), large_axis(g3_low, 3)
    own_s = sibling(own_b)
    g1_low, g3_high, w16 = bwd(
        48,
        (4, 4),
        near_s,
        add_from=8,
        extra=[f1, f3, w8, w8_z, g1_high],
        finish=spread_terms,
        tails=(SPLIT, SPLIT),
        extra_out=[w8],
        size=LONG,
    )
    r1_low, r3_high, w16_two = large_axis(g1_low, 1), large_axis(g3_high, 3), large_axis(w16, 2)
    (g0,) = bwd(56, (8,), own_s, extra=[r1_high, r3_low, g1_low], finish=add_halves, size=LONG)
    t0, t1, t2, t3, w64 = sum_groups(g0, r1_low, r3_high, w16, w16_two)
    sums = [t0, small_axis(t1, 1), small_axis(t2, 2), small_axis(t3, 3)]
    mine, w = sum_mine(meta, *sums, w64)
    far, pieces = other_z(mine), [w] + [turn(w, d) for d in (1, 2, 3)]
    crossed = cross(sum_other(meta, mine, *sums), False)
    own, weight_grad = meet(meta, nodes ** (-0.5), mine, far, *pieces)
    feature_grad = last_sum(own, crossed)
    return activations, feature_grad, weight_grad


def solution(mesh):
    in_specs = (
        P(("row", "rep"), None),
        P("row", "rep", None, None, None),
        P("row", "rep", None, None, None),
        P("row", "rep", None),
        P(),
        P(("row", "rep"), None),
    )
    out_specs = (P(("row", "rep"), None), P(("row", "rep"), None), P())
    return jax.shard_map(
        per_device, mesh=mesh, in_specs=in_specs, out_specs=out_specs, check_vma=False
    )
```

```python
import functools

import jax
import jax.numpy as jnp
import numpy as np
from jax import lax
from jax.experimental import pallas as pl
from jax.experimental.pallas import tpu as pltpu
from jax.sharding import PartitionSpec as P

B = 128
SLOTS = 4
BROWS = 8
SECTIONS = 64
ROWS = 2 * B
PIECE = 64
SPLIT = 3 * PIECE
COST = B * B * 8
LONG = 1 << 40
F32 = jnp.float32
BF16 = jnp.bfloat16
VMEM = pl.BlockSpec(memory_space=pltpu.VMEM)
SMEM = pl.BlockSpec(memory_space=pltpu.SMEM)

COUNTS = SECTIONS * SLOTS * 3
FORWARD_ORDER = COUNTS + SECTIONS
BACKWARD_ORDER = FORWARD_ORDER + SECTIONS
PLACE = BACKWARD_ORDER + SECTIONS


def group(flip, e, ds=(0, 1, 2, 3)):
    return [(flip, e, d, u) for d in ds for u in range(2)]


FORWARD_GROUPS = [
    [group(0, 0)],
    [group(0, 1), group(0, 3)],
    [group(1, 0), group(1, 1), group(1, 3)],
    [group(0, 2), group(1, 2)],
]
LOW, HIGH = (0, 1), (2, 3)
BACKWARD_GROUPS = [
    group(1, 2),
    group(1, 1, HIGH) + group(1, 3, LOW) + group(1, 1, LOW) + group(1, 3, HIGH),
    group(0, 2),
    group(1, 0),
    group(0, 1, HIGH) + group(0, 3, LOW),
    group(0, 1, LOW) + group(0, 3, HIGH),
    group(0, 0),
]


def section_order(r, entries, sign):
    flip, e, d, u = (np.array(column, np.int32) for column in zip(*entries))
    y, x, z, core = r // 16, (r // 4) % 4, (r // 2) % 2, r % 2
    role = core ^ flip
    dy, dx = jnp.where(role == 0, e, d), jnp.where(role == 0, d, e)
    return ((y + sign * dy) & 3) * 16 + ((x + sign * dx) & 3) * 4 + (z ^ role) * 2 + u


def at(y, x, z, core):
    return (y % 4) * 16 + (x % 4) * 4 + z * 2 + core


def row_permute(array, target):
    pairs = []
    for r in range(64):
        to = target(r // 16, (r // 4) % 4, (r // 2) % 2, r % 2)
        if to is not None:
            pairs.append((r, to))
    return lax.ppermute(array, "row", pairs)


def small_axis(array, d):
    return row_permute(array, lambda y, x, z, c: at(y + d * c, x + d * (1 - c), z, c))


def large_axis(array, e):
    return row_permute(array, lambda y, x, z, c: at(y + e * (1 - c), x + e * c, z, c))


def sibling(array):
    return row_permute(array, lambda y, x, z, c: at(y, x, z, 1 - c))


def cross(array, forwards):
    if forwards:
        return row_permute(array, lambda y, x, z, c: at(y, x, z, 0) if c else at(y, x, 1 - z, 1))
    return row_permute(array, lambda y, x, z, c: at(y, x, 1 - z, 0) if c else at(y, x, z, 1))


def other_z(array):
    return row_permute(array, lambda y, x, z, c: at(y, x, 1 - z, 1) if c else None)


def turn(array, d):
    return lax.ppermute(array, "rep", [(q, (q + d) % 4) for q in range(4)])


def params():
    return pltpu.CompilerParams(vmem_limit_bytes=20 * 1024 * 1024)


def cost(slots):
    return pl.CostEstimate(flops=slots * COST, bytes_accessed=slots * COST, transcendentals=0)


def small_cost(size):
    return pl.CostEstimate(flops=size // 64, bytes_accessed=size // 64, transcendentals=0)


def touch_kernel(meta, stored, out):
    out[...] = stored[0, 0:16, :].astype(F32)


def touch(meta, stored):
    return pl.pallas_call(
        touch_kernel,
        out_shape=jax.ShapeDtypeStruct((16, B), F32),
        in_specs=[SMEM, VMEM],
        out_specs=VMEM,
        compiler_params=params(),
        cost_estimate=small_cost(1 << 10),
        name="touch_blocks",
    )(meta, stored)


def pair_up_kernel(core, own, near, far, out, sem):
    @pl.when(core[0] == 0)
    def _():
        copy = pltpu.make_async_copy(own, out.at[pl.ds(0, ROWS)], sem)
        copy.start()
        out[ROWS : 2 * ROWS] = near[...]
        copy.wait()

    @pl.when(core[0] == 1)
    def _():
        out[0:ROWS] = near[...]
        out[ROWS : 2 * ROWS] = far[...]


def pair_up(core, own, near, far):
    return pl.pallas_call(
        pair_up_kernel,
        out_shape=jax.ShapeDtypeStruct((2 * ROWS, B), BF16),
        in_specs=[SMEM, pl.BlockSpec(memory_space=pl.ANY)] + [VMEM] * 2,
        out_specs=VMEM,
        scratch_shapes=[pltpu.SemaphoreType.DMA],
        compiler_params=params(),
        cost_estimate=small_cost(1 << 16),
        name="pair_up",
    )(core, own, near, far)


def place_kernel(counts, parts, *refs):
    sources, outs = refs[: len(counts)], refs[-len(parts) :]
    for out, pieces in zip(outs, parts):
        row = 0
        for source, start, size in pieces:
            out[row : row + size * ROWS] = sources[source][start * ROWS : (start + size) * ROWS]
            row += size * ROWS


def place(name, parts, sources, after=(), size=1 << 18):
    shapes = [jax.ShapeDtypeStruct((sum(p[2] for p in pieces) * ROWS, B), BF16) for pieces in parts]
    args = [*sources, *after]
    return pl.pallas_call(
        functools.partial(place_kernel, tuple(range(len(sources))), parts),
        out_shape=shapes,
        in_specs=[VMEM] * len(args),
        out_specs=[VMEM] * len(shapes),
        compiler_params=params(),
        cost_estimate=small_cost(size),
        name=name,
    )(*args)


STEP = 4


def forward_kernel(first_section, sizes, first, last, after, *refs):
    meta, stored = refs[:2]
    chunk_refs = refs[2 : 2 + len(sizes)]
    refs = refs[2 + len(sizes) + after :]
    if first:
        out_refs, acc = refs[:-1], refs[-1]
        acc[...] = jnp.zeros_like(acc)
    else:
        out_refs, acc = refs[1:-1], refs[-1]
        acc[0:BROWS] = refs[0][...]
    begin = first_section
    for size, chunk_ref in zip(sizes, chunk_refs):

        def step(g, carry, begin=begin, chunk_ref=chunk_ref):
            products, places = [], []
            for n in range(STEP):
                sid = meta[FORWARD_ORDER + begin + g * STEP + n]
                count = meta[COUNTS + sid]
                for k in range(SLOTS):
                    base = sid * (SLOTS * 3) + 3 * k
                    start = pl.multiple_of((g * STEP + n) * ROWS + meta[base + 1] * B, B)
                    source = chunk_ref[pl.ds(start, B)]
                    products.append(jnp.dot(stored[meta[base + 2]], source, preferred_element_type=F32))
                    places.append(jnp.where(k < count, meta[base], BROWS))
            for product, place in zip(products, places):
                acc[place] += product
            return carry

        lax.fori_loop(0, size // STEP, step, 0)
        begin += size
    if not last:
        out_refs[0][...] = acc[0:BROWS]
        return
    rep = meta[PLACE]
    for d in range(4):
        for b in range(2):
            piece = acc[lax.rem(rep + d, 4) * 2 + b]
            out_refs[d][b * B : (b + 1) * B] = piece.astype(out_refs[d].dtype)


def forward(meta, stored, first_section, chunk_list, start, last, after=()):
    sizes = tuple(chunk.shape[0] // ROWS for chunk in chunk_list)
    first = start is None
    if last:
        out_shape = [jax.ShapeDtypeStruct((2 * B, B), F32)] + [jax.ShapeDtypeStruct((2 * B, B), BF16)] * 3
    else:
        out_shape = [jax.ShapeDtypeStruct((BROWS, B, B), F32)]
    args = [meta, stored, *chunk_list, *after] + ([] if first else [start])
    return pl.pallas_call(
        functools.partial(forward_kernel, first_section, sizes, first, last, len(after)),
        out_shape=out_shape,
        in_specs=[SMEM] + [VMEM] * (len(args) - 1),
        out_specs=[VMEM] * len(out_shape),
        scratch_shapes=[pltpu.VMEM((BROWS + 1, B, B), F32)],
        compiler_params=params(),
        cost_estimate=cost(sum(sizes) * SLOTS),
        name="forward_slots",
    )(*args)


def middle_kernel(meta, own, p1, p2, p3, weight, cot, act, values, m1, m2, m3, w0):
    pooled = (own[...] + p1[...].astype(F32) + p2[...].astype(F32) + p3[...].astype(F32)).astype(BF16)
    hidden = jnp.dot(pooled, weight[...], preferred_element_type=F32)
    squash = jax.nn.sigmoid(hidden)
    act[...] = (hidden * squash).astype(BF16)
    slope = (cot[...].astype(F32) * squash * (1.0 + hidden * (1.0 - squash))).astype(BF16)
    values_t = lax.dot_general(weight[...], slope, (((1,), (1,)), ((), ())), preferred_element_type=F32)
    values_t = values_t.astype(BF16)
    for out in (values, m1, m2, m3):
        out[0:B] = values_t[:, :B]
        out[B:ROWS] = values_t[:, B:]
    term = lax.dot_general(pooled, slope, (((0,), (0,)), ((), ())), preferred_element_type=F32)
    rep = meta[PLACE]
    for q in range(4):
        piece = jnp.concatenate([term[q * 32 : (q + 1) * 32, :B], term[q * 32 : (q + 1) * 32, B:]], axis=0)

        @pl.when(rep == q)
        def _(piece=piece):
            w0[...] = piece

        for d, out in enumerate((m1, m2, m3)):

            @pl.when(lax.rem(rep + d + 1, 4) == q)
            def _(out=out, piece=piece):
                out[ROWS : ROWS + PIECE] = piece.astype(BF16)


def middle(meta, own, pieces, weight, cot):
    return pl.pallas_call(
        middle_kernel,
        out_shape=[jax.ShapeDtypeStruct((2 * B, 2 * B), BF16), jax.ShapeDtypeStruct((ROWS, B), BF16)]
        + [jax.ShapeDtypeStruct((ROWS + PIECE, B), BF16)] * 3
        + [jax.ShapeDtypeStruct((PIECE, B), F32)],
        in_specs=[SMEM] + [VMEM] * 6,
        out_specs=[VMEM] * 6,
        compiler_params=params(),
        cost_estimate=small_cost(1 << 16),
        name="middle_rows",
    )(meta, own, *pieces, weight, cot)


def split(total, out_ref, row):
    rest = total
    for n in range(3):
        part = rest.astype(BF16)
        out_ref[row + n * PIECE : row + (n + 1) * PIECE] = part
        rest = rest - part.astype(F32)


def joined(ref, row):
    parts = [ref[row + n * PIECE : row + (n + 1) * PIECE].astype(F32) for n in range(3)]
    return (parts[2] + parts[1]) + parts[0]


def gather_terms(extra, outs, extra_outs):
    total = extra[0][...]
    for ref in extra[1:]:
        total = total + ref[ROWS : ROWS + PIECE].astype(F32)
    split(total, outs[0], 8 * ROWS)
    extra_outs[0][...] = total


def sibling_terms(extra, outs, extra_outs):
    total = extra[0][...] + joined(extra[1], 8 * ROWS)
    extra_outs[0][...] = total
    extra_outs[1][...] = extra[2][...]


def spread_terms(extra, outs, extra_outs):
    half_1, half_3, own, other = extra[:4]
    total = own[...] + other[...]
    for out, half in zip(outs, (half_1, half_3)):
        part = slice(0, 4 * ROWS)
        out[part] = (out[part].astype(F32) + half[...].astype(F32)).astype(BF16)
        split(total, out, 4 * ROWS)
    extra_outs[0][...] = total


def pass_on(extra, outs, extra_outs):
    extra_outs[0][...] = extra[0][...]


def add_halves(extra, outs, extra_outs):
    for half, start in zip(extra[:2], (4 * ROWS, 0)):
        part = slice(start, start + 4 * ROWS)
        outs[0][part] = (outs[0][part].astype(F32) + half[...].astype(F32)).astype(BF16)


def backward_kernel(first_section, sizes, added, add_from, extras, finish, *refs):
    meta, stored = refs[:2]
    value_refs, refs = refs[2:6], refs[6:]
    if added:
        add_ref, refs = refs[0], refs[1:]
    extra, refs = refs[:extras], refs[extras:]
    out_refs, extra_outs, values = refs[: len(sizes)], refs[len(sizes) : -1], refs[-1]
    rep = meta[PLACE]
    for d in range(4):
        for b in range(2):
            values[lax.rem(rep + 4 - d, 4) * 2 + b] = value_refs[d][b * B : (b + 1) * B]
    values[BROWS] = jnp.zeros((B, B), BF16)

    begin = 0
    for size, out_ref in zip(sizes, out_refs):

        def step(g, carry, begin=begin, out_ref=out_ref):
            for m in range(STEP):
                n = g * STEP + m
                sid = meta[BACKWARD_ORDER + first_section + begin + n]
                count = meta[COUNTS + sid]
                base = sid * (SLOTS * 3)
                rows = []
                for j in range(2):
                    columns = []
                    for k in range(SLOTS):
                        live = (k < count) & (meta[base + 3 * k + 1] == j)
                        columns.append(values[jnp.where(live, meta[base + 3 * k], BROWS)])
                    rows.append(jnp.concatenate(columns, axis=1))
                left = jnp.concatenate(rows, axis=0)
                right = jnp.concatenate([stored[meta[base + 3 * k + 2]] for k in range(SLOTS)], axis=0)
                result = jnp.dot(left, right, preferred_element_type=F32)
                if added:
                    result = result + add_ref[pl.ds(pl.multiple_of((add_from + begin + n) * ROWS, ROWS), ROWS)].astype(F32)
                out_ref[pl.ds(pl.multiple_of(n * ROWS, ROWS), ROWS)] = result.astype(BF16)
            return carry

        lax.fori_loop(0, size // STEP, step, 0)
        begin += size
    if finish is not None:
        finish(extra, out_refs, extra_outs)


def backward(meta, stored, values, first_section, sizes, add=None, add_from=0, extra=(), finish=None, tails=None, extra_out=(), size=0):
    added = add is not None
    args = [meta, stored, *values] + ([add] if added else []) + list(extra)
    tails = tails or (0,) * len(sizes)
    shapes = [jax.ShapeDtypeStruct((size * ROWS + tail, B), BF16) for size, tail in zip(sizes, tails)]
    shapes += [jax.ShapeDtypeStruct(a.shape, a.dtype) for a in extra_out]
    return pl.pallas_call(
        functools.partial(backward_kernel, first_section, sizes, added, add_from, len(extra), finish),
        out_shape=shapes,
        in_specs=[SMEM] + [VMEM] * (len(args) - 1),
        out_specs=[VMEM] * len(shapes),
        scratch_shapes=[pltpu.VMEM((BROWS + 1, B, B), BF16)],
        compiler_params=params(),
        cost_estimate=small_cost(size) if size else cost(sum(sizes) * SLOTS),
        name="backward_slots",
    )(*args)


def sum_kernel(a, low, high, own, two, t0, t1, t2, t3, w):
    row = 4 * ROWS
    total = (own[...] + two[...]) + (joined(low, row) + joined(high, row))
    w[...] = total
    for d, out in enumerate((t0, t1, t2, t3)):
        half_ref = high if d >= 2 else low
        part, half = (slice(2 * ROWS * n, 2 * ROWS * (n + 1)) for n in (d, d % 2))
        out[0 : 2 * ROWS] = (a[part].astype(F32) + half_ref[half].astype(F32)).astype(BF16)
        if d:
            split(total, out, 2 * ROWS)


def sum_groups(*arrays):
    return pl.pallas_call(
        sum_kernel,
        out_shape=[jax.ShapeDtypeStruct((2 * ROWS, B), BF16)]
        + [jax.ShapeDtypeStruct((2 * ROWS + SPLIT, B), BF16)] * 3
        + [jax.ShapeDtypeStruct((PIECE, B), F32)],
        in_specs=[VMEM] * 5,
        out_specs=[VMEM] * 5,
        compiler_params=params(),
        cost_estimate=small_cost(1 << 18),
        name="sum_groups",
    )(*arrays)


def pair_kernel(meta, a, b, c, d, own, mine, other, w):
    core = meta[PLACE + 1]
    for out, unit in ((mine, core), (other, 1 - core)):
        part = pl.ds(pl.multiple_of(unit * ROWS, ROWS), ROWS)
        total = a[part].astype(F32) + b[part].astype(F32) + c[part].astype(F32) + d[part].astype(F32)
        out[...] = total.astype(BF16)
    w[...] = (own[...] + joined(c, 2 * ROWS)) + (joined(b, 2 * ROWS) + joined(d, 2 * ROWS))


def sum_pairs(meta, *arrays):
    return pl.pallas_call(
        pair_kernel,
        out_shape=[jax.ShapeDtypeStruct((ROWS, B), BF16)] * 2 + [jax.ShapeDtypeStruct((PIECE, B), F32)],
        in_specs=[SMEM] + [VMEM] * 5,
        out_specs=[VMEM] * 3,
        compiler_params=params(),
        cost_estimate=small_cost(1 << 17),
        name="sum_pairs",
    )(meta, *arrays)


def last_kernel(scaling, meta, mine, crossed, far, w0, w1, w2, w3, out, weight_grad):
    first = meta[PLACE + 1] == 0
    for s in range(2):
        part = slice(s * B, (s + 1) * B)
        own = jnp.where(first, mine[part].astype(F32), far[part].astype(F32))
        out[part] = (own + crossed[part].astype(F32)).T.astype(BF16)
    rep = meta[PLACE]
    for back, piece in enumerate((w0, w1, w2, w3)):
        rows = pl.ds(pl.multiple_of(lax.rem(rep + 4 - back, 4) * 32, 32), 32)
        weight_grad[rows, 0:B] = piece[0:32] * scaling
        weight_grad[rows, B : 2 * B] = piece[32:64] * scaling


def last_sum(meta, scaling, *arrays):
    return pl.pallas_call(
        functools.partial(last_kernel, scaling),
        out_shape=[jax.ShapeDtypeStruct((ROWS, B), BF16), jax.ShapeDtypeStruct((B, 2 * B), F32)],
        in_specs=[SMEM] + [VMEM] * 7,
        out_specs=[VMEM] * 2,
        compiler_params=params(),
        cost_estimate=small_cost(1 << 16),
        name="last_sum",
    )(meta, *arrays)


def per_device(features, adjacency, block_list, block_counts, weight, cotangent):
    stored = adjacency[0, 0]
    r = lax.axis_index("row").astype(jnp.int32)
    rep = lax.axis_index("rep").astype(jnp.int32)
    core = r % 2
    nodes = float(features.shape[0] * 256)

    order = [entry for call in FORWARD_GROUPS for part in call for entry in part]
    back_order = [entry for part in BACKWARD_GROUPS for entry in part]
    meta = jnp.concatenate(
        [
            block_list.reshape(-1),
            block_counts.reshape(-1),
            section_order(r, order, -1),
            section_order(r, back_order, 1),
            jnp.stack([rep, core]),
        ]
    )

    near_unit, far_unit = cross(features, True), other_z(features)
    pair = pair_up(core.reshape(1), features, near_unit, far_unit)
    x1, x2, x3 = small_axis(pair, 1), small_axis(pair, 2), small_axis(pair, 3)
    touched = touch(meta, stored)
    (low,) = place("place_low", [[(0, 0, 2), (1, 0, 2)]], [pair, x1])
    n1_low, n3_low = large_axis(low, 1), large_axis(low, 3)
    (high,) = place("place_high", [[(0, 0, 2), (1, 0, 2)]], [x2, x3], [touched, low])
    n1_high, n3_high = large_axis(high, 1), large_axis(high, 3)
    (acc,) = forward(meta, stored, 0, [low, high], None, False)
    f1, f3 = large_axis(n1_low, 1), large_axis(n3_high, 3)
    halves = [low, high, n1_low, n1_high, n3_low, n3_high]
    (near,) = place("place_near", [[(n, 0, 4) for n in range(6)]], halves, [acc])
    near_s = sibling(near)
    (acc,) = forward(meta, stored, 8, halves[2:], acc, False)
    (far,) = place("place_far", [[(0, 0, 4), (1, 0, 4)]], [f1, f3], [acc], size=LONG)
    far_s = sibling(far)
    (acc,) = forward(meta, stored, 24, [near_s], acc, False)
    own_part, *pieces = forward(meta, stored, 48, [far, far_s], acc, True)

    pieces = [turn(piece, d + 1) for d, piece in enumerate(pieces)]
    activations, values, m1, m2, m3, w = middle(meta, own_part, pieces, weight, cotangent)
    messages = [turn(m1, 1), turn(m2, 2), turn(m3, 3)]

    bwd = functools.partial(backward, meta, stored, [values] + messages)
    far_b, w4 = bwd(0, (8,), extra=[w] + messages, finish=gather_terms, tails=(SPLIT,), extra_out=[w])
    far_s = sibling(far_b)
    (near_b,) = bwd(8, (16,), extra=[far_b])
    h1, h3, w8, near_b = bwd(
        24, (4, 4), far_s, extra=[w4, far_s, near_b], finish=sibling_terms, extra_out=[w, near_b]
    )
    f1, f3, near_s = large_axis(h1, 1), large_axis(h3, 3), sibling(near_b)
    w8_z = row_permute(w8, lambda y, x, z, c: at(y, x, 1 - z, c))
    (own_b,) = bwd(32, (8,), extra=[h1])
    g1_high, g3_low, own_b = bwd(40, (4, 4), near_s, extra=[own_b], finish=pass_on, extra_out=[own_b])
    r1_high, r3_low = large_axis(g1_high, 1), large_axis(g3_low, 3)
    own_s = sibling(own_b)
    g1_low, g3_high, w16 = bwd(
        48,
        (4, 4),
        near_s,
        add_from=8,
        extra=[f1, f3, w8, w8_z, g1_high],
        finish=spread_terms,
        tails=(SPLIT, SPLIT),
        extra_out=[w8],
        size=LONG,
    )
    r1_low, r3_high, w16_two = large_axis(g1_low, 1), large_axis(g3_high, 3), large_axis(w16, 2)
    (g0,) = bwd(56, (8,), own_s, extra=[r1_high, r3_low, g1_low], finish=add_halves, size=LONG)
    t0, t1, t2, t3, w64 = sum_groups(g0, r1_low, r3_high, w16, w16_two)
    sums = [t0, small_axis(t1, 1), small_axis(t2, 2), small_axis(t3, 3)]
    mine, other, w = sum_pairs(meta, *sums, w64)
    far, crossed = other_z(mine), cross(other, False)
    feature_grad, weight_grad = last_sum(
        meta, nodes ** (-0.5), mine, crossed, far, w, *[turn(w, d) for d in (1, 2, 3)]
    )
    return activations, feature_grad, weight_grad


def solution(mesh):
    in_specs = (
        P(("row", "rep"), None),
        P("row", "rep", None, None, None),
        P("row", "rep", None, None, None),
        P("row", "rep", None),
        P(),
        P(("row", "rep"), None),
    )
    out_specs = (P(("row", "rep"), None), P(("row", "rep"), None), P())
    return jax.shard_map(
        per_device, mesh=mesh, in_specs=in_specs, out_specs=out_specs, check_vma=False
    )
```

```python
import functools

import jax
import jax.numpy as jnp
import numpy as np
from jax import lax
from jax.experimental import pallas as pl
from jax.experimental.pallas import tpu as pltpu
from jax.sharding import PartitionSpec as P

B = 128
SLOTS = 4
BROWS = 8
SECTIONS = 64
ROWS = 2 * B
PIECE = 64
SPLIT = 3 * PIECE
COST = B * B * 8
LONG = 1 << 40
F32 = jnp.float32
BF16 = jnp.bfloat16
VMEM = pl.BlockSpec(memory_space=pltpu.VMEM)
SMEM = pl.BlockSpec(memory_space=pltpu.SMEM)

COUNTS = SECTIONS * SLOTS * 3
FORWARD_ORDER = COUNTS + SECTIONS
BACKWARD_ORDER = FORWARD_ORDER + SECTIONS
PLACE = BACKWARD_ORDER + SECTIONS


def group(flip, e, ds=(0, 1, 2, 3)):
    return [(flip, e, d, u) for d in ds for u in range(2)]


FORWARD_GROUPS = [
    [group(0, 0)],
    [group(0, 1), group(0, 3)],
    [group(1, 0), group(1, 1), group(1, 3)],
    [group(0, 2), group(1, 2)],
]
LOW, HIGH = (0, 1), (2, 3)
BACKWARD_GROUPS = [
    group(1, 2) + group(1, 1, HIGH) + group(1, 3, LOW),
    group(1, 1, LOW) + group(1, 3, HIGH) + group(1, 0),
    group(0, 2) + group(0, 1, HIGH) + group(0, 3, LOW),
    group(0, 1, LOW) + group(0, 3, HIGH) + group(0, 0),
]


def section_order(r, entries, sign):
    flip, e, d, u = (np.array(column, np.int32) for column in zip(*entries))
    y, x, z, core = r // 16, (r // 4) % 4, (r // 2) % 2, r % 2
    role = core ^ flip
    dy, dx = jnp.where(role == 0, e, d), jnp.where(role == 0, d, e)
    return ((y + sign * dy) & 3) * 16 + ((x + sign * dx) & 3) * 4 + (z ^ role) * 2 + u


def at(y, x, z, core):
    return (y % 4) * 16 + (x % 4) * 4 + z * 2 + core


def row_permute(array, target):
    pairs = []
    for r in range(64):
        to = target(r // 16, (r // 4) % 4, (r // 2) % 2, r % 2)
        if to is not None:
            pairs.append((r, to))
    return lax.ppermute(array, "row", pairs)


def small_axis(array, d):
    return row_permute(array, lambda y, x, z, c: at(y + d * c, x + d * (1 - c), z, c))


def large_axis(array, e):
    return row_permute(array, lambda y, x, z, c: at(y + e * (1 - c), x + e * c, z, c))


def sibling(array):
    return row_permute(array, lambda y, x, z, c: at(y, x, z, 1 - c))


def cross(array, forwards):
    if forwards:
        return row_permute(array, lambda y, x, z, c: at(y, x, z, 0) if c else at(y, x, 1 - z, 1))
    return row_permute(array, lambda y, x, z, c: at(y, x, 1 - z, 0) if c else at(y, x, z, 1))


def other_z(array):
    return row_permute(array, lambda y, x, z, c: at(y, x, 1 - z, 1) if c else None)


def turn(array, d):
    return lax.ppermute(array, "rep", [(q, (q + d) % 4) for q in range(4)])


def params():
    return pltpu.CompilerParams(vmem_limit_bytes=20 * 1024 * 1024)


def cost(slots):
    return pl.CostEstimate(flops=slots * COST, bytes_accessed=slots * COST, transcendentals=0)


def small_cost(size):
    return pl.CostEstimate(flops=size // 64, bytes_accessed=size // 64, transcendentals=0)


def touch_kernel(meta, stored, out):
    out[...] = stored[0, 0:16, :].astype(F32)


def touch(meta, stored):
    return pl.pallas_call(
        touch_kernel,
        out_shape=jax.ShapeDtypeStruct((16, B), F32),
        in_specs=[SMEM, VMEM],
        out_specs=VMEM,
        compiler_params=params(),
        cost_estimate=small_cost(1 << 10),
        name="touch_blocks",
    )(meta, stored)


def pair_up_kernel(core, own, near, far, out, sem):
    @pl.when(core[0] == 0)
    def _():
        copy = pltpu.make_async_copy(own, out.at[pl.ds(0, ROWS)], sem)
        copy.start()
        out[ROWS : 2 * ROWS] = near[...]
        copy.wait()

    @pl.when(core[0] == 1)
    def _():
        out[0:ROWS] = near[...]
        out[ROWS : 2 * ROWS] = far[...]


def pair_up(core, own, near, far):
    return pl.pallas_call(
        pair_up_kernel,
        out_shape=jax.ShapeDtypeStruct((2 * ROWS, B), BF16),
        in_specs=[SMEM, pl.BlockSpec(memory_space=pl.ANY)] + [VMEM] * 2,
        out_specs=VMEM,
        scratch_shapes=[pltpu.SemaphoreType.DMA],
        compiler_params=params(),
        cost_estimate=small_cost(1 << 16),
        name="pair_up",
    )(core, own, near, far)


def place_kernel(counts, parts, *refs):
    sources, outs = refs[: len(counts)], refs[-len(parts) :]
    for out, pieces in zip(outs, parts):
        row = 0
        for source, start, size in pieces:
            out[row : row + size * ROWS] = sources[source][start * ROWS : (start + size) * ROWS]
            row += size * ROWS


def place(name, parts, sources, after=(), size=1 << 18):
    shapes = [jax.ShapeDtypeStruct((sum(p[2] for p in pieces) * ROWS, B), BF16) for pieces in parts]
    args = [*sources, *after]
    return pl.pallas_call(
        functools.partial(place_kernel, tuple(range(len(sources))), parts),
        out_shape=shapes,
        in_specs=[VMEM] * len(args),
        out_specs=[VMEM] * len(shapes),
        compiler_params=params(),
        cost_estimate=small_cost(size),
        name=name,
    )(*args)


STEP = 4


def forward_kernel(first_section, sizes, first, last, after, *refs):
    meta, stored = refs[:2]
    chunk_refs = refs[2 : 2 + len(sizes)]
    refs = refs[2 + len(sizes) + after :]
    if first:
        out_refs, acc = refs[:-1], refs[-1]
        acc[...] = jnp.zeros_like(acc)
    else:
        out_refs, acc = refs[1:-1], refs[-1]
        acc[0:BROWS] = refs[0][...]
    begin = first_section
    for size, chunk_ref in zip(sizes, chunk_refs):

        def step(g, carry, begin=begin, chunk_ref=chunk_ref):
            products, places = [], []
            for n in range(STEP):
                sid = meta[FORWARD_ORDER + begin + g * STEP + n]
                count = meta[COUNTS + sid]
                for k in range(SLOTS):
                    base = sid * (SLOTS * 3) + 3 * k
                    start = pl.multiple_of((g * STEP + n) * ROWS + meta[base + 1] * B, B)
                    source = chunk_ref[pl.ds(start, B)]
                    products.append(jnp.dot(stored[meta[base + 2]], source, preferred_element_type=F32))
                    places.append(jnp.where(k < count, meta[base], BROWS))
            for product, place in zip(products, places):
                acc[place] += product
            return carry

        lax.fori_loop(0, size // STEP, step, 0)
        begin += size
    if not last:
        out_refs[0][...] = acc[0:BROWS]
        return
    rep = meta[PLACE]
    for d in range(4):
        for b in range(2):
            piece = acc[lax.rem(rep + d, 4) * 2 + b]
            out_refs[d][b * B : (b + 1) * B] = piece.astype(out_refs[d].dtype)


def forward(meta, stored, first_section, chunk_list, start, last, after=()):
    sizes = tuple(chunk.shape[0] // ROWS for chunk in chunk_list)
    first = start is None
    if last:
        out_shape = [jax.ShapeDtypeStruct((2 * B, B), F32)] + [jax.ShapeDtypeStruct((2 * B, B), BF16)] * 3
    else:
        out_shape = [jax.ShapeDtypeStruct((BROWS, B, B), F32)]
    args = [meta, stored, *chunk_list, *after] + ([] if first else [start])
    return pl.pallas_call(
        functools.partial(forward_kernel, first_section, sizes, first, last, len(after)),
        out_shape=out_shape,
        in_specs=[SMEM] + [VMEM] * (len(args) - 1),
        out_specs=[VMEM] * len(out_shape),
        scratch_shapes=[pltpu.VMEM((BROWS + 1, B, B), F32)],
        compiler_params=params(),
        cost_estimate=cost(sum(sizes) * SLOTS),
        name="forward_slots",
    )(*args)


def middle_kernel(meta, own, p1, p2, p3, weight, cot, act, values, m1, m2, m3, w0):
    pooled = (own[...] + p1[...].astype(F32) + p2[...].astype(F32) + p3[...].astype(F32)).astype(BF16)
    hidden = jnp.dot(pooled, weight[...], preferred_element_type=F32)
    squash = jax.nn.sigmoid(hidden)
    act[...] = (hidden * squash).astype(BF16)
    slope = (cot[...].astype(F32) * squash * (1.0 + hidden * (1.0 - squash))).astype(BF16)
    values_t = lax.dot_general(weight[...], slope, (((1,), (1,)), ((), ())), preferred_element_type=F32)
    values_t = values_t.astype(BF16)
    for out in (values, m1, m2, m3):
        out[0:B] = values_t[:, :B]
        out[B:ROWS] = values_t[:, B:]
    term = lax.dot_general(pooled, slope, (((0,), (0,)), ((), ())), preferred_element_type=F32)
    rep = meta[PLACE]
    for q in range(4):
        piece = jnp.concatenate([term[q * 32 : (q + 1) * 32, :B], term[q * 32 : (q + 1) * 32, B:]], axis=0)

        @pl.when(rep == q)
        def _(piece=piece):
            w0[...] = piece

        for d, out in enumerate((m1, m2, m3)):

            @pl.when(lax.rem(rep + d + 1, 4) == q)
            def _(out=out, piece=piece):
                out[ROWS : ROWS + PIECE] = piece.astype(BF16)


def middle(meta, own, pieces, weight, cot):
    return pl.pallas_call(
        middle_kernel,
        out_shape=[jax.ShapeDtypeStruct((2 * B, 2 * B), BF16), jax.ShapeDtypeStruct((ROWS, B), BF16)]
        + [jax.ShapeDtypeStruct((ROWS + PIECE, B), BF16)] * 3
        + [jax.ShapeDtypeStruct((PIECE, B), F32)],
        in_specs=[SMEM] + [VMEM] * 6,
        out_specs=[VMEM] * 6,
        compiler_params=params(),
        cost_estimate=small_cost(1 << 16),
        name="middle_rows",
    )(meta, own, *pieces, weight, cot)


def split(total, out_ref, row):
    rest = total
    for n in range(3):
        part = rest.astype(BF16)
        out_ref[row + n * PIECE : row + (n + 1) * PIECE] = part
        rest = rest - part.astype(F32)


def joined(ref, row):
    parts = [ref[row + n * PIECE : row + (n + 1) * PIECE].astype(F32) for n in range(3)]
    return (parts[2] + parts[1]) + parts[0]


def gather_terms(extra, outs, extra_outs):
    total = extra[0][...]
    for ref in extra[1:]:
        total = total + ref[ROWS : ROWS + PIECE].astype(F32)
    split(total, outs[0], 16 * ROWS)
    extra_outs[0][...] = total


def sibling_terms(extra, outs, extra_outs):
    extra_outs[0][...] = extra[0][...] + joined(extra[1], 16 * ROWS)


def backward_kernel(first_section, sizes, added, extras, finish, *refs):
    meta, stored = refs[:2]
    value_refs, refs = refs[2:6], refs[6:]
    if added:
        add_ref, refs = refs[0], refs[1:]
    extra, refs = refs[:extras], refs[extras:]
    out_refs, extra_outs, values = refs[: len(sizes)], refs[len(sizes) : -1], refs[-1]
    rep = meta[PLACE]
    for d in range(4):
        for b in range(2):
            values[lax.rem(rep + 4 - d, 4) * 2 + b] = value_refs[d][b * B : (b + 1) * B]
    values[BROWS] = jnp.zeros((B, B), BF16)

    begin = 0
    for size, out_ref in zip(sizes, out_refs):

        def step(g, carry, begin=begin, out_ref=out_ref):
            for m in range(STEP):
                n = g * STEP + m
                sid = meta[BACKWARD_ORDER + first_section + begin + n]
                count = meta[COUNTS + sid]
                base = sid * (SLOTS * 3)
                rows = []
                for j in range(2):
                    columns = []
                    for k in range(SLOTS):
                        live = (k < count) & (meta[base + 3 * k + 1] == j)
                        columns.append(values[jnp.where(live, meta[base + 3 * k], BROWS)])
                    rows.append(jnp.concatenate(columns, axis=1))
                left = jnp.concatenate(rows, axis=0)
                right = jnp.concatenate([stored[meta[base + 3 * k + 2]] for k in range(SLOTS)], axis=0)
                result = jnp.dot(left, right, preferred_element_type=F32)
                if added:
                    result = result + add_ref[pl.ds(pl.multiple_of((begin + n) * ROWS, ROWS), ROWS)].astype(F32)
                out_ref[pl.ds(pl.multiple_of(n * ROWS, ROWS), ROWS)] = result.astype(BF16)
            return carry

        lax.fori_loop(0, size // STEP, step, 0)
        begin += size
    if finish is not None:
        finish(extra, out_refs, extra_outs)


def backward(meta, stored, values, first_section, sizes, add=None, extra=(), finish=None, tails=None, extra_out=(), size=0):
    added = add is not None
    args = [meta, stored, *values] + ([add] if added else []) + list(extra)
    tails = tails or (0,) * len(sizes)
    shapes = [jax.ShapeDtypeStruct((size * ROWS + tail, B), BF16) for size, tail in zip(sizes, tails)]
    shapes += [jax.ShapeDtypeStruct(a.shape, a.dtype) for a in extra_out]
    return pl.pallas_call(
        functools.partial(backward_kernel, first_section, sizes, added, len(extra), finish),
        out_shape=shapes,
        in_specs=[SMEM] + [VMEM] * (len(args) - 1),
        out_specs=[VMEM] * len(shapes),
        scratch_shapes=[pltpu.VMEM((BROWS + 1, B, B), BF16)],
        compiler_params=params(),
        cost_estimate=small_cost(size) if size else cost(sum(sizes) * SLOTS),
        name="backward_slots",
    )(*args)


def late_kernel(a, b, half_1, half_3, own, other, out_1, out_3, w):
    total = own[...] + other[...]
    w[...] = total
    for near, half, out in ((a, half_1, out_1), (b, half_3, out_3)):
        out[0 : 4 * ROWS] = (near[...].astype(F32) + half[...].astype(F32)).astype(BF16)
        split(total, out, 4 * ROWS)


def add_late(*arrays):
    return pl.pallas_call(
        late_kernel,
        out_shape=[jax.ShapeDtypeStruct((4 * ROWS + SPLIT, B), BF16)] * 2 + [jax.ShapeDtypeStruct((PIECE, B), F32)],
        in_specs=[VMEM] * 6,
        out_specs=[VMEM] * 3,
        compiler_params=params(),
        cost_estimate=small_cost(1 << 18),
        name="add_late",
    )(*arrays)


def early_kernel(a, high, low, after, out):
    for half, start in ((low, 0), (high, 4 * ROWS)):
        part = slice(start, start + 4 * ROWS)
        out[part] = (a[part].astype(F32) + half[...].astype(F32)).astype(BF16)


def add_early(*arrays):
    return pl.pallas_call(
        early_kernel,
        out_shape=jax.ShapeDtypeStruct((8 * ROWS, B), BF16),
        in_specs=[VMEM] * 4,
        out_specs=VMEM,
        compiler_params=params(),
        cost_estimate=small_cost(LONG),
        name="add_early",
    )(*arrays)


def sum_kernel(a, low, high, own, two, t0, t1, t2, t3, w):
    row = 4 * ROWS
    total = (own[...] + two[...]) + (joined(low, row) + joined(high, row))
    w[...] = total
    for d, out in enumerate((t0, t1, t2, t3)):
        half_ref = high if d >= 2 else low
        part, half = (slice(2 * ROWS * n, 2 * ROWS * (n + 1)) for n in (d, d % 2))
        out[0 : 2 * ROWS] = (a[part].astype(F32) + half_ref[half].astype(F32)).astype(BF16)
        if d:
            split(total, out, 2 * ROWS)


def sum_groups(*arrays):
    return pl.pallas_call(
        sum_kernel,
        out_shape=[jax.ShapeDtypeStruct((2 * ROWS, B), BF16)]
        + [jax.ShapeDtypeStruct((2 * ROWS + SPLIT, B), BF16)] * 3
        + [jax.ShapeDtypeStruct((PIECE, B), F32)],
        in_specs=[VMEM] * 5,
        out_specs=[VMEM] * 5,
        compiler_params=params(),
        cost_estimate=small_cost(1 << 18),
        name="sum_groups",
    )(*arrays)


def pair_kernel(meta, a, b, c, d, own, mine, other, w):
    core = meta[PLACE + 1]
    for out, unit in ((mine, core), (other, 1 - core)):
        part = pl.ds(pl.multiple_of(unit * ROWS, ROWS), ROWS)
        total = a[part].astype(F32) + b[part].astype(F32) + c[part].astype(F32) + d[part].astype(F32)
        out[...] = total.astype(BF16)
    w[...] = (own[...] + joined(c, 2 * ROWS)) + (joined(b, 2 * ROWS) + joined(d, 2 * ROWS))


def sum_pairs(meta, *arrays):
    return pl.pallas_call(
        pair_kernel,
        out_shape=[jax.ShapeDtypeStruct((ROWS, B), BF16)] * 2 + [jax.ShapeDtypeStruct((PIECE, B), F32)],
        in_specs=[SMEM] + [VMEM] * 5,
        out_specs=[VMEM] * 3,
        compiler_params=params(),
        cost_estimate=small_cost(1 << 17),
        name="sum_pairs",
    )(meta, *arrays)


def last_kernel(scaling, meta, mine, far, crossed, w0, w1, w2, w3, out, weight_grad):
    first = meta[PLACE + 1] == 0
    for s in range(2):
        part = slice(s * B, (s + 1) * B)
        own = jnp.where(first, mine[part].astype(F32), far[part].astype(F32))
        out[part] = (own + crossed[part].astype(F32)).T.astype(BF16)
    rep = meta[PLACE]
    for back, piece in enumerate((w0, w1, w2, w3)):
        rows = pl.ds(pl.multiple_of(lax.rem(rep + 4 - back, 4) * 32, 32), 32)
        weight_grad[rows, 0:B] = piece[0:32] * scaling
        weight_grad[rows, B : 2 * B] = piece[32:64] * scaling


def last_sum(meta, scaling, *arrays):
    return pl.pallas_call(
        functools.partial(last_kernel, scaling),
        out_shape=[jax.ShapeDtypeStruct((ROWS, B), BF16), jax.ShapeDtypeStruct((B, 2 * B), F32)],
        in_specs=[SMEM] + [VMEM] * 7,
        out_specs=[VMEM] * 2,
        compiler_params=params(),
        cost_estimate=small_cost(1 << 16),
        name="last_sum",
    )(meta, *arrays)


def per_device(features, adjacency, block_list, block_counts, weight, cotangent):
    stored = adjacency[0, 0]
    r = lax.axis_index("row").astype(jnp.int32)
    rep = lax.axis_index("rep").astype(jnp.int32)
    core = r % 2
    nodes = float(features.shape[0] * 256)

    order = [entry for call in FORWARD_GROUPS for part in call for entry in part]
    back_order = [entry for part in BACKWARD_GROUPS for entry in part]
    meta = jnp.concatenate(
        [
            block_list.reshape(-1),
            block_counts.reshape(-1),
            section_order(r, order, -1),
            section_order(r, back_order, 1),
            jnp.stack([rep, core]),
        ]
    )

    near_unit, far_unit = cross(features, True), other_z(features)
    pair = pair_up(core.reshape(1), features, near_unit, far_unit)
    x1, x2, x3 = small_axis(pair, 1), small_axis(pair, 2), small_axis(pair, 3)
    touched = touch(meta, stored)
    (low,) = place("place_low", [[(0, 0, 2), (1, 0, 2)]], [pair, x1])
    n1_low, n3_low = large_axis(low, 1), large_axis(low, 3)
    (high,) = place("place_high", [[(0, 0, 2), (1, 0, 2)]], [x2, x3], [touched, low])
    n1_high, n3_high = large_axis(high, 1), large_axis(high, 3)
    (acc,) = forward(meta, stored, 0, [low, high], None, False)
    f1, f3 = large_axis(n1_low, 1), large_axis(n3_high, 3)
    halves = [low, high, n1_low, n1_high, n3_low, n3_high]
    (near,) = place("place_near", [[(n, 0, 4) for n in range(6)]], halves, [acc])
    near_s = sibling(near)
    (acc,) = forward(meta, stored, 8, halves[2:], acc, False)
    (far,) = place("place_far", [[(0, 0, 4), (1, 0, 4)]], [f1, f3], [acc], size=LONG)
    far_s = sibling(far)
    (acc,) = forward(meta, stored, 24, [near_s], acc, False)
    own_part, *pieces = forward(meta, stored, 48, [far, far_s], acc, True)

    pieces = [turn(piece, d + 1) for d, piece in enumerate(pieces)]
    activations, values, m1, m2, m3, w = middle(meta, own_part, pieces, weight, cotangent)
    messages = [turn(m1, 1), turn(m2, 2), turn(m3, 3)]

    bwd = functools.partial(backward, meta, stored, [values] + messages)
    first_b, w4 = bwd(0, (16,), extra=[w] + messages, finish=gather_terms, tails=(SPLIT,), extra_out=[w])
    first_s = sibling(first_b)
    (second_b,) = bwd(16, (16,), extra=[first_b])
    second_s = sibling(second_b)
    h1, h3, g1_high, g3_low, w8 = bwd(
        32, (4, 4, 4, 4), first_s, extra=[w4, first_s, second_b], finish=sibling_terms, extra_out=[w], size=LONG
    )
    f1, f3 = large_axis(h1, 1), large_axis(h3, 3)
    r1_high, r3_low = large_axis(g1_high, 1), large_axis(g3_low, 3)
    w8_z = row_permute(w8, lambda y, x, z, c: at(y, x, 1 - z, c))
    l1_low, l3_high, g0 = bwd(48, (4, 4, 8), second_s, extra=[h1])
    g1_low, g3_high, w16 = add_late(l1_low, l3_high, f1, f3, w8, w8_z)
    r1_low, r3_high, w16_two = large_axis(g1_low, 1), large_axis(g3_high, 3), large_axis(w16, 2)
    g0 = add_early(g0, r1_high, r3_low, g1_low)
    t0, t1, t2, t3, w64 = sum_groups(g0, r1_low, r3_high, w16, w16_two)
    sums = [t0, small_axis(t1, 1), small_axis(t2, 2), small_axis(t3, 3)]
    mine, other, w = sum_pairs(meta, *sums, w64)
    far, crossed = other_z(mine), cross(other, False)
    feature_grad, weight_grad = last_sum(
        meta, nodes ** (-0.5), mine, far, crossed, w, *[turn(w, d) for d in (1, 2, 3)]
    )
    return activations, feature_grad, weight_grad


def solution(mesh):
    in_specs = (
        P(("row", "rep"), None),
        P("row", "rep", None, None, None),
        P("row", "rep", None, None, None),
        P("row", "rep", None),
        P(),
        P(("row", "rep"), None),
    )
    out_specs = (P(("row", "rep"), None), P(("row", "rep"), None), P())
    return jax.shard_map(
        per_device, mesh=mesh, in_specs=in_specs, out_specs=out_specs, check_vma=False
    )
```

```python
import functools

import jax
import jax.numpy as jnp
import numpy as np
from jax import lax
from jax.experimental import pallas as pl
from jax.experimental.pallas import tpu as pltpu
from jax.sharding import PartitionSpec as P

B = 128
SLOTS = 4
BROWS = 8
SECTIONS = 64
ROWS = 2 * B
PIECE = 64
SPLIT = 3 * PIECE
COST = B * B * 8
LONG = 1 << 40
F32 = jnp.float32
BF16 = jnp.bfloat16
VMEM = pl.BlockSpec(memory_space=pltpu.VMEM)
SMEM = pl.BlockSpec(memory_space=pltpu.SMEM)

COUNTS = SECTIONS * SLOTS * 3
FORWARD_ORDER = COUNTS + SECTIONS
BACKWARD_ORDER = FORWARD_ORDER + SECTIONS
PLACE = BACKWARD_ORDER + SECTIONS


def group(flip, e, ds=(0, 1, 2, 3)):
    return [(flip, e, d, u) for d in ds for u in range(2)]


FORWARD_GROUPS = [
    [group(0, 0)],
    [group(0, 1), group(0, 3)],
    [group(1, 0), group(1, 1), group(1, 3)],
    [group(0, 2), group(1, 2)],
]
LOW, HIGH = (0, 1), (2, 3)
BACKWARD_GROUPS = [
    group(1, 2) + group(1, 1, HIGH) + group(1, 3, LOW),
    group(1, 1, LOW) + group(1, 3, HIGH) + group(1, 0),
    group(0, 2) + group(0, 1, HIGH) + group(0, 3, LOW),
    group(0, 1, LOW) + group(0, 3, HIGH) + group(0, 0),
]


def section_order(r, entries, sign):
    flip, e, d, u = (np.array(column, np.int32) for column in zip(*entries))
    y, x, z, core = r // 16, (r // 4) % 4, (r // 2) % 2, r % 2
    role = core ^ flip
    dy, dx = jnp.where(role == 0, e, d), jnp.where(role == 0, d, e)
    return ((y + sign * dy) & 3) * 16 + ((x + sign * dx) & 3) * 4 + (z ^ role) * 2 + u


def at(y, x, z, core):
    return (y % 4) * 16 + (x % 4) * 4 + z * 2 + core


def row_permute(array, target):
    pairs = []
    for r in range(64):
        to = target(r // 16, (r // 4) % 4, (r // 2) % 2, r % 2)
        if to is not None:
            pairs.append((r, to))
    return lax.ppermute(array, "row", pairs)


def small_axis(array, d):
    return row_permute(array, lambda y, x, z, c: at(y + d * c, x + d * (1 - c), z, c))


def large_axis(array, e):
    return row_permute(array, lambda y, x, z, c: at(y + e * (1 - c), x + e * c, z, c))


def sibling(array):
    return row_permute(array, lambda y, x, z, c: at(y, x, z, 1 - c))


def cross(array, forwards):
    if forwards:
        return row_permute(array, lambda y, x, z, c: at(y, x, z, 0) if c else at(y, x, 1 - z, 1))
    return row_permute(array, lambda y, x, z, c: at(y, x, 1 - z, 0) if c else at(y, x, z, 1))


def other_z(array):
    return row_permute(array, lambda y, x, z, c: at(y, x, 1 - z, 1) if c else at(y, x, z, 0))


def turn(array, d):
    return lax.ppermute(array, "rep", [(q, (q + d) % 4) for q in range(4)])


def params():
    return pltpu.CompilerParams(vmem_limit_bytes=20 * 1024 * 1024)


def cost(slots):
    return pl.CostEstimate(flops=slots * COST, bytes_accessed=slots * COST, transcendentals=0)


def small_cost(size):
    return pl.CostEstimate(flops=size // 64, bytes_accessed=size // 64, transcendentals=0)


def touch_kernel(meta, stored, out):
    out[...] = stored[0, 0:16, :].astype(F32)


def touch(meta, stored):
    return pl.pallas_call(
        touch_kernel,
        out_shape=jax.ShapeDtypeStruct((16, B), F32),
        in_specs=[SMEM, VMEM],
        out_specs=VMEM,
        compiler_params=params(),
        cost_estimate=small_cost(1 << 10),
        name="touch_blocks",
    )(meta, stored)


def pair_up_kernel(core, near, far, out):
    first = core[0] == 0
    out[0:ROWS] = jnp.where(first, far[...], near[...])
    out[ROWS : 2 * ROWS] = jnp.where(first, near[...], far[...])


def pair_up(core, near, far):
    return pl.pallas_call(
        pair_up_kernel,
        out_shape=jax.ShapeDtypeStruct((2 * ROWS, B), BF16),
        in_specs=[SMEM] + [VMEM] * 2,
        out_specs=VMEM,
        compiler_params=params(),
        cost_estimate=small_cost(1 << 16),
        name="pair_up",
    )(core, near, far)


def place_kernel(counts, parts, *refs):
    sources, outs = refs[: len(counts)], refs[-len(parts) :]
    for out, pieces in zip(outs, parts):
        row = 0
        for source, start, size in pieces:
            out[row : row + size * ROWS] = sources[source][start * ROWS : (start + size) * ROWS]
            row += size * ROWS


def place(name, parts, sources, after=(), size=1 << 18):
    shapes = [jax.ShapeDtypeStruct((sum(p[2] for p in pieces) * ROWS, B), BF16) for pieces in parts]
    args = [*sources, *after]
    return pl.pallas_call(
        functools.partial(place_kernel, tuple(range(len(sources))), parts),
        out_shape=shapes,
        in_specs=[VMEM] * len(args),
        out_specs=[VMEM] * len(shapes),
        compiler_params=params(),
        cost_estimate=small_cost(size),
        name=name,
    )(*args)


STEP = 4


def forward_kernel(first_section, sizes, first, last, after, *refs):
    meta, stored = refs[:2]
    chunk_refs = refs[2 : 2 + len(sizes)]
    refs = refs[2 + len(sizes) + after :]
    if first:
        out_refs, acc = refs[:-1], refs[-1]
        acc[...] = jnp.zeros_like(acc)
    else:
        out_refs, acc = refs[1:-1], refs[-1]
        acc[0:BROWS] = refs[0][...]
    begin = first_section
    for size, chunk_ref in zip(sizes, chunk_refs):

        def step(g, carry, begin=begin, chunk_ref=chunk_ref):
            products, places = [], []
            for n in range(STEP):
                sid = meta[FORWARD_ORDER + begin + g * STEP + n]
                count = meta[COUNTS + sid]
                for k in range(SLOTS):
                    base = sid * (SLOTS * 3) + 3 * k
                    start = pl.multiple_of((g * STEP + n) * ROWS + meta[base + 1] * B, B)
                    source = chunk_ref[pl.ds(start, B)]
                    products.append(jnp.dot(stored[meta[base + 2]], source, preferred_element_type=F32))
                    places.append(jnp.where(k < count, meta[base], BROWS))
            for product, place in zip(products, places):
                acc[place] += product
            return carry

        lax.fori_loop(0, size // STEP, step, 0)
        begin += size
    if not last:
        out_refs[0][...] = acc[0:BROWS]
        return
    rep = meta[PLACE]
    for d in range(4):
        for b in range(2):
            piece = acc[lax.rem(rep + d, 4) * 2 + b]
            out_refs[d][b * B : (b + 1) * B] = piece.astype(out_refs[d].dtype)


def forward(meta, stored, first_section, chunk_list, start, last, after=()):
    sizes = tuple(chunk.shape[0] // ROWS for chunk in chunk_list)
    first = start is None
    if last:
        out_shape = [jax.ShapeDtypeStruct((2 * B, B), F32)] + [jax.ShapeDtypeStruct((2 * B, B), BF16)] * 3
    else:
        out_shape = [jax.ShapeDtypeStruct((BROWS, B, B), F32)]
    args = [meta, stored, *chunk_list, *after] + ([] if first else [start])
    return pl.pallas_call(
        functools.partial(forward_kernel, first_section, sizes, first, last, len(after)),
        out_shape=out_shape,
        in_specs=[SMEM] + [VMEM] * (len(args) - 1),
        out_specs=[VMEM] * len(out_shape),
        scratch_shapes=[pltpu.VMEM((BROWS + 1, B, B), F32)],
        compiler_params=params(),
        cost_estimate=cost(sum(sizes) * SLOTS),
        name="forward_slots",
    )(*args)


def middle_kernel(meta, own, p1, p2, p3, weight, cot, act, values, m1, m2, m3, w0):
    pooled = (own[...] + p1[...].astype(F32) + p2[...].astype(F32) + p3[...].astype(F32)).astype(BF16)
    hidden = jnp.dot(pooled, weight[...], preferred_element_type=F32)
    squash = jax.nn.sigmoid(hidden)
    act[...] = (hidden * squash).astype(BF16)
    slope = (cot[...].astype(F32) * squash * (1.0 + hidden * (1.0 - squash))).astype(BF16)
    values_t = lax.dot_general(weight[...], slope, (((1,), (1,)), ((), ())), preferred_element_type=F32)
    values_t = values_t.astype(BF16)
    for out in (values, m1, m2, m3):
        out[0:B] = values_t[:, :B]
        out[B:ROWS] = values_t[:, B:]
    term = lax.dot_general(pooled, slope, (((0,), (0,)), ((), ())), preferred_element_type=F32)
    rep = meta[PLACE]
    for q in range(4):
        piece = jnp.concatenate([term[q * 32 : (q + 1) * 32, :B], term[q * 32 : (q + 1) * 32, B:]], axis=0)

        @pl.when(rep == q)
        def _(piece=piece):
            w0[...] = piece

        for d, out in enumerate((m1, m2, m3)):

            @pl.when(lax.rem(rep + d + 1, 4) == q)
            def _(out=out, piece=piece):
                out[ROWS : ROWS + PIECE] = piece.astype(BF16)


def middle(meta, own, pieces, weight, cot):
    return pl.pallas_call(
        middle_kernel,
        out_shape=[jax.ShapeDtypeStruct((2 * B, 2 * B), BF16), jax.ShapeDtypeStruct((ROWS, B), BF16)]
        + [jax.ShapeDtypeStruct((ROWS + PIECE, B), BF16)] * 3
        + [jax.ShapeDtypeStruct((PIECE, B), F32)],
        in_specs=[SMEM] + [VMEM] * 6,
        out_specs=[VMEM] * 6,
        compiler_params=params(),
        cost_estimate=small_cost(1 << 16),
        name="middle_rows",
    )(meta, own, *pieces, weight, cot)


def split(total, out_ref, row):
    rest = total
    for n in range(3):
        part = rest.astype(BF16)
        out_ref[row + n * PIECE : row + (n + 1) * PIECE] = part
        rest = rest - part.astype(F32)


def joined(ref, row):
    parts = [ref[row + n * PIECE : row + (n + 1) * PIECE].astype(F32) for n in range(3)]
    return (parts[2] + parts[1]) + parts[0]


def gather_terms(extra, outs, extra_outs):
    total = extra[0][...]
    for ref in extra[1:]:
        total = total + ref[ROWS : ROWS + PIECE].astype(F32)
    split(total, outs[0], 16 * ROWS)
    extra_outs[0][...] = total


def sibling_terms(extra, outs, extra_outs):
    extra_outs[0][...] = (extra[0][...] + joined(extra[1], 16 * ROWS)).astype(BF16)


def backward_kernel(first_section, sizes, added, extras, finish, *refs):
    meta, stored = refs[:2]
    value_refs, refs = refs[2:6], refs[6:]
    if added:
        add_ref, refs = refs[0], refs[1:]
    extra, refs = refs[:extras], refs[extras:]
    out_refs, extra_outs, values = refs[: len(sizes)], refs[len(sizes) : -1], refs[-1]
    rep = meta[PLACE]
    for d in range(4):
        for b in range(2):
            values[lax.rem(rep + 4 - d, 4) * 2 + b] = value_refs[d][b * B : (b + 1) * B]
    values[BROWS] = jnp.zeros((B, B), BF16)

    begin = 0
    for size, out_ref in zip(sizes, out_refs):

        def step(g, carry, begin=begin, out_ref=out_ref):
            for m in range(STEP):
                n = g * STEP + m
                sid = meta[BACKWARD_ORDER + first_section + begin + n]
                count = meta[COUNTS + sid]
                base = sid * (SLOTS * 3)
                rows = []
                for j in range(2):
                    columns = []
                    for k in range(SLOTS):
                        live = (k < count) & (meta[base + 3 * k + 1] == j)
                        columns.append(values[jnp.where(live, meta[base + 3 * k], BROWS)])
                    rows.append(jnp.concatenate(columns, axis=1))
                left = jnp.concatenate(rows, axis=0)
                right = jnp.concatenate([stored[meta[base + 3 * k + 2]] for k in range(SLOTS)], axis=0)
                result = jnp.dot(left, right, preferred_element_type=F32)
                if added:
                    result = result + add_ref[pl.ds(pl.multiple_of((begin + n) * ROWS, ROWS), ROWS)].astype(F32)
                out_ref[pl.ds(pl.multiple_of(n * ROWS, ROWS), ROWS)] = result.astype(BF16)
            return carry

        lax.fori_loop(0, size // STEP, step, 0)
        begin += size
    if finish is not None:
        finish(extra, out_refs, extra_outs)


def backward(meta, stored, values, first_section, sizes, add=None, extra=(), finish=None, tails=None, extra_out=(), size=0):
    added = add is not None
    args = [meta, stored, *values] + ([add] if added else []) + list(extra)
    tails = tails or (0,) * len(sizes)
    shapes = [jax.ShapeDtypeStruct((size * ROWS + tail, B), BF16) for size, tail in zip(sizes, tails)]
    shapes += [jax.ShapeDtypeStruct(a.shape, a.dtype) for a in extra_out]
    return pl.pallas_call(
        functools.partial(backward_kernel, first_section, sizes, added, len(extra), finish),
        out_shape=shapes,
        in_specs=[SMEM] + [VMEM] * (len(args) - 1),
        out_specs=[VMEM] * len(shapes),
        scratch_shapes=[pltpu.VMEM((BROWS + 1, B, B), BF16)],
        compiler_params=params(),
        cost_estimate=small_cost(size) if size else cost(sum(sizes) * SLOTS),
        name="backward_slots",
    )(*args)


def late_kernel(a, b, half_1, half_3, own, other, out_1, out_3, w):
    total = (own[...].astype(F32) + other[...].astype(F32)).astype(BF16)
    w[...] = total
    for near, half, out in ((a, half_1, out_1), (b, half_3, out_3)):
        out[0 : 4 * ROWS] = (near[...].astype(F32) + half[...].astype(F32)).astype(BF16)
        out[4 * ROWS :] = total


def add_late(*arrays):
    return pl.pallas_call(
        late_kernel,
        out_shape=[jax.ShapeDtypeStruct((4 * ROWS + PIECE, B), BF16)] * 2 + [jax.ShapeDtypeStruct((PIECE, B), BF16)],
        in_specs=[VMEM] * 6,
        out_specs=[VMEM] * 3,
        compiler_params=params(),
        cost_estimate=small_cost(1 << 18),
        name="add_late",
    )(*arrays)


def early_kernel(a, high, low, after, out):
    for half, start in ((low, 0), (high, 4 * ROWS)):
        part = slice(start, start + 4 * ROWS)
        out[part] = (a[part].astype(F32) + half[...].astype(F32)).astype(BF16)


def add_early(*arrays):
    return pl.pallas_call(
        early_kernel,
        out_shape=jax.ShapeDtypeStruct((8 * ROWS, B), BF16),
        in_specs=[VMEM] * 4,
        out_specs=VMEM,
        compiler_params=params(),
        cost_estimate=small_cost(LONG),
        name="add_early",
    )(*arrays)


def sum_kernel(a, low, high, own, two, t0, t1, t2, t3, w):
    tail = slice(4 * ROWS, 4 * ROWS + PIECE)
    total = own[...].astype(F32) + two[...].astype(F32)
    total = total + (low[tail].astype(F32) + high[tail].astype(F32))
    w[...] = total
    for d, out in enumerate((t0, t1, t2, t3)):
        half_ref = high if d >= 2 else low
        part, half = (slice(2 * ROWS * n, 2 * ROWS * (n + 1)) for n in (d, d % 2))
        out[0 : 2 * ROWS] = (a[part].astype(F32) + half_ref[half].astype(F32)).astype(BF16)
        if d:
            split(total, out, 2 * ROWS)


def sum_groups(*arrays):
    return pl.pallas_call(
        sum_kernel,
        out_shape=[jax.ShapeDtypeStruct((2 * ROWS, B), BF16)]
        + [jax.ShapeDtypeStruct((2 * ROWS + SPLIT, B), BF16)] * 3
        + [jax.ShapeDtypeStruct((PIECE, B), F32)],
        in_specs=[VMEM] * 5,
        out_specs=[VMEM] * 5,
        compiler_params=params(),
        cost_estimate=small_cost(1 << 18),
        name="sum_groups",
    )(*arrays)


def pair_kernel(meta, a, b, c, d, own, mine, other, w):
    core = meta[PLACE + 1]
    for out, unit in ((mine, core), (other, 1 - core)):
        part = pl.ds(pl.multiple_of(unit * ROWS, ROWS), ROWS)
        total = a[part].astype(F32) + b[part].astype(F32) + c[part].astype(F32) + d[part].astype(F32)
        out[...] = total.astype(BF16)
    w[...] = (own[...] + joined(c, 2 * ROWS)) + (joined(b, 2 * ROWS) + joined(d, 2 * ROWS))


def sum_pairs(meta, *arrays):
    return pl.pallas_call(
        pair_kernel,
        out_shape=[jax.ShapeDtypeStruct((ROWS, B), BF16)] * 2 + [jax.ShapeDtypeStruct((PIECE, B), F32)],
        in_specs=[SMEM] + [VMEM] * 5,
        out_specs=[VMEM] * 3,
        compiler_params=params(),
        cost_estimate=small_cost(1 << 17),
        name="sum_pairs",
    )(meta, *arrays)


def last_kernel(scaling, meta, far, crossed, w0, w1, w2, w3, out, weight_grad):
    for s in range(2):
        part = slice(s * B, (s + 1) * B)
        out[part] = (far[part].astype(F32) + crossed[part].astype(F32)).T.astype(BF16)
    rep = meta[PLACE]
    for back, piece in enumerate((w0, w1, w2, w3)):
        rows = pl.ds(pl.multiple_of(lax.rem(rep + 4 - back, 4) * 32, 32), 32)
        weight_grad[rows, 0:B] = piece[0:32] * scaling
        weight_grad[rows, B : 2 * B] = piece[32:64] * scaling


def last_sum(meta, scaling, *arrays):
    return pl.pallas_call(
        functools.partial(last_kernel, scaling),
        out_shape=[jax.ShapeDtypeStruct((ROWS, B), BF16), jax.ShapeDtypeStruct((B, 2 * B), F32)],
        in_specs=[SMEM] + [VMEM] * 6,
        out_specs=[VMEM] * 2,
        compiler_params=params(),
        cost_estimate=small_cost(1 << 16),
        name="last_sum",
    )(meta, *arrays)


def per_device(features, adjacency, block_list, block_counts, weight, cotangent):
    stored = adjacency[0, 0]
    r = lax.axis_index("row").astype(jnp.int32)
    rep = lax.axis_index("rep").astype(jnp.int32)
    core = r % 2
    nodes = float(features.shape[0] * 256)

    order = [entry for call in FORWARD_GROUPS for part in call for entry in part]
    back_order = [entry for part in BACKWARD_GROUPS for entry in part]
    meta = jnp.concatenate(
        [
            block_list.reshape(-1),
            block_counts.reshape(-1),
            section_order(r, order, -1),
            section_order(r, back_order, 1),
            jnp.stack([rep, core]),
        ]
    )

    near_unit, far_unit = cross(features, True), other_z(features)
    pair = pair_up(core.reshape(1), near_unit, far_unit)
    x1, x2, x3 = small_axis(pair, 1), small_axis(pair, 2), small_axis(pair, 3)
    touched = touch(meta, stored)
    (low,) = place("place_low", [[(0, 0, 2), (1, 0, 2)]], [pair, x1])
    n1_low, n3_low = large_axis(low, 1), large_axis(low, 3)
    (high,) = place("place_high", [[(0, 0, 2), (1, 0, 2)]], [x2, x3], [touched, low])
    n1_high, n3_high = large_axis(high, 1), large_axis(high, 3)
    (acc,) = forward(meta, stored, 0, [low, high], None, False)
    f1, f3 = large_axis(n1_low, 1), large_axis(n3_high, 3)
    halves = [low, high, n1_low, n1_high, n3_low, n3_high]
    (near,) = place("place_near", [[(n, 0, 4) for n in range(6)]], halves, [acc])
    near_s = sibling(near)
    (acc,) = forward(meta, stored, 8, halves[2:], acc, False)
    (far,) = place("place_far", [[(0, 0, 4), (1, 0, 4)]], [f1, f3], [acc], size=LONG)
    far_s = sibling(far)
    (acc,) = forward(meta, stored, 24, [near_s], acc, False)
    own_part, *pieces = forward(meta, stored, 48, [far, far_s], acc, True)

    pieces = [turn(piece, d + 1) for d, piece in enumerate(pieces)]
    activations, values, m1, m2, m3, w = middle(meta, own_part, pieces, weight, cotangent)
    messages = [turn(m1, 1), turn(m2, 2), turn(m3, 3)]

    bwd = functools.partial(backward, meta, stored, [values] + messages)
    first_b, w4 = bwd(0, (16,), extra=[w] + messages, finish=gather_terms, tails=(SPLIT,), extra_out=[w])
    first_s = sibling(first_b)
    (second_b,) = bwd(16, (16,), extra=[first_b])
    second_s = sibling(second_b)
    h1, h3, g1_high, g3_low, w8 = bwd(
        32, (4, 4, 4, 4), first_s, extra=[w4, first_s, second_b], finish=sibling_terms, extra_out=[messages[0][:PIECE]], size=LONG
    )
    f1, f3 = large_axis(h1, 1), large_axis(h3, 3)
    r1_high, r3_low = large_axis(g1_high, 1), large_axis(g3_low, 3)
    w8_z = row_permute(w8, lambda y, x, z, c: at(y, x, 1 - z, c))
    l1_low, l3_high, g0 = bwd(48, (4, 4, 8), second_s, extra=[h1])
    g1_low, g3_high, w16 = add_late(l1_low, l3_high, f1, f3, w8, w8_z)
    r1_low, r3_high, w16_two = large_axis(g1_low, 1), large_axis(g3_high, 3), large_axis(w16, 2)
    g0 = add_early(g0, r1_high, r3_low, g1_low)
    t0, t1, t2, t3, w64 = sum_groups(g0, r1_low, r3_high, w16, w16_two)
    sums = [t0, small_axis(t1, 1), small_axis(t2, 2), small_axis(t3, 3)]
    mine, other, w = sum_pairs(meta, *sums, w64)
    far, crossed = other_z(mine), cross(other, False)
    feature_grad, weight_grad = last_sum(
        meta, nodes ** (-0.5), far, crossed, w, *[turn(w, d) for d in (1, 2, 3)]
    )
    return activations, feature_grad, weight_grad


def solution(mesh):
    in_specs = (
        P(("row", "rep"), None),
        P("row", "rep", None, None, None),
        P("row", "rep", None, None, None),
        P("row", "rep", None),
        P(),
        P(("row", "rep"), None),
    )
    out_specs = (P(("row", "rep"), None), P(("row", "rep"), None), P())
    return jax.shard_map(
        per_device, mesh=mesh, in_specs=in_specs, out_specs=out_specs, check_vma=False
    )
```

```python
import functools

import jax
import jax.numpy as jnp
import numpy as np
from jax import lax
from jax.experimental import pallas as pl
from jax.experimental.pallas import tpu as pltpu
from jax.sharding import PartitionSpec as P

B = 128
SLOTS = 4
BROWS = 8
SECTIONS = 64
ROWS = 2 * B
PIECE = 64
SPLIT = 3 * PIECE
COST = B * B * 8
LONG = 1 << 40
SECOND = 0
F32 = jnp.float32
BF16 = jnp.bfloat16
VMEM = pl.BlockSpec(memory_space=pltpu.VMEM)
SMEM = pl.BlockSpec(memory_space=pltpu.SMEM)

COUNTS = SECTIONS * SLOTS * 3
FORWARD_ORDER = COUNTS + SECTIONS
BACKWARD_ORDER = FORWARD_ORDER + SECTIONS
PLACE = BACKWARD_ORDER + SECTIONS


def group(flip, e, ds=(0, 1, 2, 3)):
    return [(flip, e, d, u) for d in ds for u in range(2)]


FORWARD_GROUPS = [
    [group(0, 0)],
    [group(0, 1), group(0, 3)],
    [group(1, 0), group(1, 1), group(1, 3)],
    [group(0, 2), group(1, 2)],
]
LOW, HIGH = (0, 1), (2, 3)
BACKWARD_GROUPS = [
    group(1, 2) + group(1, 1, HIGH) + group(1, 3, LOW),
    group(1, 1, LOW) + group(1, 3, HIGH) + group(1, 0),
    group(0, 2) + group(0, 1, HIGH) + group(0, 3, LOW),
    group(0, 1, LOW) + group(0, 3, HIGH) + group(0, 0),
]


def section_order(r, entries, sign):
    flip, e, d, u = (np.array(column, np.int32) for column in zip(*entries))
    y, x, z, core = r // 16, (r // 4) % 4, (r // 2) % 2, r % 2
    role = core ^ flip
    dy, dx = jnp.where(role == 0, e, d), jnp.where(role == 0, d, e)
    return ((y + sign * dy) & 3) * 16 + ((x + sign * dx) & 3) * 4 + (z ^ role) * 2 + u


def at(y, x, z, core):
    return (y % 4) * 16 + (x % 4) * 4 + z * 2 + core


def row_permute(array, target):
    pairs = []
    for r in range(64):
        to = target(r // 16, (r // 4) % 4, (r // 2) % 2, r % 2)
        if to is not None:
            pairs.append((r, to))
    return lax.ppermute(array, "row", pairs)


def small_axis(array, d):
    return row_permute(array, lambda y, x, z, c: at(y + d * c, x + d * (1 - c), z, c))


def large_axis(array, e):
    return row_permute(array, lambda y, x, z, c: at(y + e * (1 - c), x + e * c, z, c))


def sibling(array):
    return row_permute(array, lambda y, x, z, c: at(y, x, z, 1 - c))


def cross(array, forwards):
    if forwards:
        return row_permute(array, lambda y, x, z, c: at(y, x, z, 0) if c else at(y, x, 1 - z, 1))
    return row_permute(array, lambda y, x, z, c: at(y, x, 1 - z, 0) if c else at(y, x, z, 1))


def other_z(array):
    return row_permute(array, lambda y, x, z, c: at(y, x, 1 - z, 1) if c else at(y, x, z, 0))


def turn(array, d):
    return lax.ppermute(array, "rep", [(q, (q + d) % 4) for q in range(4)])


def params():
    return pltpu.CompilerParams(vmem_limit_bytes=20 * 1024 * 1024)


def cost(slots):
    return pl.CostEstimate(flops=slots * COST, bytes_accessed=slots * COST, transcendentals=0)


def small_cost(size):
    return pl.CostEstimate(flops=size // 64, bytes_accessed=size // 64, transcendentals=0)


def touch_kernel(meta, stored, out):
    out[...] = stored[0, 0:16, :].astype(F32)


def touch(meta, stored):
    return pl.pallas_call(
        touch_kernel,
        out_shape=jax.ShapeDtypeStruct((16, B), F32),
        in_specs=[SMEM, VMEM],
        out_specs=VMEM,
        compiler_params=params(),
        cost_estimate=small_cost(1 << 10),
        name="touch_blocks",
    )(meta, stored)


def pair_up_kernel(core, near, far, out):
    first = core[0] == 0
    out[0:ROWS] = jnp.where(first, far[...], near[...])
    out[ROWS : 2 * ROWS] = jnp.where(first, near[...], far[...])


def pair_up(core, near, far):
    return pl.pallas_call(
        pair_up_kernel,
        out_shape=jax.ShapeDtypeStruct((2 * ROWS, B), BF16),
        in_specs=[SMEM] + [VMEM] * 2,
        out_specs=VMEM,
        compiler_params=params(),
        cost_estimate=small_cost(1 << 16),
        name="pair_up",
    )(core, near, far)


def place_kernel(counts, parts, *refs):
    sources, outs = refs[: len(counts)], refs[-len(parts) :]
    for out, pieces in zip(outs, parts):
        row = 0
        for source, start, size in pieces:
            out[row : row + size * ROWS] = sources[source][start * ROWS : (start + size) * ROWS]
            row += size * ROWS


def place(name, parts, sources, after=(), size=1 << 18):
    shapes = [jax.ShapeDtypeStruct((sum(p[2] for p in pieces) * ROWS, B), BF16) for pieces in parts]
    args = [*sources, *after]
    return pl.pallas_call(
        functools.partial(place_kernel, tuple(range(len(sources))), parts),
        out_shape=shapes,
        in_specs=[VMEM] * len(args),
        out_specs=[VMEM] * len(shapes),
        compiler_params=params(),
        cost_estimate=small_cost(size),
        name=name,
    )(*args)


STEP = 4


def forward_kernel(first_section, sizes, first, last, after, *refs):
    meta, stored = refs[:2]
    chunk_refs = refs[2 : 2 + len(sizes)]
    refs = refs[2 + len(sizes) + after :]
    if first:
        out_refs, acc = refs[:-1], refs[-1]
        acc[...] = jnp.zeros_like(acc)
    else:
        out_refs, acc = refs[1:-1], refs[-1]
        acc[0:BROWS] = refs[0][...]
    begin = first_section
    for size, chunk_ref in zip(sizes, chunk_refs):

        def step(g, carry, begin=begin, chunk_ref=chunk_ref):
            products, places = [], []
            for n in range(STEP):
                sid = meta[FORWARD_ORDER + begin + g * STEP + n]
                count = meta[COUNTS + sid]
                for k in range(SLOTS):
                    base = sid * (SLOTS * 3) + 3 * k
                    start = pl.multiple_of((g * STEP + n) * ROWS + meta[base + 1] * B, B)
                    source = chunk_ref[pl.ds(start, B)]
                    products.append(jnp.dot(stored[meta[base + 2]], source, preferred_element_type=F32))
                    places.append(jnp.where(k < count, meta[base], BROWS))
            for product, place in zip(products, places):
                acc[place] += product
            return carry

        lax.fori_loop(0, size // STEP, step, 0)
        begin += size
    if not last:
        out_refs[0][...] = acc[0:BROWS]
        return
    rep = meta[PLACE]
    for d in range(4):
        for b in range(2):
            piece = acc[lax.rem(rep + d, 4) * 2 + b]
            out_refs[d][b * B : (b + 1) * B] = piece.astype(out_refs[d].dtype)


def forward(meta, stored, first_section, chunk_list, start, last, after=()):
    sizes = tuple(chunk.shape[0] // ROWS for chunk in chunk_list)
    first = start is None
    if last:
        out_shape = [jax.ShapeDtypeStruct((2 * B, B), F32)] + [jax.ShapeDtypeStruct((2 * B, B), BF16)] * 3
    else:
        out_shape = [jax.ShapeDtypeStruct((BROWS, B, B), F32)]
    args = [meta, stored, *chunk_list, *after] + ([] if first else [start])
    return pl.pallas_call(
        functools.partial(forward_kernel, first_section, sizes, first, last, len(after)),
        out_shape=out_shape,
        in_specs=[SMEM] + [VMEM] * (len(args) - 1),
        out_specs=[VMEM] * len(out_shape),
        scratch_shapes=[pltpu.VMEM((BROWS + 1, B, B), F32)],
        compiler_params=params(),
        cost_estimate=cost(sum(sizes) * SLOTS),
        name="forward_slots",
    )(*args)


def middle_kernel(meta, own, p1, p2, p3, weight, cot, act, values, m1, m2, m3, w0):
    pooled = (own[...] + p1[...].astype(F32) + p2[...].astype(F32) + p3[...].astype(F32)).astype(BF16)
    hidden = jnp.dot(pooled, weight[...], preferred_element_type=F32)
    squash = jax.nn.sigmoid(hidden)
    act[...] = (hidden * squash).astype(BF16)
    slope = (cot[...].astype(F32) * squash * (1.0 + hidden * (1.0 - squash))).astype(BF16)
    values_t = lax.dot_general(weight[...], slope, (((1,), (1,)), ((), ())), preferred_element_type=F32)
    values_t = values_t.astype(BF16)
    for out in (values, m1, m2, m3):
        out[0:B] = values_t[:, :B]
        out[B:ROWS] = values_t[:, B:]
    term = lax.dot_general(pooled, slope, (((0,), (0,)), ((), ())), preferred_element_type=F32)
    rep = meta[PLACE]
    for q in range(4):
        piece = jnp.concatenate([term[q * 32 : (q + 1) * 32, :B], term[q * 32 : (q + 1) * 32, B:]], axis=0)

        @pl.when(rep == q)
        def _(piece=piece):
            w0[...] = piece

        for d, out in enumerate((m1, m2, m3)):

            @pl.when(lax.rem(rep + d + 1, 4) == q)
            def _(out=out, piece=piece):
                out[ROWS : ROWS + PIECE] = piece.astype(BF16)


def middle(meta, own, pieces, weight, cot):
    return pl.pallas_call(
        middle_kernel,
        out_shape=[jax.ShapeDtypeStruct((2 * B, 2 * B), BF16), jax.ShapeDtypeStruct((ROWS, B), BF16)]
        + [jax.ShapeDtypeStruct((ROWS + PIECE, B), BF16)] * 3
        + [jax.ShapeDtypeStruct((PIECE, B), F32)],
        in_specs=[SMEM] + [VMEM] * 6,
        out_specs=[VMEM] * 6,
        compiler_params=params(),
        cost_estimate=small_cost(1 << 16),
        name="middle_rows",
    )(meta, own, *pieces, weight, cot)


def split(total, out_ref, row):
    rest = total
    for n in range(3):
        part = rest.astype(BF16)
        out_ref[row + n * PIECE : row + (n + 1) * PIECE] = part
        rest = rest - part.astype(F32)


def joined(ref, row):
    parts = [ref[row + n * PIECE : row + (n + 1) * PIECE].astype(F32) for n in range(3)]
    return (parts[2] + parts[1]) + parts[0]


def gather_terms(extra, outs, extra_outs):
    total = extra[0][...]
    for ref in extra[1:]:
        total = total + ref[ROWS : ROWS + PIECE].astype(F32)
    total = total.astype(BF16)
    outs[0][16 * ROWS :] = total
    extra_outs[0][...] = total


def meet_terms(extra, outs, extra_outs):
    own, first, other, cross_other = extra[:4]
    here = own[...].astype(F32) + first[16 * ROWS :].astype(F32)
    there = other[...].astype(F32) + cross_other[...].astype(F32)
    extra_outs[0][...] = (here + there).astype(BF16)


def backward_kernel(first_section, sizes, added, extras, finish, *refs):
    meta, stored = refs[:2]
    value_refs, refs = refs[2:6], refs[6:]
    if added:
        add_ref, refs = refs[0], refs[1:]
    extra, refs = refs[:extras], refs[extras:]
    out_refs, extra_outs, values = refs[: len(sizes)], refs[len(sizes) : -1], refs[-1]
    rep = meta[PLACE]
    for d in range(4):
        for b in range(2):
            values[lax.rem(rep + 4 - d, 4) * 2 + b] = value_refs[d][b * B : (b + 1) * B]
    values[BROWS] = jnp.zeros((B, B), BF16)

    begin = 0
    for size, out_ref in zip(sizes, out_refs):

        def step(g, carry, begin=begin, out_ref=out_ref):
            for m in range(STEP):
                n = g * STEP + m
                sid = meta[BACKWARD_ORDER + first_section + begin + n]
                count = meta[COUNTS + sid]
                base = sid * (SLOTS * 3)
                rows = []
                for j in range(2):
                    columns = []
                    for k in range(SLOTS):
                        live = (k < count) & (meta[base + 3 * k + 1] == j)
                        columns.append(values[jnp.where(live, meta[base + 3 * k], BROWS)])
                    rows.append(jnp.concatenate(columns, axis=1))
                left = jnp.concatenate(rows, axis=0)
                right = jnp.concatenate([stored[meta[base + 3 * k + 2]] for k in range(SLOTS)], axis=0)
                result = jnp.dot(left, right, preferred_element_type=F32)
                if added:
                    result = result + add_ref[pl.ds(pl.multiple_of((begin + n) * ROWS, ROWS), ROWS)].astype(F32)
                out_ref[pl.ds(pl.multiple_of(n * ROWS, ROWS), ROWS)] = result.astype(BF16)
            return carry

        lax.fori_loop(0, size // STEP, step, 0)
        begin += size
    if finish is not None:
        finish(extra, out_refs, extra_outs)


def backward(meta, stored, values, first_section, sizes, add=None, extra=(), finish=None, tails=None, extra_out=(), size=0):
    added = add is not None
    args = [meta, stored, *values] + ([add] if added else []) + list(extra)
    tails = tails or (0,) * len(sizes)
    shapes = [jax.ShapeDtypeStruct((size * ROWS + tail, B), BF16) for size, tail in zip(sizes, tails)]
    shapes += [jax.ShapeDtypeStruct(a.shape, a.dtype) for a in extra_out]
    return pl.pallas_call(
        functools.partial(backward_kernel, first_section, sizes, added, len(extra), finish),
        out_shape=shapes,
        in_specs=[SMEM] + [VMEM] * (len(args) - 1),
        out_specs=[VMEM] * len(shapes),
        scratch_shapes=[pltpu.VMEM((BROWS + 1, B, B), BF16)],
        compiler_params=params(),
        cost_estimate=small_cost(size) if size else cost(sum(sizes) * SLOTS),
        name="backward_slots",
    )(*args)


def late_kernel(a, b, half_1, half_3, w, out_1, out_3):
    for near, half, out in ((a, half_1, out_1), (b, half_3, out_3)):
        out[0 : 4 * ROWS] = (near[...].astype(F32) + half[...].astype(F32)).astype(BF16)
        out[4 * ROWS :] = w[...]


def add_late(*arrays):
    return pl.pallas_call(
        late_kernel,
        out_shape=[jax.ShapeDtypeStruct((4 * ROWS + PIECE, B), BF16)] * 2,
        in_specs=[VMEM] * 5,
        out_specs=[VMEM] * 2,
        compiler_params=params(),
        cost_estimate=small_cost(1 << 18),
        name="add_late",
    )(*arrays)


def early_kernel(a, high, low, after, out):
    for half, start in ((low, 0), (high, 4 * ROWS)):
        part = slice(start, start + 4 * ROWS)
        out[part] = (a[part].astype(F32) + half[...].astype(F32)).astype(BF16)


def add_early(*arrays):
    return pl.pallas_call(
        early_kernel,
        out_shape=jax.ShapeDtypeStruct((8 * ROWS, B), BF16),
        in_specs=[VMEM] * 4,
        out_specs=VMEM,
        compiler_params=params(),
        cost_estimate=small_cost(LONG),
        name="add_early",
    )(*arrays)


def sum_kernel(a, low, high, own, two, t0, t1, t2, t3, w):
    tail = slice(4 * ROWS, 4 * ROWS + PIECE)
    total = own[...].astype(F32) + two[...].astype(F32)
    total = total + (low[tail].astype(F32) + high[tail].astype(F32))
    w[...] = total
    for d, out in enumerate((t0, t1, t2, t3)):
        half_ref = high if d >= 2 else low
        part, half = (slice(2 * ROWS * n, 2 * ROWS * (n + 1)) for n in (d, d % 2))
        out[0 : 2 * ROWS] = (a[part].astype(F32) + half_ref[half].astype(F32)).astype(BF16)
        if d:
            split(total, out, 2 * ROWS)


def sum_groups(*arrays):
    return pl.pallas_call(
        sum_kernel,
        out_shape=[jax.ShapeDtypeStruct((2 * ROWS, B), BF16)]
        + [jax.ShapeDtypeStruct((2 * ROWS + SPLIT, B), BF16)] * 3
        + [jax.ShapeDtypeStruct((PIECE, B), F32)],
        in_specs=[VMEM] * 5,
        out_specs=[VMEM] * 5,
        compiler_params=params(),
        cost_estimate=small_cost(1 << 18),
        name="sum_groups",
    )(*arrays)


def pair_kernel(meta, a, b, c, d, own, mine, other, w):
    core = meta[PLACE + 1]
    for out, unit in ((mine, core), (other, 1 - core)):
        part = pl.ds(pl.multiple_of(unit * ROWS, ROWS), ROWS)
        total = a[part].astype(F32) + b[part].astype(F32) + c[part].astype(F32) + d[part].astype(F32)
        out[...] = total.astype(BF16)
    w[...] = (own[...] + joined(c, 2 * ROWS)) + (joined(b, 2 * ROWS) + joined(d, 2 * ROWS))


def sum_pairs(meta, *arrays):
    return pl.pallas_call(
        pair_kernel,
        out_shape=[jax.ShapeDtypeStruct((ROWS, B), BF16)] * 2 + [jax.ShapeDtypeStruct((PIECE, B), F32)],
        in_specs=[SMEM] + [VMEM] * 5,
        out_specs=[VMEM] * 3,
        compiler_params=params(),
        cost_estimate=small_cost(1 << 17),
        name="sum_pairs",
    )(meta, *arrays)


def last_kernel(scaling, meta, far, crossed, w0, w1, w2, w3, out, weight_grad):
    for s in range(2):
        part = slice(s * B, (s + 1) * B)
        out[part] = (far[part].astype(F32) + crossed[part].astype(F32)).T.astype(BF16)
    rep = meta[PLACE]
    for back, piece in enumerate((w0, w1, w2, w3)):
        rows = pl.ds(pl.multiple_of(lax.rem(rep + 4 - back, 4) * 32, 32), 32)
        weight_grad[rows, 0:B] = piece[0:32] * scaling
        weight_grad[rows, B : 2 * B] = piece[32:64] * scaling


def last_sum(meta, scaling, *arrays):
    return pl.pallas_call(
        functools.partial(last_kernel, scaling),
        out_shape=[jax.ShapeDtypeStruct((ROWS, B), BF16), jax.ShapeDtypeStruct((B, 2 * B), F32)],
        in_specs=[SMEM] + [VMEM] * 6,
        out_specs=[VMEM] * 2,
        compiler_params=params(),
        cost_estimate=small_cost(1 << 16),
        name="last_sum",
    )(meta, *arrays)


def per_device(features, adjacency, block_list, block_counts, weight, cotangent):
    stored = adjacency[0, 0]
    r = lax.axis_index("row").astype(jnp.int32)
    rep = lax.axis_index("rep").astype(jnp.int32)
    core = r % 2
    nodes = float(features.shape[0] * 256)

    order = [entry for call in FORWARD_GROUPS for part in call for entry in part]
    back_order = [entry for part in BACKWARD_GROUPS for entry in part]
    meta = jnp.concatenate(
        [
            block_list.reshape(-1),
            block_counts.reshape(-1),
            section_order(r, order, -1),
            section_order(r, back_order, 1),
            jnp.stack([rep, core]),
        ]
    )

    near_unit, far_unit = cross(features, True), other_z(features)
    pair = pair_up(core.reshape(1), near_unit, far_unit)
    x1, x2, x3 = small_axis(pair, 1), small_axis(pair, 2), small_axis(pair, 3)
    touched = touch(meta, stored)
    (low,) = place("place_low", [[(0, 0, 2), (1, 0, 2)]], [pair, x1])
    n1_low, n3_low = large_axis(low, 1), large_axis(low, 3)
    (high,) = place("place_high", [[(0, 0, 2), (1, 0, 2)]], [x2, x3], [touched, low])
    n1_high, n3_high = large_axis(high, 1), large_axis(high, 3)
    (acc,) = forward(meta, stored, 0, [low, high], None, False)
    f1, f3 = large_axis(n1_low, 1), large_axis(n3_high, 3)
    halves = [low, high, n1_low, n1_high, n3_low, n3_high]
    (near,) = place("place_near", [[(n, 0, 4) for n in range(6)]], halves, [acc])
    near_s = sibling(near)
    (acc,) = forward(meta, stored, 8, halves[2:], acc, False)
    (far,) = place("place_far", [[(0, 0, 4), (1, 0, 4)]], [f1, f3], [acc], size=LONG)
    far_s = sibling(far)
    (acc,) = forward(meta, stored, 24, [near_s], acc, False)
    own_part, *pieces = forward(meta, stored, 48, [far, far_s], acc, True)

    pieces = [turn(piece, d + 1) for d, piece in enumerate(pieces)]
    activations, values, m1, m2, m3, w = middle(meta, own_part, pieces, weight, cotangent)
    messages = [turn(m1, 1), turn(m2, 2), turn(m3, 3)]

    bwd = functools.partial(backward, meta, stored, [values] + messages)
    piece = jnp.zeros((PIECE, B), BF16)
    first_b, w4 = bwd(0, (16,), extra=[w] + messages, finish=gather_terms, tails=(PIECE,), extra_out=[piece])
    first_s = sibling(first_b)
    w4_z = row_permute(w4, lambda y, x, z, c: at(y, x, 1 - z, c))
    w4_cross = row_permute(w4, lambda y, x, z, c: at(y, x, 1 - z, 1 - c))
    (second_b,) = bwd(16, (16,), extra=[first_b])
    second_s = sibling(second_b)
    h1, h3, g1_high, g3_low = bwd(32, (4, 4, 4, 4), first_s, extra=[second_b], size=LONG)
    f1, f3 = large_axis(h1, 1), large_axis(h3, 3)
    r1_high, r3_low = large_axis(g1_high, 1), large_axis(g3_low, 3)
    l1_low, l3_high, g0, w16 = bwd(
        48, (4, 4, 8), second_s, extra=[w4, first_s, w4_z, w4_cross, h1], finish=meet_terms, extra_out=[piece], size=SECOND
    )
    w16_two = large_axis(w16, 2)
    g1_low, g3_high = add_late(l1_low, l3_high, f1, f3, w16)
    r1_low, r3_high = large_axis(g1_low, 1), large_axis(g3_high, 3)
    g0 = add_early(g0, r1_high, r3_low, g1_low)
    t0, t1, t2, t3, w64 = sum_groups(g0, r1_low, r3_high, w16, w16_two)
    sums = [t0, small_axis(t1, 1), small_axis(t2, 2), small_axis(t3, 3)]
    mine, other, w = sum_pairs(meta, *sums, w64)
    far, crossed = other_z(mine), cross(other, False)
    feature_grad, weight_grad = last_sum(
        meta, nodes ** (-0.5), far, crossed, w, *[turn(w, d) for d in (1, 2, 3)]
    )
    return activations, feature_grad, weight_grad


def solution(mesh):
    in_specs = (
        P(("row", "rep"), None),
        P("row", "rep", None, None, None),
        P("row", "rep", None, None, None),
        P("row", "rep", None),
        P(),
        P(("row", "rep"), None),
    )
    out_specs = (P(("row", "rep"), None), P(("row", "rep"), None), P())
    return jax.shard_map(
        per_device, mesh=mesh, in_specs=in_specs, out_specs=out_specs, check_vma=False
    )
```

```python
import functools

import jax
import jax.numpy as jnp
import numpy as np
from jax import lax
from jax.experimental import pallas as pl
from jax.experimental.pallas import tpu as pltpu
from jax.sharding import PartitionSpec as P

B = 128
SLOTS = 4
BROWS = 8
SECTIONS = 64
ROWS = 2 * B
PIECE = 64
SPLIT = 3 * PIECE
COST = B * B * 8
LONG = 1 << 40
F32 = jnp.float32
BF16 = jnp.bfloat16
VMEM = pl.BlockSpec(memory_space=pltpu.VMEM)
SMEM = pl.BlockSpec(memory_space=pltpu.SMEM)

COUNTS = SECTIONS * SLOTS * 3
FORWARD_ORDER = COUNTS + SECTIONS
BACKWARD_ORDER = FORWARD_ORDER + SECTIONS
PLACE = BACKWARD_ORDER + SECTIONS


def group(flip, e, ds=(0, 1, 2, 3)):
    return [(flip, e, d, u) for d in ds for u in range(2)]


FORWARD_GROUPS = [
    [group(0, 0)],
    [group(0, 1), group(0, 3)],
    [group(1, 0), group(1, 1), group(1, 3)],
    [group(0, 2), group(1, 2)],
]
LOW, HIGH = (0, 1), (2, 3)
BACKWARD_GROUPS = [
    group(1, 2, LOW) + group(1, 1, HIGH) + group(1, 2, HIGH) + group(1, 3, LOW),
    group(1, 1, LOW) + group(1, 3, HIGH) + group(1, 0),
    group(0, 2, LOW) + group(0, 1, HIGH) + group(0, 2, HIGH) + group(0, 3, LOW),
    group(0, 1, LOW) + group(0, 3, HIGH) + group(0, 0),
]


def section_order(r, entries, sign):
    flip, e, d, u = (np.array(column, np.int32) for column in zip(*entries))
    y, x, z, core = r // 16, (r // 4) % 4, (r // 2) % 2, r % 2
    role = core ^ flip
    dy, dx = jnp.where(role == 0, e, d), jnp.where(role == 0, d, e)
    return ((y + sign * dy) & 3) * 16 + ((x + sign * dx) & 3) * 4 + (z ^ role) * 2 + u


def at(y, x, z, core):
    return (y % 4) * 16 + (x % 4) * 4 + z * 2 + core


def row_permute(array, target):
    pairs = []
    for r in range(64):
        to = target(r // 16, (r // 4) % 4, (r // 2) % 2, r % 2)
        if to is not None:
            pairs.append((r, to))
    return lax.ppermute(array, "row", pairs)


def small_axis(array, d):
    return row_permute(array, lambda y, x, z, c: at(y + d * c, x + d * (1 - c), z, c))


def large_axis(array, e):
    return row_permute(array, lambda y, x, z, c: at(y + e * (1 - c), x + e * c, z, c))


def sibling(array):
    return row_permute(array, lambda y, x, z, c: at(y, x, z, 1 - c))


def cross(array, forwards):
    if forwards:
        return row_permute(array, lambda y, x, z, c: at(y, x, z, 0) if c else at(y, x, 1 - z, 1))
    return row_permute(array, lambda y, x, z, c: at(y, x, 1 - z, 0) if c else at(y, x, z, 1))


def other_z(array):
    return row_permute(array, lambda y, x, z, c: at(y, x, 1 - z, 1) if c else at(y, x, z, 0))


def turn(array, d):
    return lax.ppermute(array, "rep", [(q, (q + d) % 4) for q in range(4)])


def params():
    return pltpu.CompilerParams(vmem_limit_bytes=20 * 1024 * 1024)


def cost(slots):
    return pl.CostEstimate(flops=slots * COST, bytes_accessed=slots * COST, transcendentals=0)


def small_cost(size):
    return pl.CostEstimate(flops=size // 64, bytes_accessed=size // 64, transcendentals=0)


def touch_kernel(meta, stored, out):
    out[...] = stored[0, 0:16, :].astype(F32)


def touch(meta, stored):
    return pl.pallas_call(
        touch_kernel,
        out_shape=jax.ShapeDtypeStruct((16, B), F32),
        in_specs=[SMEM, VMEM],
        out_specs=VMEM,
        compiler_params=params(),
        cost_estimate=small_cost(1 << 10),
        name="touch_blocks",
    )(meta, stored)


def pair_up_kernel(core, near, far, out):
    first = core[0] == 0
    out[0:ROWS] = jnp.where(first, far[...], near[...])
    out[ROWS : 2 * ROWS] = jnp.where(first, near[...], far[...])


def pair_up(core, near, far):
    return pl.pallas_call(
        pair_up_kernel,
        out_shape=jax.ShapeDtypeStruct((2 * ROWS, B), BF16),
        in_specs=[SMEM] + [VMEM] * 2,
        out_specs=VMEM,
        compiler_params=params(),
        cost_estimate=small_cost(1 << 16),
        name="pair_up",
    )(core, near, far)


def place_kernel(counts, parts, *refs):
    sources, outs = refs[: len(counts)], refs[-len(parts) :]
    for out, pieces in zip(outs, parts):
        row = 0
        for source, start, size in pieces:
            out[row : row + size * ROWS] = sources[source][start * ROWS : (start + size) * ROWS]
            row += size * ROWS


def place(name, parts, sources, after=(), size=1 << 18):
    shapes = [jax.ShapeDtypeStruct((sum(p[2] for p in pieces) * ROWS, B), BF16) for pieces in parts]
    args = [*sources, *after]
    return pl.pallas_call(
        functools.partial(place_kernel, tuple(range(len(sources))), parts),
        out_shape=shapes,
        in_specs=[VMEM] * len(args),
        out_specs=[VMEM] * len(shapes),
        compiler_params=params(),
        cost_estimate=small_cost(size),
        name=name,
    )(*args)


STEP = 4


def forward_kernel(first_section, sizes, first, last, after, *refs):
    meta, stored = refs[:2]
    chunk_refs = refs[2 : 2 + len(sizes)]
    refs = refs[2 + len(sizes) + after :]
    if first:
        out_refs, acc = refs[:-1], refs[-1]
        acc[...] = jnp.zeros_like(acc)
    else:
        out_refs, acc = refs[1:-1], refs[-1]
        acc[0:BROWS] = refs[0][...]
    begin = first_section
    for size, chunk_ref in zip(sizes, chunk_refs):

        def step(g, carry, begin=begin, chunk_ref=chunk_ref):
            products, places = [], []
            for n in range(STEP):
                sid = meta[FORWARD_ORDER + begin + g * STEP + n]
                count = meta[COUNTS + sid]
                for k in range(SLOTS):
                    base = sid * (SLOTS * 3) + 3 * k
                    start = pl.multiple_of((g * STEP + n) * ROWS + meta[base + 1] * B, B)
                    source = chunk_ref[pl.ds(start, B)]
                    products.append(jnp.dot(stored[meta[base + 2]], source, preferred_element_type=F32))
                    places.append(jnp.where(k < count, meta[base], BROWS))
            for product, place in zip(products, places):
                acc[place] += product
            return carry

        lax.fori_loop(0, size // STEP, step, 0)
        begin += size
    if not last:
        out_refs[0][...] = acc[0:BROWS]
        return
    rep = meta[PLACE]
    for d in range(4):
        for b in range(2):
            piece = acc[lax.rem(rep + d, 4) * 2 + b]
            out_refs[d][b * B : (b + 1) * B] = piece.astype(out_refs[d].dtype)


def forward(meta, stored, first_section, chunk_list, start, last, after=()):
    sizes = tuple(chunk.shape[0] // ROWS for chunk in chunk_list)
    first = start is None
    if last:
        out_shape = [jax.ShapeDtypeStruct((2 * B, B), F32)] + [jax.ShapeDtypeStruct((2 * B, B), BF16)] * 3
    else:
        out_shape = [jax.ShapeDtypeStruct((BROWS, B, B), F32)]
    args = [meta, stored, *chunk_list, *after] + ([] if first else [start])
    return pl.pallas_call(
        functools.partial(forward_kernel, first_section, sizes, first, last, len(after)),
        out_shape=out_shape,
        in_specs=[SMEM] + [VMEM] * (len(args) - 1),
        out_specs=[VMEM] * len(out_shape),
        scratch_shapes=[pltpu.VMEM((BROWS + 1, B, B), F32)],
        compiler_params=params(),
        cost_estimate=cost(sum(sizes) * SLOTS),
        name="forward_slots",
    )(*args)


def middle_kernel(meta, own, p1, p2, p3, weight, cot, act, values, m1, m2, m3, w0):
    pooled = (own[...] + p1[...].astype(F32) + p2[...].astype(F32) + p3[...].astype(F32)).astype(BF16)
    hidden = jnp.dot(pooled, weight[...], preferred_element_type=F32)
    squash = jax.nn.sigmoid(hidden)
    act[...] = (hidden * squash).astype(BF16)
    slope = (cot[...].astype(F32) * squash * (1.0 + hidden * (1.0 - squash))).astype(BF16)
    values_t = lax.dot_general(weight[...], slope, (((1,), (1,)), ((), ())), preferred_element_type=F32)
    values_t = values_t.astype(BF16)
    for out in (values, m1, m2, m3):
        out[0:B] = values_t[:, :B]
        out[B:ROWS] = values_t[:, B:]
    term = lax.dot_general(pooled, slope, (((0,), (0,)), ((), ())), preferred_element_type=F32)
    rep = meta[PLACE]
    for q in range(4):
        piece = jnp.concatenate([term[q * 32 : (q + 1) * 32, :B], term[q * 32 : (q + 1) * 32, B:]], axis=0)

        @pl.when(rep == q)
        def _(piece=piece):
            w0[...] = piece

        for d, out in enumerate((m1, m2, m3)):

            @pl.when(lax.rem(rep + d + 1, 4) == q)
            def _(out=out, piece=piece):
                out[ROWS : ROWS + PIECE] = piece.astype(BF16)


def middle(meta, own, pieces, weight, cot):
    return pl.pallas_call(
        middle_kernel,
        out_shape=[jax.ShapeDtypeStruct((2 * B, 2 * B), BF16), jax.ShapeDtypeStruct((ROWS, B), BF16)]
        + [jax.ShapeDtypeStruct((ROWS + PIECE, B), BF16)] * 3
        + [jax.ShapeDtypeStruct((PIECE, B), F32)],
        in_specs=[SMEM] + [VMEM] * 6,
        out_specs=[VMEM] * 6,
        compiler_params=params(),
        cost_estimate=small_cost(1 << 16),
        name="middle_rows",
    )(meta, own, *pieces, weight, cot)


def split(total, out_ref, row):
    rest = total
    for n in range(3):
        part = rest.astype(BF16)
        out_ref[row + n * PIECE : row + (n + 1) * PIECE] = part
        rest = rest - part.astype(F32)


def joined(ref, row):
    parts = [ref[row + n * PIECE : row + (n + 1) * PIECE].astype(F32) for n in range(3)]
    return (parts[2] + parts[1]) + parts[0]


def gather_terms(extra, outs, extra_outs):
    total = extra[0][...]
    for ref in extra[1:]:
        total = total + ref[ROWS : ROWS + PIECE].astype(F32)
    split(total, outs[0], 16 * ROWS)
    extra_outs[0][...] = total


def sibling_terms(extra, outs, extra_outs):
    extra_outs[0][...] = (extra[0][...] + joined(extra[1], 16 * ROWS)).astype(BF16)


def backward_kernel(first_section, sizes, added, extras, finish, *refs):
    meta, stored = refs[:2]
    value_refs, refs = refs[2:6], refs[6:]
    if added:
        add_ref, refs = refs[0], refs[1:]
    extra, refs = refs[:extras], refs[extras:]
    out_refs, extra_outs, values = refs[: len(sizes)], refs[len(sizes) : -1], refs[-1]
    rep = meta[PLACE]
    for d in range(4):
        for b in range(2):
            values[lax.rem(rep + 4 - d, 4) * 2 + b] = value_refs[d][b * B : (b + 1) * B]
    values[BROWS] = jnp.zeros((B, B), BF16)

    begin = 0
    for size, out_ref in zip(sizes, out_refs):

        def step(g, carry, begin=begin, out_ref=out_ref):
            for m in range(STEP):
                n = g * STEP + m
                sid = meta[BACKWARD_ORDER + first_section + begin + n]
                count = meta[COUNTS + sid]
                base = sid * (SLOTS * 3)
                rows = []
                for j in range(2):
                    columns = []
                    for k in range(SLOTS):
                        live = (k < count) & (meta[base + 3 * k + 1] == j)
                        columns.append(values[jnp.where(live, meta[base + 3 * k], BROWS)])
                    rows.append(jnp.concatenate(columns, axis=1))
                left = jnp.concatenate(rows, axis=0)
                right = jnp.concatenate([stored[meta[base + 3 * k + 2]] for k in range(SLOTS)], axis=0)
                result = jnp.dot(left, right, preferred_element_type=F32)
                if added:
                    result = result + add_ref[pl.ds(pl.multiple_of((begin + n) * ROWS, ROWS), ROWS)].astype(F32)
                out_ref[pl.ds(pl.multiple_of(n * ROWS, ROWS), ROWS)] = result.astype(BF16)
            return carry

        lax.fori_loop(0, size // STEP, step, 0)
        begin += size
    if finish is not None:
        finish(extra, out_refs, extra_outs)


def backward(meta, stored, values, first_section, sizes, add=None, extra=(), finish=None, tails=None, extra_out=(), size=0):
    added = add is not None
    args = [meta, stored, *values] + ([add] if added else []) + list(extra)
    tails = tails or (0,) * len(sizes)
    shapes = [jax.ShapeDtypeStruct((size * ROWS + tail, B), BF16) for size, tail in zip(sizes, tails)]
    shapes += [jax.ShapeDtypeStruct(a.shape, a.dtype) for a in extra_out]
    return pl.pallas_call(
        functools.partial(backward_kernel, first_section, sizes, added, len(extra), finish),
        out_shape=shapes,
        in_specs=[SMEM] + [VMEM] * (len(args) - 1),
        out_specs=[VMEM] * len(shapes),
        scratch_shapes=[pltpu.VMEM((BROWS + 1, B, B), BF16)],
        compiler_params=params(),
        cost_estimate=small_cost(size) if size else cost(sum(sizes) * SLOTS),
        name="backward_slots",
    )(*args)


def late_kernel(a, b, half_1, half_3, own, other, out_1, out_3, w):
    total = (own[...].astype(F32) + other[...].astype(F32)).astype(BF16)
    w[...] = total
    for near, half, out in ((a, half_1, out_1), (b, half_3, out_3)):
        out[0 : 4 * ROWS] = (near[...].astype(F32) + half[0 : 4 * ROWS].astype(F32)).astype(BF16)
        out[4 * ROWS :] = total


def add_late(*arrays):
    return pl.pallas_call(
        late_kernel,
        out_shape=[jax.ShapeDtypeStruct((4 * ROWS + PIECE, B), BF16)] * 2 + [jax.ShapeDtypeStruct((PIECE, B), BF16)],
        in_specs=[VMEM] * 6,
        out_specs=[VMEM] * 3,
        compiler_params=params(),
        cost_estimate=small_cost(1 << 18),
        name="add_late",
    )(*arrays)


def sum_kernel(a, early_1, early_3, late_1, late_3, own, two, t0, t1, t2, t3, w):
    tail = slice(4 * ROWS, 4 * ROWS + PIECE)
    total = own[...].astype(F32) + two[...].astype(F32)
    total = total + (late_1[tail].astype(F32) + late_3[tail].astype(F32))
    w[...] = total
    for d, out in enumerate((t0, t1, t2, t3)):
        early, late = (early_1, late_3) if d >= 2 else (early_3, late_1)
        start = 2 * ROWS * (d % 2)
        group_sum = a[2 * ROWS * d : 2 * ROWS * (d + 1)].astype(F32)
        group_sum = group_sum + early[4 * ROWS + start : 6 * ROWS + start].astype(F32)
        group_sum = group_sum + late[start : start + 2 * ROWS].astype(F32)
        out[0 : 2 * ROWS] = group_sum.astype(BF16)
        if d:
            split(total, out, 2 * ROWS)


def sum_groups(*arrays):
    return pl.pallas_call(
        sum_kernel,
        out_shape=[jax.ShapeDtypeStruct((2 * ROWS, B), BF16)]
        + [jax.ShapeDtypeStruct((2 * ROWS + SPLIT, B), BF16)] * 3
        + [jax.ShapeDtypeStruct((PIECE, B), F32)],
        in_specs=[VMEM] * 7,
        out_specs=[VMEM] * 5,
        compiler_params=params(),
        cost_estimate=small_cost(1 << 18),
        name="sum_groups",
    )(*arrays)


def pair_kernel(meta, a, b, c, d, own, mine, other, w):
    core = meta[PLACE + 1]
    for out, unit in ((mine, core), (other, 1 - core)):
        part = pl.ds(pl.multiple_of(unit * ROWS, ROWS), ROWS)
        total = a[part].astype(F32) + b[part].astype(F32) + c[part].astype(F32) + d[part].astype(F32)
        out[...] = total.astype(BF16)
    w[...] = (own[...] + joined(c, 2 * ROWS)) + (joined(b, 2 * ROWS) + joined(d, 2 * ROWS))


def sum_pairs(meta, *arrays):
    return pl.pallas_call(
        pair_kernel,
        out_shape=[jax.ShapeDtypeStruct((ROWS, B), BF16)] * 2 + [jax.ShapeDtypeStruct((PIECE, B), F32)],
        in_specs=[SMEM] + [VMEM] * 5,
        out_specs=[VMEM] * 3,
        compiler_params=params(),
        cost_estimate=small_cost(1 << 17),
        name="sum_pairs",
    )(meta, *arrays)


def last_kernel(scaling, meta, far, crossed, w0, w1, w2, w3, out, weight_grad):
    for s in range(2):
        part = slice(s * B, (s + 1) * B)
        out[part] = (far[part].astype(F32) + crossed[part].astype(F32)).T.astype(BF16)
    rep = meta[PLACE]
    for back, piece in enumerate((w0, w1, w2, w3)):
        rows = pl.ds(pl.multiple_of(lax.rem(rep + 4 - back, 4) * 32, 32), 32)
        weight_grad[rows, 0:B] = piece[0:32] * scaling
        weight_grad[rows, B : 2 * B] = piece[32:64] * scaling


def last_sum(meta, scaling, *arrays):
    return pl.pallas_call(
        functools.partial(last_kernel, scaling),
        out_shape=[jax.ShapeDtypeStruct((ROWS, B), BF16), jax.ShapeDtypeStruct((B, 2 * B), F32)],
        in_specs=[SMEM] + [VMEM] * 6,
        out_specs=[VMEM] * 2,
        compiler_params=params(),
        cost_estimate=small_cost(1 << 16),
        name="last_sum",
    )(meta, *arrays)


def per_device(features, adjacency, block_list, block_counts, weight, cotangent):
    stored = adjacency[0, 0]
    r = lax.axis_index("row").astype(jnp.int32)
    rep = lax.axis_index("rep").astype(jnp.int32)
    core = r % 2
    nodes = float(features.shape[0] * 256)

    order = [entry for call in FORWARD_GROUPS for part in call for entry in part]
    back_order = [entry for part in BACKWARD_GROUPS for entry in part]
    meta = jnp.concatenate(
        [
            block_list.reshape(-1),
            block_counts.reshape(-1),
            section_order(r, order, -1),
            section_order(r, back_order, 1),
            jnp.stack([rep, core]),
        ]
    )

    near_unit, far_unit = cross(features, True), other_z(features)
    pair = pair_up(core.reshape(1), near_unit, far_unit)
    x1, x2, x3 = small_axis(pair, 1), small_axis(pair, 2), small_axis(pair, 3)
    touched = touch(meta, stored)
    (low,) = place("place_low", [[(0, 0, 2), (1, 0, 2)]], [pair, x1])
    n1_low, n3_low = large_axis(low, 1), large_axis(low, 3)
    (high,) = place("place_high", [[(0, 0, 2), (1, 0, 2)]], [x2, x3], [touched, low])
    n1_high, n3_high = large_axis(high, 1), large_axis(high, 3)
    (acc,) = forward(meta, stored, 0, [low, high], None, False)
    f1, f3 = large_axis(n1_low, 1), large_axis(n3_high, 3)
    halves = [low, high, n1_low, n1_high, n3_low, n3_high]
    (near,) = place("place_near", [[(n, 0, 4) for n in range(6)]], halves, [acc])
    near_s = sibling(near)
    (acc,) = forward(meta, stored, 8, halves[2:], acc, False)
    (far,) = place("place_far", [[(0, 0, 4), (1, 0, 4)]], [f1, f3], [acc], size=LONG)
    far_s = sibling(far)
    (acc,) = forward(meta, stored, 24, [near_s], acc, False)
    own_part, *pieces = forward(meta, stored, 48, [far, far_s], acc, True)

    pieces = [turn(piece, d + 1) for d, piece in enumerate(pieces)]
    activations, values, m1, m2, m3, w = middle(meta, own_part, pieces, weight, cotangent)
    messages = [turn(m1, 1), turn(m2, 2), turn(m3, 3)]

    bwd = functools.partial(backward, meta, stored, [values] + messages)
    first_b, w4 = bwd(0, (16,), extra=[w] + messages, finish=gather_terms, tails=(SPLIT,), extra_out=[w])
    first_s = sibling(first_b)
    (second_b,) = bwd(16, (16,), extra=[first_b])
    second_s = sibling(second_b)
    e1, e3, w8 = bwd(
        32,
        (8, 8),
        first_s,
        extra=[w4, first_s, second_b],
        finish=sibling_terms,
        extra_out=[messages[0][:PIECE]],
        size=LONG,
    )
    r1, r3 = large_axis(e1, 1), large_axis(e3, 3)
    w8_z = row_permute(w8, lambda y, x, z, c: at(y, x, 1 - z, c))
    l1, l3, g0 = bwd(48, (4, 4, 8), second_s, extra=[e1])
    l1, l3, w16 = add_late(l1, l3, r1, r3, w8, w8_z)
    l1, l3, w16_two = large_axis(l1, 1), large_axis(l3, 3), large_axis(w16, 2)
    t0, t1, t2, t3, w64 = sum_groups(g0, r1, r3, l1, l3, w16, w16_two)
    sums = [t0, small_axis(t1, 1), small_axis(t2, 2), small_axis(t3, 3)]
    mine, other, w = sum_pairs(meta, *sums, w64)
    far, crossed = other_z(mine), cross(other, False)
    feature_grad, weight_grad = last_sum(
        meta, nodes ** (-0.5), far, crossed, w, *[turn(w, d) for d in (1, 2, 3)]
    )
    return activations, feature_grad, weight_grad


def solution(mesh):
    in_specs = (
        P(("row", "rep"), None),
        P("row", "rep", None, None, None),
        P("row", "rep", None, None, None),
        P("row", "rep", None),
        P(),
        P(("row", "rep"), None),
    )
    out_specs = (P(("row", "rep"), None), P(("row", "rep"), None), P())
    return jax.shard_map(
        per_device, mesh=mesh, in_specs=in_specs, out_specs=out_specs, check_vma=False
    )
```

```python
import functools

import jax
import jax.numpy as jnp
import numpy as np
from jax import lax
from jax.experimental import pallas as pl
from jax.experimental.pallas import tpu as pltpu
from jax.sharding import PartitionSpec as P

B = 128
SLOTS = 4
BROWS = 8
SECTIONS = 64
ROWS = 2 * B
PIECE = 64
SPLIT = 3 * PIECE
COST = B * B * 8
LONG = 1 << 40
F32 = jnp.float32
BF16 = jnp.bfloat16
VMEM = pl.BlockSpec(memory_space=pltpu.VMEM)
SMEM = pl.BlockSpec(memory_space=pltpu.SMEM)

COUNTS = SECTIONS * SLOTS * 3
FORWARD_ORDER = COUNTS + SECTIONS
BACKWARD_ORDER = FORWARD_ORDER + SECTIONS
PLACE = BACKWARD_ORDER + SECTIONS


def group(flip, e, ds=(0, 1, 2, 3)):
    return [(flip, e, d, u) for d in ds for u in range(2)]


FORWARD_GROUPS = [
    [group(0, 0)],
    [group(0, 1), group(0, 3)],
    [group(1, 0), group(1, 1), group(1, 3)],
    [group(0, 2), group(1, 2)],
]
LOW, HIGH = (0, 1), (2, 3)
BACKWARD_GROUPS = [
    group(1, 2, LOW) + group(1, 1, HIGH) + group(1, 2, HIGH) + group(1, 3, LOW),
    group(1, 1, LOW) + group(1, 3, HIGH) + group(1, 0),
    group(0, 2, LOW) + group(0, 1, HIGH) + group(0, 2, HIGH) + group(0, 3, LOW),
    group(0, 1, LOW) + group(0, 3, HIGH) + group(0, 0),
]


def section_order(r, entries, sign):
    flip, e, d, u = (np.array(column, np.int32) for column in zip(*entries))
    y, x, z, core = r // 16, (r // 4) % 4, (r // 2) % 2, r % 2
    role = core ^ flip
    dy, dx = jnp.where(role == 0, e, d), jnp.where(role == 0, d, e)
    return ((y + sign * dy) & 3) * 16 + ((x + sign * dx) & 3) * 4 + (z ^ role) * 2 + u


def at(y, x, z, core):
    return (y % 4) * 16 + (x % 4) * 4 + z * 2 + core


def row_permute(array, target):
    pairs = []
    for r in range(64):
        to = target(r // 16, (r // 4) % 4, (r // 2) % 2, r % 2)
        if to is not None:
            pairs.append((r, to))
    return lax.ppermute(array, "row", pairs)


def small_axis(array, d):
    return row_permute(array, lambda y, x, z, c: at(y + d * c, x + d * (1 - c), z, c))


def large_axis(array, e):
    return row_permute(array, lambda y, x, z, c: at(y + e * (1 - c), x + e * c, z, c))


def sibling(array):
    return row_permute(array, lambda y, x, z, c: at(y, x, z, 1 - c))


def cross(array, forwards):
    if forwards:
        return row_permute(array, lambda y, x, z, c: at(y, x, z, 0) if c else at(y, x, 1 - z, 1))
    return row_permute(array, lambda y, x, z, c: at(y, x, 1 - z, 0) if c else at(y, x, z, 1))


def other_z(array):
    return row_permute(array, lambda y, x, z, c: at(y, x, 1 - z, 1) if c else at(y, x, z, 0))


def turn(array, d):
    return lax.ppermute(array, "rep", [(q, (q + d) % 4) for q in range(4)])


def params():
    return pltpu.CompilerParams(vmem_limit_bytes=20 * 1024 * 1024)


def cost(slots):
    return pl.CostEstimate(flops=slots * COST, bytes_accessed=slots * COST, transcendentals=0)


def small_cost(size):
    return pl.CostEstimate(flops=size // 64, bytes_accessed=size // 64, transcendentals=0)


def touch_kernel(meta, stored, out):
    out[...] = stored[0, 0:16, :].astype(F32)


def touch(meta, stored):
    return pl.pallas_call(
        touch_kernel,
        out_shape=jax.ShapeDtypeStruct((16, B), F32),
        in_specs=[SMEM, VMEM],
        out_specs=VMEM,
        compiler_params=params(),
        cost_estimate=small_cost(1 << 10),
        name="touch_blocks",
    )(meta, stored)


def own_core():
    return lax.rem(lax.axis_index("row"), 2)


def pair_up_kernel(near, far, out):
    first = own_core() == 0
    out[0:ROWS] = jnp.where(first, far[...], near[...])
    out[ROWS : 2 * ROWS] = jnp.where(first, near[...], far[...])


def pair_up(near, far):
    return pl.pallas_call(
        pair_up_kernel,
        out_shape=jax.ShapeDtypeStruct((2 * ROWS, B), BF16),
        in_specs=[VMEM] * 2,
        out_specs=VMEM,
        compiler_params=params(),
        cost_estimate=small_cost(1 << 16),
        name="pair_up",
    )(near, far)


def place_kernel(counts, parts, *refs):
    sources, outs = refs[: len(counts)], refs[-len(parts) :]
    for out, pieces in zip(outs, parts):
        row = 0
        for source, start, size in pieces:
            out[row : row + size * ROWS] = sources[source][start * ROWS : (start + size) * ROWS]
            row += size * ROWS


def place(name, parts, sources, after=(), size=1 << 18):
    shapes = [jax.ShapeDtypeStruct((sum(p[2] for p in pieces) * ROWS, B), BF16) for pieces in parts]
    args = [*sources, *after]
    return pl.pallas_call(
        functools.partial(place_kernel, tuple(range(len(sources))), parts),
        out_shape=shapes,
        in_specs=[VMEM] * len(args),
        out_specs=[VMEM] * len(shapes),
        compiler_params=params(),
        cost_estimate=small_cost(size),
        name=name,
    )(*args)


STEP = 4


def forward_kernel(first_section, sizes, first, last, after, *refs):
    meta, stored = refs[:2]
    chunk_refs = refs[2 : 2 + len(sizes)]
    refs = refs[2 + len(sizes) + after :]
    if first:
        out_refs, acc = refs[:-1], refs[-1]
        acc[...] = jnp.zeros_like(acc)
    else:
        out_refs, acc = refs[1:-1], refs[-1]
        acc[0:BROWS] = refs[0][...]
    begin = first_section
    for size, chunk_ref in zip(sizes, chunk_refs):

        def step(g, carry, begin=begin, chunk_ref=chunk_ref):
            products, places = [], []
            for n in range(STEP):
                sid = meta[FORWARD_ORDER + begin + g * STEP + n]
                count = meta[COUNTS + sid]
                for k in range(SLOTS):
                    base = sid * (SLOTS * 3) + 3 * k
                    start = pl.multiple_of((g * STEP + n) * ROWS + meta[base + 1] * B, B)
                    source = chunk_ref[pl.ds(start, B)]
                    products.append(jnp.dot(stored[meta[base + 2]], source, preferred_element_type=F32))
                    places.append(jnp.where(k < count, meta[base], BROWS))
            for product, place in zip(products, places):
                acc[place] += product
            return carry

        lax.fori_loop(0, size // STEP, step, 0)
        begin += size
    if not last:
        out_refs[0][...] = acc[0:BROWS]
        return
    rep = meta[PLACE]
    for d in range(4):
        for b in range(2):
            piece = acc[lax.rem(rep + d, 4) * 2 + b]
            out_refs[d][b * B : (b + 1) * B] = piece.astype(out_refs[d].dtype)


def forward(meta, stored, first_section, chunk_list, start, last, after=()):
    sizes = tuple(chunk.shape[0] // ROWS for chunk in chunk_list)
    first = start is None
    if last:
        out_shape = [jax.ShapeDtypeStruct((2 * B, B), F32)] + [jax.ShapeDtypeStruct((2 * B, B), BF16)] * 3
    else:
        out_shape = [jax.ShapeDtypeStruct((BROWS, B, B), F32)]
    args = [meta, stored, *chunk_list, *after] + ([] if first else [start])
    return pl.pallas_call(
        functools.partial(forward_kernel, first_section, sizes, first, last, len(after)),
        out_shape=out_shape,
        in_specs=[SMEM] + [VMEM] * (len(args) - 1),
        out_specs=[VMEM] * len(out_shape),
        scratch_shapes=[pltpu.VMEM((BROWS + 1, B, B), F32)],
        compiler_params=params(),
        cost_estimate=cost(sum(sizes) * SLOTS),
        name="forward_slots",
    )(*args)


def middle_kernel(own, p1, p2, p3, weight, cot, act, values, m1, m2, m3, w0):
    pooled = (own[...] + p1[...].astype(F32) + p2[...].astype(F32) + p3[...].astype(F32)).astype(BF16)
    hidden = jnp.dot(pooled, weight[...], preferred_element_type=F32)
    squash = jax.nn.sigmoid(hidden)
    act[...] = (hidden * squash).astype(BF16)
    slope = (cot[...].astype(F32) * squash * (1.0 + hidden * (1.0 - squash))).astype(BF16)
    values_t = lax.dot_general(weight[...], slope, (((1,), (1,)), ((), ())), preferred_element_type=F32)
    values_t = values_t.astype(BF16)
    for out in (values, m1, m2, m3):
        out[0:B] = values_t[:, :B]
        out[B:ROWS] = values_t[:, B:]
    term = lax.dot_general(pooled, slope, (((0,), (0,)), ((), ())), preferred_element_type=F32)
    rep = lax.axis_index("rep")
    for q in range(4):
        piece = jnp.concatenate([term[q * 32 : (q + 1) * 32, :B], term[q * 32 : (q + 1) * 32, B:]], axis=0)

        @pl.when(rep == q)
        def _(piece=piece):
            w0[...] = piece

        for d, out in enumerate((m1, m2, m3)):

            @pl.when(lax.rem(rep + d + 1, 4) == q)
            def _(out=out, piece=piece):
                out[ROWS : ROWS + PIECE] = piece.astype(BF16)


def middle(own, pieces, weight, cot):
    return pl.pallas_call(
        middle_kernel,
        out_shape=[jax.ShapeDtypeStruct((2 * B, 2 * B), BF16), jax.ShapeDtypeStruct((ROWS, B), BF16)]
        + [jax.ShapeDtypeStruct((ROWS + PIECE, B), BF16)] * 3
        + [jax.ShapeDtypeStruct((PIECE, B), F32)],
        in_specs=[VMEM] * 6,
        out_specs=[VMEM] * 6,
        compiler_params=params(),
        cost_estimate=small_cost(1 << 16),
        name="middle_rows",
    )(own, *pieces, weight, cot)


def split(total, out_ref, row):
    rest = total
    for n in range(3):
        part = rest.astype(BF16)
        out_ref[row + n * PIECE : row + (n + 1) * PIECE] = part
        rest = rest - part.astype(F32)


def joined(ref, row):
    parts = [ref[row + n * PIECE : row + (n + 1) * PIECE].astype(F32) for n in range(3)]
    return (parts[2] + parts[1]) + parts[0]


def gather_terms(extra, outs, extra_outs):
    total = extra[0][...]
    for ref in extra[1:]:
        total = total + ref[ROWS : ROWS + PIECE].astype(F32)
    split(total, outs[0], 16 * ROWS)
    extra_outs[0][...] = total


def sibling_terms(extra, outs, extra_outs):
    extra_outs[0][...] = (extra[0][...] + joined(extra[1], 16 * ROWS)).astype(BF16)


def backward_kernel(first_section, sizes, added, extras, finish, *refs):
    meta, stored = refs[:2]
    value_refs, refs = refs[2:6], refs[6:]
    if added:
        add_ref, refs = refs[0], refs[1:]
    extra, refs = refs[:extras], refs[extras:]
    out_refs, extra_outs, values = refs[: len(sizes)], refs[len(sizes) : -1], refs[-1]
    rep = meta[PLACE]
    for d in range(4):
        for b in range(2):
            values[lax.rem(rep + 4 - d, 4) * 2 + b] = value_refs[d][b * B : (b + 1) * B]
    values[BROWS] = jnp.zeros((B, B), BF16)

    begin = 0
    for size, out_ref in zip(sizes, out_refs):

        def step(g, carry, begin=begin, out_ref=out_ref):
            for m in range(STEP):
                n = g * STEP + m
                sid = meta[BACKWARD_ORDER + first_section + begin + n]
                count = meta[COUNTS + sid]
                base = sid * (SLOTS * 3)
                rows = []
                for j in range(2):
                    columns = []
                    for k in range(SLOTS):
                        live = (k < count) & (meta[base + 3 * k + 1] == j)
                        columns.append(values[jnp.where(live, meta[base + 3 * k], BROWS)])
                    rows.append(jnp.concatenate(columns, axis=1))
                left = jnp.concatenate(rows, axis=0)
                right = jnp.concatenate([stored[meta[base + 3 * k + 2]] for k in range(SLOTS)], axis=0)
                result = jnp.dot(left, right, preferred_element_type=F32)
                if added:
                    result = result + add_ref[pl.ds(pl.multiple_of((begin + n) * ROWS, ROWS), ROWS)].astype(F32)
                out_ref[pl.ds(pl.multiple_of(n * ROWS, ROWS), ROWS)] = result.astype(BF16)
            return carry

        lax.fori_loop(0, size // STEP, step, 0)
        begin += size
    if finish is not None:
        finish(extra, out_refs, extra_outs)


def backward(meta, stored, values, first_section, sizes, add=None, extra=(), finish=None, tails=None, extra_out=(), size=0):
    added = add is not None
    args = [meta, stored, *values] + ([add] if added else []) + list(extra)
    tails = tails or (0,) * len(sizes)
    shapes = [jax.ShapeDtypeStruct((size * ROWS + tail, B), BF16) for size, tail in zip(sizes, tails)]
    shapes += [jax.ShapeDtypeStruct(a.shape, a.dtype) for a in extra_out]
    return pl.pallas_call(
        functools.partial(backward_kernel, first_section, sizes, added, len(extra), finish),
        out_shape=shapes,
        in_specs=[SMEM] + [VMEM] * (len(args) - 1),
        out_specs=[VMEM] * len(shapes),
        scratch_shapes=[pltpu.VMEM((BROWS + 1, B, B), BF16)],
        compiler_params=params(),
        cost_estimate=small_cost(size) if size else cost(sum(sizes) * SLOTS),
        name="backward_slots",
    )(*args)


def late_kernel(a, b, half_1, half_3, own, other, out_1, out_3, w):
    total = (own[...].astype(F32) + other[...].astype(F32)).astype(BF16)
    w[...] = total
    for near, half, out in ((a, half_1, out_1), (b, half_3, out_3)):
        out[0 : 4 * ROWS] = (near[...].astype(F32) + half[0 : 4 * ROWS].astype(F32)).astype(BF16)
        out[4 * ROWS :] = total


def add_late(*arrays):
    return pl.pallas_call(
        late_kernel,
        out_shape=[jax.ShapeDtypeStruct((4 * ROWS + PIECE, B), BF16)] * 2 + [jax.ShapeDtypeStruct((PIECE, B), BF16)],
        in_specs=[VMEM] * 6,
        out_specs=[VMEM] * 3,
        compiler_params=params(),
        cost_estimate=small_cost(1 << 18),
        name="add_late",
    )(*arrays)


def sum_kernel(a, early_1, early_3, late_1, late_3, own, two, t0, t1, t2, t3, w):
    tail = slice(4 * ROWS, 4 * ROWS + PIECE)
    total = own[...].astype(F32) + two[...].astype(F32)
    total = total + (late_1[tail].astype(F32) + late_3[tail].astype(F32))
    w[...] = total
    for d, out in enumerate((t0, t1, t2, t3)):
        early, late = (early_1, late_3) if d >= 2 else (early_3, late_1)
        start = 2 * ROWS * (d % 2)
        group_sum = a[2 * ROWS * d : 2 * ROWS * (d + 1)].astype(F32)
        group_sum = group_sum + early[4 * ROWS + start : 6 * ROWS + start].astype(F32)
        group_sum = group_sum + late[start : start + 2 * ROWS].astype(F32)
        out[0 : 2 * ROWS] = group_sum.astype(BF16)
        if d:
            split(total, out, 2 * ROWS)


def sum_groups(*arrays):
    return pl.pallas_call(
        sum_kernel,
        out_shape=[jax.ShapeDtypeStruct((2 * ROWS, B), BF16)]
        + [jax.ShapeDtypeStruct((2 * ROWS + SPLIT, B), BF16)] * 3
        + [jax.ShapeDtypeStruct((PIECE, B), F32)],
        in_specs=[VMEM] * 7,
        out_specs=[VMEM] * 5,
        compiler_params=params(),
        cost_estimate=small_cost(1 << 18),
        name="sum_groups",
    )(*arrays)


def pair_kernel(a, b, c, d, own, mine, other, w):
    core = own_core()
    for out, unit in ((mine, core), (other, 1 - core)):
        part = pl.ds(pl.multiple_of(unit * ROWS, ROWS), ROWS)
        total = a[part].astype(F32) + b[part].astype(F32) + c[part].astype(F32) + d[part].astype(F32)
        out[...] = total.astype(BF16)
    w[...] = (own[...] + joined(c, 2 * ROWS)) + (joined(b, 2 * ROWS) + joined(d, 2 * ROWS))


def sum_pairs(*arrays):
    return pl.pallas_call(
        pair_kernel,
        out_shape=[jax.ShapeDtypeStruct((ROWS, B), BF16)] * 2 + [jax.ShapeDtypeStruct((PIECE, B), F32)],
        in_specs=[VMEM] * 5,
        out_specs=[VMEM] * 3,
        compiler_params=params(),
        cost_estimate=small_cost(1 << 17),
        name="sum_pairs",
    )(*arrays)


def last_kernel(scaling, far, crossed, w0, w1, w2, w3, out, weight_grad):
    for s in range(2):
        part = slice(s * B, (s + 1) * B)
        out[part] = (far[part].astype(F32) + crossed[part].astype(F32)).T.astype(BF16)
    rep = lax.axis_index("rep")
    for back, piece in enumerate((w0, w1, w2, w3)):
        rows = pl.ds(pl.multiple_of(lax.rem(rep + 4 - back, 4) * 32, 32), 32)
        weight_grad[rows, 0:B] = piece[0:32] * scaling
        weight_grad[rows, B : 2 * B] = piece[32:64] * scaling


def last_sum(scaling, *arrays):
    return pl.pallas_call(
        functools.partial(last_kernel, scaling),
        out_shape=[jax.ShapeDtypeStruct((ROWS, B), BF16), jax.ShapeDtypeStruct((B, 2 * B), F32)],
        in_specs=[VMEM] * 6,
        out_specs=[VMEM] * 2,
        compiler_params=params(),
        cost_estimate=small_cost(1 << 16),
        name="last_sum",
    )(*arrays)


def per_device(features, adjacency, block_list, block_counts, weight, cotangent):
    stored = adjacency[0, 0]
    r = lax.axis_index("row").astype(jnp.int32)
    rep = lax.axis_index("rep").astype(jnp.int32)
    nodes = float(features.shape[0] * 256)

    order = [entry for call in FORWARD_GROUPS for part in call for entry in part]
    back_order = [entry for part in BACKWARD_GROUPS for entry in part]
    meta = jnp.concatenate(
        [
            block_list.reshape(-1),
            block_counts.reshape(-1),
            section_order(r, order, -1),
            section_order(r, back_order, 1),
            rep.reshape(1),
        ]
    )

    near_unit, far_unit = cross(features, True), other_z(features)
    pair = pair_up(near_unit, far_unit)
    x1, x2, x3 = small_axis(pair, 1), small_axis(pair, 2), small_axis(pair, 3)
    touched = touch(meta, stored)
    (low,) = place("place_low", [[(0, 0, 2), (1, 0, 2)]], [pair, x1])
    n1_low, n3_low = large_axis(low, 1), large_axis(low, 3)
    (high,) = place("place_high", [[(0, 0, 2), (1, 0, 2)]], [x2, x3], [touched, low])
    n1_high, n3_high = large_axis(high, 1), large_axis(high, 3)
    (acc,) = forward(meta, stored, 0, [low, high], None, False)
    f1, f3 = large_axis(n1_low, 1), large_axis(n3_high, 3)
    halves = [low, high, n1_low, n1_high, n3_low, n3_high]
    (near,) = place("place_near", [[(n, 0, 4) for n in range(6)]], halves, [acc])
    near_s = sibling(near)
    (acc,) = forward(meta, stored, 8, halves[2:], acc, False)
    (far,) = place("place_far", [[(0, 0, 4), (1, 0, 4)]], [f1, f3], [acc], size=LONG)
    far_s = sibling(far)
    (acc,) = forward(meta, stored, 24, [near_s], acc, False)
    own_part, *pieces = forward(meta, stored, 48, [far, far_s], acc, True)

    pieces = [turn(piece, d + 1) for d, piece in enumerate(pieces)]
    activations, values, m1, m2, m3, w = middle(own_part, pieces, weight, cotangent)
    messages = [turn(m1, 1), turn(m2, 2), turn(m3, 3)]

    bwd = functools.partial(backward, meta, stored, [values] + messages)
    first_b, w4 = bwd(0, (16,), extra=[w] + messages, finish=gather_terms, tails=(SPLIT,), extra_out=[w])
    first_s = sibling(first_b)
    (second_b,) = bwd(16, (16,), extra=[first_b])
    second_s = sibling(second_b)
    e1, e3, w8 = bwd(
        32,
        (8, 8),
        first_s,
        extra=[w4, first_s, second_b],
        finish=sibling_terms,
        extra_out=[messages[0][:PIECE]],
        size=LONG,
    )
    r1, r3 = large_axis(e1, 1), large_axis(e3, 3)
    w8_z = row_permute(w8, lambda y, x, z, c: at(y, x, 1 - z, c))
    l1, l3, g0 = bwd(48, (4, 4, 8), second_s, extra=[e1])
    l1, l3, w16 = add_late(l1, l3, r1, r3, w8, w8_z)
    l1, l3, w16_two = large_axis(l1, 1), large_axis(l3, 3), large_axis(w16, 2)
    t0, t1, t2, t3, w64 = sum_groups(g0, r1, r3, l1, l3, w16, w16_two)
    sums = [t0, small_axis(t1, 1), small_axis(t2, 2), small_axis(t3, 3)]
    mine, other, w = sum_pairs(*sums, w64)
    far, crossed = other_z(mine), cross(other, False)
    feature_grad, weight_grad = last_sum(
        nodes ** (-0.5), far, crossed, w, *[turn(w, d) for d in (1, 2, 3)]
    )
    return activations, feature_grad, weight_grad


def solution(mesh):
    in_specs = (
        P(("row", "rep"), None),
        P("row", "rep", None, None, None),
        P("row", "rep", None, None, None),
        P("row", "rep", None),
        P(),
        P(("row", "rep"), None),
    )
    out_specs = (P(("row", "rep"), None), P(("row", "rep"), None), P())
    return jax.shard_map(
        per_device, mesh=mesh, in_specs=in_specs, out_specs=out_specs, check_vma=False
    )
```

```python
import functools

import jax
import jax.numpy as jnp
import numpy as np
from jax import lax
from jax.experimental import pallas as pl
from jax.experimental.pallas import tpu as pltpu
from jax.sharding import PartitionSpec as P

B = 128
SLOTS = 4
BROWS = 8
SECTIONS = 64
ROWS = 2 * B
PIECE = 64
SPLIT = 3 * PIECE
COST = B * B * 8
LONG = 1 << 40
TURNS = (2, 1, 3)
F32 = jnp.float32
BF16 = jnp.bfloat16
VMEM = pl.BlockSpec(memory_space=pltpu.VMEM)
SMEM = pl.BlockSpec(memory_space=pltpu.SMEM)

COUNTS = SECTIONS * SLOTS * 3
FORWARD_ORDER = COUNTS + SECTIONS
BACKWARD_ORDER = FORWARD_ORDER + SECTIONS
PLACE = BACKWARD_ORDER + SECTIONS


def group(flip, e, ds=(0, 1, 2, 3)):
    return [(flip, e, d, u) for d in ds for u in range(2)]


FORWARD_GROUPS = [
    [group(0, 0)],
    [group(0, 1), group(0, 3)],
    [group(1, 0), group(1, 1), group(1, 3)],
    [group(0, 2), group(1, 2)],
]
LOW, HIGH = (0, 1), (2, 3)
BACKWARD_GROUPS = [
    group(1, 2, LOW) + group(1, 1, HIGH) + group(1, 2, HIGH) + group(1, 3, LOW),
    group(1, 1, LOW) + group(1, 3, HIGH) + group(1, 0),
    group(0, 2, LOW) + group(0, 1, HIGH) + group(0, 2, HIGH) + group(0, 3, LOW),
    group(0, 1, LOW) + group(0, 3, HIGH) + group(0, 0),
]


def section_order(r, entries, sign):
    flip, e, d, u = (np.array(column, np.int32) for column in zip(*entries))
    y, x, z, core = r // 16, (r // 4) % 4, (r // 2) % 2, r % 2
    role = core ^ flip
    dy, dx = jnp.where(role == 0, e, d), jnp.where(role == 0, d, e)
    return ((y + sign * dy) & 3) * 16 + ((x + sign * dx) & 3) * 4 + (z ^ role) * 2 + u


def at(y, x, z, core):
    return (y % 4) * 16 + (x % 4) * 4 + z * 2 + core


def row_permute(array, target):
    pairs = []
    for r in range(64):
        to = target(r // 16, (r // 4) % 4, (r // 2) % 2, r % 2)
        if to is not None:
            pairs.append((r, to))
    return lax.ppermute(array, "row", pairs)


def small_axis(array, d):
    return row_permute(array, lambda y, x, z, c: at(y + d * c, x + d * (1 - c), z, c))


def large_axis(array, e):
    return row_permute(array, lambda y, x, z, c: at(y + e * (1 - c), x + e * c, z, c))


def sibling(array):
    return row_permute(array, lambda y, x, z, c: at(y, x, z, 1 - c))


def cross(array, forwards):
    if forwards:
        return row_permute(array, lambda y, x, z, c: at(y, x, z, 0) if c else at(y, x, 1 - z, 1))
    return row_permute(array, lambda y, x, z, c: at(y, x, 1 - z, 0) if c else at(y, x, z, 1))


def other_z(array):
    return row_permute(array, lambda y, x, z, c: at(y, x, 1 - z, 1) if c else at(y, x, z, 0))


def turn(array, d):
    return lax.ppermute(array, "rep", [(q, (q + d) % 4) for q in range(4)])


def params():
    return pltpu.CompilerParams(vmem_limit_bytes=20 * 1024 * 1024)


def cost(slots):
    return pl.CostEstimate(flops=slots * COST, bytes_accessed=slots * COST, transcendentals=0)


def small_cost(size):
    return pl.CostEstimate(flops=size // 64, bytes_accessed=size // 64, transcendentals=0)


def touch_kernel(meta, stored, out):
    out[...] = stored[0, 0:16, :].astype(F32)


def touch(meta, stored):
    return pl.pallas_call(
        touch_kernel,
        out_shape=jax.ShapeDtypeStruct((16, B), F32),
        in_specs=[SMEM, VMEM],
        out_specs=VMEM,
        compiler_params=params(),
        cost_estimate=small_cost(1 << 10),
        name="touch_blocks",
    )(meta, stored)


def own_core():
    return lax.rem(lax.axis_index("row"), 2)


def pair_up_kernel(near, far, out):
    first = own_core() == 0
    out[0:ROWS] = jnp.where(first, far[...], near[...])
    out[ROWS : 2 * ROWS] = jnp.where(first, near[...], far[...])


def pair_up(near, far):
    return pl.pallas_call(
        pair_up_kernel,
        out_shape=jax.ShapeDtypeStruct((2 * ROWS, B), BF16),
        in_specs=[VMEM] * 2,
        out_specs=VMEM,
        compiler_params=params(),
        cost_estimate=small_cost(1 << 16),
        name="pair_up",
    )(near, far)


def place_kernel(counts, parts, *refs):
    sources, outs = refs[: len(counts)], refs[-len(parts) :]
    for out, pieces in zip(outs, parts):
        row = 0
        for source, start, size in pieces:
            out[row : row + size * ROWS] = sources[source][start * ROWS : (start + size) * ROWS]
            row += size * ROWS


def place(name, parts, sources, after=(), size=1 << 18):
    shapes = [jax.ShapeDtypeStruct((sum(p[2] for p in pieces) * ROWS, B), BF16) for pieces in parts]
    args = [*sources, *after]
    return pl.pallas_call(
        functools.partial(place_kernel, tuple(range(len(sources))), parts),
        out_shape=shapes,
        in_specs=[VMEM] * len(args),
        out_specs=[VMEM] * len(shapes),
        compiler_params=params(),
        cost_estimate=small_cost(size),
        name=name,
    )(*args)


STEP = 4


def forward_kernel(first_section, sizes, first, last, after, *refs):
    meta, stored = refs[:2]
    chunk_refs = refs[2 : 2 + len(sizes)]
    refs = refs[2 + len(sizes) + after :]
    if first:
        out_refs, acc = refs[:-1], refs[-1]
        acc[...] = jnp.zeros_like(acc)
    else:
        out_refs, acc = refs[1:-1], refs[-1]
        acc[0:BROWS] = refs[0][...]
    begin = first_section
    for size, chunk_ref in zip(sizes, chunk_refs):

        def step(g, carry, begin=begin, chunk_ref=chunk_ref):
            products, places = [], []
            for n in range(STEP):
                sid = meta[FORWARD_ORDER + begin + g * STEP + n]
                count = meta[COUNTS + sid]
                for k in range(SLOTS):
                    base = sid * (SLOTS * 3) + 3 * k
                    start = pl.multiple_of((g * STEP + n) * ROWS + meta[base + 1] * B, B)
                    source = chunk_ref[pl.ds(start, B)]
                    products.append(jnp.dot(stored[meta[base + 2]], source, preferred_element_type=F32))
                    places.append(jnp.where(k < count, meta[base], BROWS))
            for product, place in zip(products, places):
                acc[place] += product
            return carry

        lax.fori_loop(0, size // STEP, step, 0)
        begin += size
    if not last:
        out_refs[0][...] = acc[0:BROWS]
        return
    rep = meta[PLACE]
    for d in range(4):
        for b in range(2):
            piece = acc[lax.rem(rep + d, 4) * 2 + b]
            out_refs[d][b * B : (b + 1) * B] = piece.astype(out_refs[d].dtype)


def forward(meta, stored, first_section, chunk_list, start, last, after=()):
    sizes = tuple(chunk.shape[0] // ROWS for chunk in chunk_list)
    first = start is None
    if last:
        out_shape = [jax.ShapeDtypeStruct((2 * B, B), F32)] + [jax.ShapeDtypeStruct((2 * B, B), BF16)] * 3
    else:
        out_shape = [jax.ShapeDtypeStruct((BROWS, B, B), F32)]
    args = [meta, stored, *chunk_list, *after] + ([] if first else [start])
    return pl.pallas_call(
        functools.partial(forward_kernel, first_section, sizes, first, last, len(after)),
        out_shape=out_shape,
        in_specs=[SMEM] + [VMEM] * (len(args) - 1),
        out_specs=[VMEM] * len(out_shape),
        scratch_shapes=[pltpu.VMEM((BROWS + 1, B, B), F32)],
        compiler_params=params(),
        cost_estimate=cost(sum(sizes) * SLOTS),
        name="forward_slots",
    )(*args)


def middle_kernel(own, p1, p2, p3, weight, cot, act, values, m1, m2, m3, w0):
    pooled = (own[...] + p1[...].astype(F32) + p2[...].astype(F32) + p3[...].astype(F32)).astype(BF16)
    hidden = jnp.dot(pooled, weight[...], preferred_element_type=F32)
    squash = jax.nn.sigmoid(hidden)
    act[...] = (hidden * squash).astype(BF16)
    slope = (cot[...].astype(F32) * squash * (1.0 + hidden * (1.0 - squash))).astype(BF16)
    values_t = lax.dot_general(weight[...], slope, (((1,), (1,)), ((), ())), preferred_element_type=F32)
    values_t = values_t.astype(BF16)
    for out in (values, m1, m2, m3):
        out[0:B] = values_t[:, :B]
        out[B:ROWS] = values_t[:, B:]
    term = lax.dot_general(pooled, slope, (((0,), (0,)), ((), ())), preferred_element_type=F32)
    rep = lax.axis_index("rep")
    for q in range(4):
        piece = jnp.concatenate([term[q * 32 : (q + 1) * 32, :B], term[q * 32 : (q + 1) * 32, B:]], axis=0)

        @pl.when(rep == q)
        def _(piece=piece):
            w0[...] = piece

        for d, out in enumerate((m1, m2, m3)):

            @pl.when(lax.rem(rep + d + 1, 4) == q)
            def _(out=out, piece=piece):
                out[ROWS : ROWS + PIECE] = piece.astype(BF16)


def middle(own, pieces, weight, cot):
    return pl.pallas_call(
        middle_kernel,
        out_shape=[jax.ShapeDtypeStruct((2 * B, 2 * B), BF16), jax.ShapeDtypeStruct((ROWS, B), BF16)]
        + [jax.ShapeDtypeStruct((ROWS + PIECE, B), BF16)] * 3
        + [jax.ShapeDtypeStruct((PIECE, B), F32)],
        in_specs=[VMEM] * 6,
        out_specs=[VMEM] * 6,
        compiler_params=params(),
        cost_estimate=small_cost(1 << 16),
        name="middle_rows",
    )(own, *pieces, weight, cot)


def split(total, out_ref, row):
    rest = total
    for n in range(3):
        part = rest.astype(BF16)
        out_ref[row + n * PIECE : row + (n + 1) * PIECE] = part
        rest = rest - part.astype(F32)


def joined(ref, row):
    parts = [ref[row + n * PIECE : row + (n + 1) * PIECE].astype(F32) for n in range(3)]
    return (parts[2] + parts[1]) + parts[0]


def gather_terms(extra, outs, extra_outs):
    total = extra[0][...]
    for ref in extra[1:]:
        total = total + ref[ROWS : ROWS + PIECE].astype(F32)
    split(total, outs[0], 16 * ROWS)
    extra_outs[0][...] = total


def sibling_terms(extra, outs, extra_outs):
    extra_outs[0][...] = (extra[0][...] + joined(extra[1], 16 * ROWS)).astype(BF16)


def backward_kernel(first_section, sizes, added, extras, finish, *refs):
    meta, stored = refs[:2]
    value_refs, refs = refs[2:6], refs[6:]
    if added:
        add_ref, refs = refs[0], refs[1:]
    extra, refs = refs[:extras], refs[extras:]
    out_refs, extra_outs, values = refs[: len(sizes)], refs[len(sizes) : -1], refs[-1]
    rep = meta[PLACE]
    for d, value_ref in zip((0, *TURNS), value_refs):
        for b in range(2):
            values[lax.rem(rep + 4 - d, 4) * 2 + b] = value_ref[b * B : (b + 1) * B]
    values[BROWS] = jnp.zeros((B, B), BF16)

    begin = 0
    for size, out_ref in zip(sizes, out_refs):

        def step(g, carry, begin=begin, out_ref=out_ref):
            for m in range(STEP):
                n = g * STEP + m
                sid = meta[BACKWARD_ORDER + first_section + begin + n]
                count = meta[COUNTS + sid]
                base = sid * (SLOTS * 3)
                rows = []
                for j in range(2):
                    columns = []
                    for k in range(SLOTS):
                        live = (k < count) & (meta[base + 3 * k + 1] == j)
                        columns.append(values[jnp.where(live, meta[base + 3 * k], BROWS)])
                    rows.append(jnp.concatenate(columns, axis=1))
                left = jnp.concatenate(rows, axis=0)
                right = jnp.concatenate([stored[meta[base + 3 * k + 2]] for k in range(SLOTS)], axis=0)
                result = jnp.dot(left, right, preferred_element_type=F32)
                if added:
                    result = result + add_ref[pl.ds(pl.multiple_of((begin + n) * ROWS, ROWS), ROWS)].astype(F32)
                out_ref[pl.ds(pl.multiple_of(n * ROWS, ROWS), ROWS)] = result.astype(BF16)
            return carry

        lax.fori_loop(0, size // STEP, step, 0)
        begin += size
    if finish is not None:
        finish(extra, out_refs, extra_outs)


def backward(meta, stored, values, first_section, sizes, add=None, extra=(), finish=None, tails=None, extra_out=(), size=0):
    added = add is not None
    args = [meta, stored, *values] + ([add] if added else []) + list(extra)
    tails = tails or (0,) * len(sizes)
    shapes = [jax.ShapeDtypeStruct((size * ROWS + tail, B), BF16) for size, tail in zip(sizes, tails)]
    shapes += [jax.ShapeDtypeStruct(a.shape, a.dtype) for a in extra_out]
    return pl.pallas_call(
        functools.partial(backward_kernel, first_section, sizes, added, len(extra), finish),
        out_shape=shapes,
        in_specs=[SMEM] + [VMEM] * (len(args) - 1),
        out_specs=[VMEM] * len(shapes),
        scratch_shapes=[pltpu.VMEM((BROWS + 1, B, B), BF16)],
        compiler_params=params(),
        cost_estimate=small_cost(size) if size else cost(sum(sizes) * SLOTS),
        name="backward_slots",
    )(*args)


def late_kernel(a, b, half_1, half_3, own, other, out_1, out_3, w):
    total = (own[...].astype(F32) + other[...].astype(F32)).astype(BF16)
    w[...] = total
    for near, half, out in ((a, half_1, out_1), (b, half_3, out_3)):
        out[0 : 4 * ROWS] = (near[...].astype(F32) + half[0 : 4 * ROWS].astype(F32)).astype(BF16)
        out[4 * ROWS :] = total


def add_late(*arrays):
    return pl.pallas_call(
        late_kernel,
        out_shape=[jax.ShapeDtypeStruct((4 * ROWS + PIECE, B), BF16)] * 2 + [jax.ShapeDtypeStruct((PIECE, B), BF16)],
        in_specs=[VMEM] * 6,
        out_specs=[VMEM] * 3,
        compiler_params=params(),
        cost_estimate=small_cost(1 << 18),
        name="add_late",
    )(*arrays)


def sum_kernel(a, early_1, early_3, late_1, late_3, own, two, t0, t1, t2, t3, w):
    tail = slice(4 * ROWS, 4 * ROWS + PIECE)
    total = own[...].astype(F32) + two[...].astype(F32)
    total = total + (late_1[tail].astype(F32) + late_3[tail].astype(F32))
    w[...] = total
    for d, out in enumerate((t0, t1, t2, t3)):
        early, late = (early_1, late_3) if d >= 2 else (early_3, late_1)
        start = 2 * ROWS * (d % 2)
        group_sum = a[2 * ROWS * d : 2 * ROWS * (d + 1)].astype(F32)
        group_sum = group_sum + early[4 * ROWS + start : 6 * ROWS + start].astype(F32)
        group_sum = group_sum + late[start : start + 2 * ROWS].astype(F32)
        out[0 : 2 * ROWS] = group_sum.astype(BF16)
        if d:
            split(total, out, 2 * ROWS)


def sum_groups(*arrays):
    return pl.pallas_call(
        sum_kernel,
        out_shape=[jax.ShapeDtypeStruct((2 * ROWS, B), BF16)]
        + [jax.ShapeDtypeStruct((2 * ROWS + SPLIT, B), BF16)] * 3
        + [jax.ShapeDtypeStruct((PIECE, B), F32)],
        in_specs=[VMEM] * 7,
        out_specs=[VMEM] * 5,
        compiler_params=params(),
        cost_estimate=small_cost(1 << 18),
        name="sum_groups",
    )(*arrays)


def pair_kernel(a, b, c, d, own, mine, other, w):
    core = own_core()
    for out, unit in ((mine, core), (other, 1 - core)):
        part = pl.ds(pl.multiple_of(unit * ROWS, ROWS), ROWS)
        total = a[part].astype(F32) + b[part].astype(F32) + c[part].astype(F32) + d[part].astype(F32)
        out[...] = total.astype(BF16)
    w[...] = (own[...] + joined(b, 2 * ROWS)) + (joined(c, 2 * ROWS) + joined(d, 2 * ROWS))


def sum_pairs(*arrays):
    return pl.pallas_call(
        pair_kernel,
        out_shape=[jax.ShapeDtypeStruct((ROWS, B), BF16)] * 2 + [jax.ShapeDtypeStruct((PIECE, B), F32)],
        in_specs=[VMEM] * 5,
        out_specs=[VMEM] * 3,
        compiler_params=params(),
        cost_estimate=small_cost(1 << 17),
        name="sum_pairs",
    )(*arrays)


def last_kernel(scaling, far, crossed, w0, w1, w2, w3, out, weight_grad):
    for s in range(2):
        part = slice(s * B, (s + 1) * B)
        out[part] = (far[part].astype(F32) + crossed[part].astype(F32)).T.astype(BF16)
    rep = lax.axis_index("rep")
    for back, piece in zip((0, *TURNS), (w0, w1, w2, w3)):
        rows = pl.ds(pl.multiple_of(lax.rem(rep + 4 - back, 4) * 32, 32), 32)
        weight_grad[rows, 0:B] = piece[0:32] * scaling
        weight_grad[rows, B : 2 * B] = piece[32:64] * scaling


def last_sum(scaling, *arrays):
    return pl.pallas_call(
        functools.partial(last_kernel, scaling),
        out_shape=[jax.ShapeDtypeStruct((ROWS, B), BF16), jax.ShapeDtypeStruct((B, 2 * B), F32)],
        in_specs=[VMEM] * 6,
        out_specs=[VMEM] * 2,
        compiler_params=params(),
        cost_estimate=small_cost(1 << 16),
        name="last_sum",
    )(*arrays)


def per_device(features, adjacency, block_list, block_counts, weight, cotangent):
    stored = adjacency[0, 0]
    r = lax.axis_index("row").astype(jnp.int32)
    rep = lax.axis_index("rep").astype(jnp.int32)
    nodes = float(features.shape[0] * 256)

    order = [entry for call in FORWARD_GROUPS for part in call for entry in part]
    back_order = [entry for part in BACKWARD_GROUPS for entry in part]
    meta = jnp.concatenate(
        [
            block_list.reshape(-1),
            block_counts.reshape(-1),
            section_order(r, order, -1),
            section_order(r, back_order, 1),
            rep.reshape(1),
        ]
    )

    near_unit, far_unit = cross(features, True), other_z(features)
    pair = pair_up(near_unit, far_unit)
    x2, x1, x3 = small_axis(pair, 2), small_axis(pair, 1), small_axis(pair, 3)
    touched = touch(meta, stored)
    (low,) = place("place_low", [[(0, 0, 2), (1, 0, 2)]], [pair, x1])
    n1_low, n3_low = large_axis(low, 1), large_axis(low, 3)
    (high,) = place("place_high", [[(0, 0, 2), (1, 0, 2)]], [x2, x3], [touched, low])
    n1_high, n3_high = large_axis(high, 1), large_axis(high, 3)
    (acc,) = forward(meta, stored, 0, [low, high], None, False)
    f1, f3 = large_axis(n1_low, 1), large_axis(n3_high, 3)
    halves = [low, high, n1_low, n1_high, n3_low, n3_high]
    (near,) = place("place_near", [[(n, 0, 4) for n in range(6)]], halves, [acc])
    near_s = sibling(near)
    (acc,) = forward(meta, stored, 8, halves[2:], acc, False)
    (far,) = place("place_far", [[(0, 0, 4), (1, 0, 4)]], [f1, f3], [acc], size=LONG)
    far_s = sibling(far)
    (acc,) = forward(meta, stored, 24, [near_s], acc, False)
    own_part, *pieces = forward(meta, stored, 48, [far, far_s], acc, True)

    pieces = [turn(pieces[d - 1], d) for d in TURNS]
    activations, values, m1, m2, m3, w = middle(own_part, pieces, weight, cotangent)
    messages = [turn((m1, m2, m3)[d - 1], d) for d in TURNS]

    bwd = functools.partial(backward, meta, stored, [values] + messages)
    first_b, w4 = bwd(0, (16,), extra=[w] + messages, finish=gather_terms, tails=(SPLIT,), extra_out=[w])
    first_s = sibling(first_b)
    (second_b,) = bwd(16, (16,), extra=[first_b])
    second_s = sibling(second_b)
    e1, e3, w8 = bwd(
        32,
        (8, 8),
        first_s,
        extra=[w4, first_s, second_b],
        finish=sibling_terms,
        extra_out=[messages[0][:PIECE]],
        size=LONG,
    )
    r1, r3 = large_axis(e1, 1), large_axis(e3, 3)
    w8_z = row_permute(w8, lambda y, x, z, c: at(y, x, 1 - z, c))
    l1, l3, g0 = bwd(48, (4, 4, 8), second_s, extra=[e1])
    l1, l3, w16 = add_late(l1, l3, r1, r3, w8, w8_z)
    l1, l3, w16_two = large_axis(l1, 1), large_axis(l3, 3), large_axis(w16, 2)
    t0, t1, t2, t3, w64 = sum_groups(g0, r1, r3, l1, l3, w16, w16_two)
    sums = [t0, small_axis(t2, 2), small_axis(t1, 1), small_axis(t3, 3)]
    mine, other, w = sum_pairs(*sums, w64)
    far, crossed = other_z(mine), cross(other, False)
    feature_grad, weight_grad = last_sum(
        nodes ** (-0.5), far, crossed, w, *[turn(w, d) for d in TURNS]
    )
    return activations, feature_grad, weight_grad


def solution(mesh):
    in_specs = (
        P(("row", "rep"), None),
        P("row", "rep", None, None, None),
        P("row", "rep", None, None, None),
        P("row", "rep", None),
        P(),
        P(("row", "rep"), None),
    )
    out_specs = (P(("row", "rep"), None), P(("row", "rep"), None), P())
    return jax.shard_map(
        per_device, mesh=mesh, in_specs=in_specs, out_specs=out_specs, check_vma=False
    )
```

```python
import functools

import jax
import jax.numpy as jnp
import numpy as np
from jax import lax
from jax.experimental import pallas as pl
from jax.experimental.pallas import tpu as pltpu
from jax.sharding import PartitionSpec as P

B = 128
SLOTS = 4
BROWS = 8
SECTIONS = 64
ROWS = 2 * B
PIECE = 64
SPLIT = 3 * PIECE
COST = B * B * 8
LONG = 1 << 40
TURNS = (2, 1, 3)
F32 = jnp.float32
BF16 = jnp.bfloat16
VMEM = pl.BlockSpec(memory_space=pltpu.VMEM)
SMEM = pl.BlockSpec(memory_space=pltpu.SMEM)

COUNTS = SECTIONS * SLOTS * 3
FORWARD_ORDER = COUNTS + SECTIONS
BACKWARD_ORDER = FORWARD_ORDER + SECTIONS
PLACE = BACKWARD_ORDER + SECTIONS


def group(flip, e, ds=(0, 1, 2, 3)):
    return [(flip, e, d, u) for d in ds for u in range(2)]


GATHERED = (0, 2, 1, 3)
FORWARD_GROUPS = [
    [group(0, 0, GATHERED)],
    [group(0, 1, GATHERED), group(0, 3, GATHERED)],
    [group(1, 0, GATHERED), group(1, 1, GATHERED), group(1, 3, GATHERED)],
    [group(0, 2, GATHERED), group(1, 2, GATHERED)],
]
LOW, HIGH = (0, 1), (2, 3)
BACKWARD_GROUPS = [
    group(1, 2, LOW) + group(1, 1, HIGH) + group(1, 2, HIGH) + group(1, 3, LOW),
    group(1, 1, LOW) + group(1, 3, HIGH) + group(1, 0),
    group(0, 2, LOW) + group(0, 1, HIGH) + group(0, 2, HIGH) + group(0, 3, LOW),
    group(0, 1, LOW) + group(0, 3, HIGH) + group(0, 0),
]


def section_order(r, entries, sign):
    flip, e, d, u = (np.array(column, np.int32) for column in zip(*entries))
    y, x, z, core = r // 16, (r // 4) % 4, (r // 2) % 2, r % 2
    role = core ^ flip
    dy, dx = jnp.where(role == 0, e, d), jnp.where(role == 0, d, e)
    return ((y + sign * dy) & 3) * 16 + ((x + sign * dx) & 3) * 4 + (z ^ role) * 2 + u


def at(y, x, z, core):
    return (y % 4) * 16 + (x % 4) * 4 + z * 2 + core


def row_permute(array, target):
    pairs = []
    for r in range(64):
        to = target(r // 16, (r // 4) % 4, (r // 2) % 2, r % 2)
        if to is not None:
            pairs.append((r, to))
    return lax.ppermute(array, "row", pairs)


def small_axis(array, d):
    return row_permute(array, lambda y, x, z, c: at(y + d * c, x + d * (1 - c), z, c))


def large_axis(array, e):
    return row_permute(array, lambda y, x, z, c: at(y + e * (1 - c), x + e * c, z, c))


def sibling(array):
    return row_permute(array, lambda y, x, z, c: at(y, x, z, 1 - c))


def cross(array, forwards):
    if forwards:
        return row_permute(array, lambda y, x, z, c: at(y, x, z, 0) if c else at(y, x, 1 - z, 1))
    return row_permute(array, lambda y, x, z, c: at(y, x, 1 - z, 0) if c else at(y, x, z, 1))


def other_z(array):
    return row_permute(array, lambda y, x, z, c: at(y, x, 1 - z, 1) if c else at(y, x, z, 0))


def turn(array, d):
    return lax.ppermute(array, "rep", [(q, (q + d) % 4) for q in range(4)])


def params():
    return pltpu.CompilerParams(vmem_limit_bytes=20 * 1024 * 1024)


def cost(slots):
    return pl.CostEstimate(flops=slots * COST, bytes_accessed=slots * COST, transcendentals=0)


def small_cost(size):
    return pl.CostEstimate(flops=size // 64, bytes_accessed=size // 64, transcendentals=0)


def touch_kernel(meta, stored, out):
    out[...] = stored[0, 0:16, :].astype(F32)


def touch(meta, stored):
    return pl.pallas_call(
        touch_kernel,
        out_shape=jax.ShapeDtypeStruct((16, B), F32),
        in_specs=[SMEM, VMEM],
        out_specs=VMEM,
        compiler_params=params(),
        cost_estimate=small_cost(1 << 10),
        name="touch_blocks",
    )(meta, stored)


def own_core():
    return lax.rem(lax.axis_index("row"), 2)


def pair_up_kernel(near, far, out):
    first = own_core() == 0
    out[0:ROWS] = jnp.where(first, far[...], near[...])
    out[ROWS : 2 * ROWS] = jnp.where(first, near[...], far[...])


def pair_up(near, far):
    return pl.pallas_call(
        pair_up_kernel,
        out_shape=jax.ShapeDtypeStruct((2 * ROWS, B), BF16),
        in_specs=[VMEM] * 2,
        out_specs=VMEM,
        compiler_params=params(),
        cost_estimate=small_cost(1 << 16),
        name="pair_up",
    )(near, far)


def place_kernel(counts, parts, *refs):
    sources, outs = refs[: len(counts)], refs[-len(parts) :]
    for out, pieces in zip(outs, parts):
        row = 0
        for source, start, size in pieces:
            out[row : row + size * ROWS] = sources[source][start * ROWS : (start + size) * ROWS]
            row += size * ROWS


def place(name, parts, sources, after=(), size=1 << 18):
    shapes = [jax.ShapeDtypeStruct((sum(p[2] for p in pieces) * ROWS, B), BF16) for pieces in parts]
    args = [*sources, *after]
    return pl.pallas_call(
        functools.partial(place_kernel, tuple(range(len(sources))), parts),
        out_shape=shapes,
        in_specs=[VMEM] * len(args),
        out_specs=[VMEM] * len(shapes),
        compiler_params=params(),
        cost_estimate=small_cost(size),
        name=name,
    )(*args)


STEP = 4


def forward_kernel(first_section, sizes, first, last, after, *refs):
    meta, stored = refs[:2]
    chunk_refs = refs[2 : 2 + len(sizes)]
    refs = refs[2 + len(sizes) + after :]
    if first:
        out_refs, acc = refs[:-1], refs[-1]
        acc[...] = jnp.zeros_like(acc)
    else:
        out_refs, acc = refs[1:-1], refs[-1]
        acc[0:BROWS] = refs[0][...]
    begin = first_section
    for size, chunk_ref in zip(sizes, chunk_refs):

        def step(g, carry, begin=begin, chunk_ref=chunk_ref):
            products, places = [], []
            for n in range(STEP):
                sid = meta[FORWARD_ORDER + begin + g * STEP + n]
                count = meta[COUNTS + sid]
                for k in range(SLOTS):
                    base = sid * (SLOTS * 3) + 3 * k
                    start = pl.multiple_of((g * STEP + n) * ROWS + meta[base + 1] * B, B)
                    source = chunk_ref[pl.ds(start, B)]
                    products.append(jnp.dot(stored[meta[base + 2]], source, preferred_element_type=F32))
                    places.append(jnp.where(k < count, meta[base], BROWS))
            for product, place in zip(products, places):
                acc[place] += product
            return carry

        lax.fori_loop(0, size // STEP, step, 0)
        begin += size
    if not last:
        out_refs[0][...] = acc[0:BROWS]
        return
    rep = meta[PLACE]
    for d in range(4):
        for b in range(2):
            piece = acc[lax.rem(rep + d, 4) * 2 + b]
            out_refs[d][b * B : (b + 1) * B] = piece.astype(out_refs[d].dtype)


def forward(meta, stored, first_section, chunk_list, start, last, after=()):
    sizes = tuple(chunk.shape[0] // ROWS for chunk in chunk_list)
    first = start is None
    if last:
        out_shape = [jax.ShapeDtypeStruct((2 * B, B), F32)] + [jax.ShapeDtypeStruct((2 * B, B), BF16)] * 3
    else:
        out_shape = [jax.ShapeDtypeStruct((BROWS, B, B), F32)]
    args = [meta, stored, *chunk_list, *after] + ([] if first else [start])
    return pl.pallas_call(
        functools.partial(forward_kernel, first_section, sizes, first, last, len(after)),
        out_shape=out_shape,
        in_specs=[SMEM] + [VMEM] * (len(args) - 1),
        out_specs=[VMEM] * len(out_shape),
        scratch_shapes=[pltpu.VMEM((BROWS + 1, B, B), F32)],
        compiler_params=params(),
        cost_estimate=cost(sum(sizes) * SLOTS),
        name="forward_slots",
    )(*args)


def middle_kernel(own, p1, p2, p3, weight, cot, act, values, m1, m2, m3, w0):
    pooled = (own[...] + p1[...].astype(F32) + p2[...].astype(F32) + p3[...].astype(F32)).astype(BF16)
    hidden = jnp.dot(pooled, weight[...], preferred_element_type=F32)
    squash = jax.nn.sigmoid(hidden)
    act[...] = (hidden * squash).astype(BF16)
    slope = (cot[...].astype(F32) * squash * (1.0 + hidden * (1.0 - squash))).astype(BF16)
    values_t = lax.dot_general(weight[...], slope, (((1,), (1,)), ((), ())), preferred_element_type=F32)
    values_t = values_t.astype(BF16)
    for out in (values, m1, m2, m3):
        out[0:B] = values_t[:, :B]
        out[B:ROWS] = values_t[:, B:]
    term = lax.dot_general(pooled, slope, (((0,), (0,)), ((), ())), preferred_element_type=F32)
    rep = lax.axis_index("rep")
    for q in range(4):
        piece = jnp.concatenate([term[q * 32 : (q + 1) * 32, :B], term[q * 32 : (q + 1) * 32, B:]], axis=0)

        @pl.when(rep == q)
        def _(piece=piece):
            w0[...] = piece

        for d, out in enumerate((m1, m2, m3)):

            @pl.when(lax.rem(rep + d + 1, 4) == q)
            def _(out=out, piece=piece):
                out[ROWS : ROWS + PIECE] = piece.astype(BF16)


def middle(own, pieces, weight, cot):
    return pl.pallas_call(
        middle_kernel,
        out_shape=[jax.ShapeDtypeStruct((2 * B, 2 * B), BF16), jax.ShapeDtypeStruct((ROWS, B), BF16)]
        + [jax.ShapeDtypeStruct((ROWS + PIECE, B), BF16)] * 3
        + [jax.ShapeDtypeStruct((PIECE, B), F32)],
        in_specs=[VMEM] * 6,
        out_specs=[VMEM] * 6,
        compiler_params=params(),
        cost_estimate=small_cost(1 << 16),
        name="middle_rows",
    )(own, *pieces, weight, cot)


def split(total, out_ref, row):
    rest = total
    for n in range(3):
        part = rest.astype(BF16)
        out_ref[row + n * PIECE : row + (n + 1) * PIECE] = part
        rest = rest - part.astype(F32)


def joined(ref, row):
    parts = [ref[row + n * PIECE : row + (n + 1) * PIECE].astype(F32) for n in range(3)]
    return (parts[2] + parts[1]) + parts[0]


def gather_terms(extra, outs, extra_outs):
    total = extra[0][...]
    for ref in extra[1:]:
        total = total + ref[ROWS : ROWS + PIECE].astype(F32)
    split(total, outs[0], 16 * ROWS)
    extra_outs[0][...] = total


def sibling_terms(extra, outs, extra_outs):
    extra_outs[0][...] = (extra[0][...] + joined(extra[1], 16 * ROWS)).astype(BF16)


def backward_kernel(first_section, sizes, added, extras, finish, *refs):
    meta, stored = refs[:2]
    value_refs, refs = refs[2:6], refs[6:]
    if added:
        add_ref, refs = refs[0], refs[1:]
    extra, refs = refs[:extras], refs[extras:]
    out_refs, extra_outs, values = refs[: len(sizes)], refs[len(sizes) : -1], refs[-1]
    rep = meta[PLACE]
    for d, value_ref in zip((0, *TURNS), value_refs):
        for b in range(2):
            values[lax.rem(rep + 4 - d, 4) * 2 + b] = value_ref[b * B : (b + 1) * B]
    values[BROWS] = jnp.zeros((B, B), BF16)

    begin = 0
    for size, out_ref in zip(sizes, out_refs):

        def step(g, carry, begin=begin, out_ref=out_ref):
            for m in range(STEP):
                n = g * STEP + m
                sid = meta[BACKWARD_ORDER + first_section + begin + n]
                count = meta[COUNTS + sid]
                base = sid * (SLOTS * 3)
                rows = []
                for j in range(2):
                    columns = []
                    for k in range(SLOTS):
                        live = (k < count) & (meta[base + 3 * k + 1] == j)
                        columns.append(values[jnp.where(live, meta[base + 3 * k], BROWS)])
                    rows.append(jnp.concatenate(columns, axis=1))
                left = jnp.concatenate(rows, axis=0)
                right = jnp.concatenate([stored[meta[base + 3 * k + 2]] for k in range(SLOTS)], axis=0)
                result = jnp.dot(left, right, preferred_element_type=F32)
                if added:
                    result = result + add_ref[pl.ds(pl.multiple_of((begin + n) * ROWS, ROWS), ROWS)].astype(F32)
                out_ref[pl.ds(pl.multiple_of(n * ROWS, ROWS), ROWS)] = result.astype(BF16)
            return carry

        lax.fori_loop(0, size // STEP, step, 0)
        begin += size
    if finish is not None:
        finish(extra, out_refs, extra_outs)


def backward(meta, stored, values, first_section, sizes, add=None, extra=(), finish=None, tails=None, extra_out=(), size=0):
    added = add is not None
    args = [meta, stored, *values] + ([add] if added else []) + list(extra)
    tails = tails or (0,) * len(sizes)
    shapes = [jax.ShapeDtypeStruct((size * ROWS + tail, B), BF16) for size, tail in zip(sizes, tails)]
    shapes += [jax.ShapeDtypeStruct(a.shape, a.dtype) for a in extra_out]
    return pl.pallas_call(
        functools.partial(backward_kernel, first_section, sizes, added, len(extra), finish),
        out_shape=shapes,
        in_specs=[SMEM] + [VMEM] * (len(args) - 1),
        out_specs=[VMEM] * len(shapes),
        scratch_shapes=[pltpu.VMEM((BROWS + 1, B, B), BF16)],
        compiler_params=params(),
        cost_estimate=small_cost(size) if size else cost(sum(sizes) * SLOTS),
        name="backward_slots",
    )(*args)


def late_kernel(a, b, half_1, half_3, own, other, out_1, out_3, w):
    total = (own[...].astype(F32) + other[...].astype(F32)).astype(BF16)
    w[...] = total
    for near, half, out in ((a, half_1, out_1), (b, half_3, out_3)):
        out[0 : 4 * ROWS] = (near[...].astype(F32) + half[0 : 4 * ROWS].astype(F32)).astype(BF16)
        out[4 * ROWS :] = total


def add_late(*arrays):
    return pl.pallas_call(
        late_kernel,
        out_shape=[jax.ShapeDtypeStruct((4 * ROWS + PIECE, B), BF16)] * 2 + [jax.ShapeDtypeStruct((PIECE, B), BF16)],
        in_specs=[VMEM] * 6,
        out_specs=[VMEM] * 3,
        compiler_params=params(),
        cost_estimate=small_cost(1 << 18),
        name="add_late",
    )(*arrays)


def sum_kernel(a, early_1, early_3, late_1, late_3, own, two, t0, t1, t2, t3, w):
    tail = slice(4 * ROWS, 4 * ROWS + PIECE)
    total = own[...].astype(F32) + two[...].astype(F32)
    total = total + (late_1[tail].astype(F32) + late_3[tail].astype(F32))
    w[...] = total
    for d, out in enumerate((t0, t1, t2, t3)):
        early, late = (early_1, late_3) if d >= 2 else (early_3, late_1)
        start = 2 * ROWS * (d % 2)
        group_sum = a[2 * ROWS * d : 2 * ROWS * (d + 1)].astype(F32)
        group_sum = group_sum + early[4 * ROWS + start : 6 * ROWS + start].astype(F32)
        group_sum = group_sum + late[start : start + 2 * ROWS].astype(F32)
        out[0 : 2 * ROWS] = group_sum.astype(BF16)
        if d:
            split(total, out, 2 * ROWS)


def sum_groups(*arrays):
    return pl.pallas_call(
        sum_kernel,
        out_shape=[jax.ShapeDtypeStruct((2 * ROWS, B), BF16)]
        + [jax.ShapeDtypeStruct((2 * ROWS + SPLIT, B), BF16)] * 3
        + [jax.ShapeDtypeStruct((PIECE, B), F32)],
        in_specs=[VMEM] * 7,
        out_specs=[VMEM] * 5,
        compiler_params=params(),
        cost_estimate=small_cost(1 << 18),
        name="sum_groups",
    )(*arrays)


def pair_kernel(a, b, c, d, own, mine, other, w):
    core = own_core()
    for out, unit in ((mine, core), (other, 1 - core)):
        part = pl.ds(pl.multiple_of(unit * ROWS, ROWS), ROWS)
        total = a[part].astype(F32) + b[part].astype(F32) + c[part].astype(F32) + d[part].astype(F32)
        out[...] = total.astype(BF16)
    w[...] = (own[...] + joined(b, 2 * ROWS)) + (joined(c, 2 * ROWS) + joined(d, 2 * ROWS))


def sum_pairs(*arrays):
    return pl.pallas_call(
        pair_kernel,
        out_shape=[jax.ShapeDtypeStruct((ROWS, B), BF16)] * 2 + [jax.ShapeDtypeStruct((PIECE, B), F32)],
        in_specs=[VMEM] * 5,
        out_specs=[VMEM] * 3,
        compiler_params=params(),
        cost_estimate=small_cost(1 << 17),
        name="sum_pairs",
    )(*arrays)


def last_kernel(scaling, far, crossed, w0, w1, w2, w3, out, weight_grad):
    for s in range(2):
        part = slice(s * B, (s + 1) * B)
        out[part] = (far[part].astype(F32) + crossed[part].astype(F32)).T.astype(BF16)
    rep = lax.axis_index("rep")
    for back, piece in zip((0, *TURNS), (w0, w1, w2, w3)):
        rows = pl.ds(pl.multiple_of(lax.rem(rep + 4 - back, 4) * 32, 32), 32)
        weight_grad[rows, 0:B] = piece[0:32] * scaling
        weight_grad[rows, B : 2 * B] = piece[32:64] * scaling


def last_sum(scaling, *arrays):
    return pl.pallas_call(
        functools.partial(last_kernel, scaling),
        out_shape=[jax.ShapeDtypeStruct((ROWS, B), BF16), jax.ShapeDtypeStruct((B, 2 * B), F32)],
        in_specs=[VMEM] * 6,
        out_specs=[VMEM] * 2,
        compiler_params=params(),
        cost_estimate=small_cost(1 << 16),
        name="last_sum",
    )(*arrays)


def per_device(features, adjacency, block_list, block_counts, weight, cotangent):
    stored = adjacency[0, 0]
    r = lax.axis_index("row").astype(jnp.int32)
    rep = lax.axis_index("rep").astype(jnp.int32)
    nodes = float(features.shape[0] * 256)

    order = [entry for call in FORWARD_GROUPS for part in call for entry in part]
    back_order = [entry for part in BACKWARD_GROUPS for entry in part]
    meta = jnp.concatenate(
        [
            block_list.reshape(-1),
            block_counts.reshape(-1),
            section_order(r, order, -1),
            section_order(r, back_order, 1),
            rep.reshape(1),
        ]
    )

    near_unit, far_unit = cross(features, True), other_z(features)
    pair = pair_up(near_unit, far_unit)
    x2, x1, x3 = small_axis(pair, 2), small_axis(pair, 1), small_axis(pair, 3)
    touched = touch(meta, stored)
    (low,) = place("place_low", [[(0, 0, 2), (1, 0, 2)]], [pair, x2])
    n1_low, n3_low = large_axis(low, 1), large_axis(low, 3)
    (high,) = place("place_high", [[(0, 0, 2), (1, 0, 2)]], [x1, x3], [touched, low])
    n1_high, n3_high = large_axis(high, 1), large_axis(high, 3)
    (acc,) = forward(meta, stored, 0, [low, high], None, False)
    f1, f3 = large_axis(n1_low, 1), large_axis(n3_high, 3)
    halves = [low, high, n1_low, n1_high, n3_low, n3_high]
    (near,) = place("place_near", [[(n, 0, 4) for n in range(6)]], halves, [acc])
    near_s = sibling(near)
    (acc,) = forward(meta, stored, 8, halves[2:], acc, False)
    (far,) = place("place_far", [[(0, 0, 4), (1, 0, 4)]], [f1, f3], [acc], size=LONG)
    far_s = sibling(far)
    (acc,) = forward(meta, stored, 24, [near_s], acc, False)
    own_part, *pieces = forward(meta, stored, 48, [far, far_s], acc, True)

    pieces = [turn(pieces[d - 1], d) for d in TURNS]
    activations, values, m1, m2, m3, w = middle(own_part, pieces, weight, cotangent)
    messages = [turn((m1, m2, m3)[d - 1], d) for d in TURNS]

    bwd = functools.partial(backward, meta, stored, [values] + messages)
    first_b, w4 = bwd(0, (16,), extra=[w] + messages, finish=gather_terms, tails=(SPLIT,), extra_out=[w])
    first_s = sibling(first_b)
    (second_b,) = bwd(16, (16,), extra=[first_b])
    second_s = sibling(second_b)
    e1, e3, w8 = bwd(
        32,
        (8, 8),
        first_s,
        extra=[w4, first_s, second_b],
        finish=sibling_terms,
        extra_out=[messages[0][:PIECE]],
        size=LONG,
    )
    r1, r3 = large_axis(e1, 1), large_axis(e3, 3)
    w8_z = row_permute(w8, lambda y, x, z, c: at(y, x, 1 - z, c))
    l1, l3, g0 = bwd(48, (4, 4, 8), second_s, extra=[e1])
    l1, l3, w16 = add_late(l1, l3, r1, r3, w8, w8_z)
    l1, l3, w16_two = large_axis(l1, 1), large_axis(l3, 3), large_axis(w16, 2)
    t0, t1, t2, t3, w64 = sum_groups(g0, r1, r3, l1, l3, w16, w16_two)
    sums = [t0, small_axis(t2, 2), small_axis(t1, 1), small_axis(t3, 3)]
    mine, other, w = sum_pairs(*sums, w64)
    far, crossed = other_z(mine), cross(other, False)
    feature_grad, weight_grad = last_sum(
        nodes ** (-0.5), far, crossed, w, *[turn(w, d) for d in TURNS]
    )
    return activations, feature_grad, weight_grad


def solution(mesh):
    in_specs = (
        P(("row", "rep"), None),
        P("row", "rep", None, None, None),
        P("row", "rep", None, None, None),
        P("row", "rep", None),
        P(),
        P(("row", "rep"), None),
    )
    out_specs = (P(("row", "rep"), None), P(("row", "rep"), None), P())
    return jax.shard_map(
        per_device, mesh=mesh, in_specs=in_specs, out_specs=out_specs, check_vma=False
    )
```
